128 devices in a mesh: seq: 8 (over z, core), dp: 16 (over y, x).
Axes of the slice: x: 4, y: 4, z: 4, core: 2. Of those that a mesh axis runs over, the one named last changes fastest.
Arguments:
- inputs: bfloat16 [16, 1024, 768], P('dp', 'seq'), may hold values from -6 to 6
- doc_ids: int32 [16, 1024], P('dp', 'seq'), may hold values from 0 to 4, as said below
- cotangent: bfloat16 [16, 1024, 768], P('dp', 'seq'), may hold values from -6 to 6
- w_query: float32 [768, 768], P(('seq', 'dp')), may hold values from -0.21875 to 0.21875
- w_key: float32 [768, 768], P(('seq', 'dp')), may hold values from -0.21875 to 0.21875
- w_value: float32 [768, 768], P(('seq', 'dp')), may hold values from -0.21875 to 0.21875
- w_output: float32 [768, 768], P(('seq', 'dp')), may hold values from -3.5 to 3.5
- w_gate: float32 [768, 3072], P(('seq', 'dp')), may hold values from -0.21875 to 0.21875
- w_up: float32 [768, 3072], P(('seq', 'dp')), may hold values from -0.21875 to 0.21875
- w_down: float32 [3072, 768], P(('seq', 'dp')), may hold values from -0.109375 to 0.109375
- norm_gains: float32 [768, 2], P(('seq', 'dp')), may hold values from 0.5 to 1.5
- mom_query: float32 [768, 768], P(('seq', 'dp')), may hold values from -80 to 80
- mom_key: float32 [768, 768], P(('seq', 'dp')), may hold values from -80 to 80
- mom_value: float32 [768, 768], P(('seq', 'dp')), may hold values from -80 to 80
- mom_output: float32 [768, 768], P(('seq', 'dp')), may hold values from -3.5 to 3.5
- mom_gate: float32 [768, 3072], P(('seq', 'dp')), may hold values from -40 to 40
- mom_up: float32 [768, 3072], P(('seq', 'dp')), may hold values from -40 to 40
- mom_down: float32 [3072, 768], P(('seq', 'dp')), may hold values from -40 to 40
- mom_gains: float32 [768, 2], P(('seq', 'dp')), may hold values from -80 to 80
- avg_query: float32 [768, 768], P(('seq', 'dp')), may hold values from -0.21875 to 0.21875
- avg_key: float32 [768, 768], P(('seq', 'dp')), may hold values from -0.21875 to 0.21875
- avg_value: float32 [768, 768], P(('seq', 'dp')), may hold values from -0.21875 to 0.21875
- avg_output: float32 [768, 768], P(('seq', 'dp')), may hold values from -3.5 to 3.5
- avg_gate: float32 [768, 3072], P(('seq', 'dp')), may hold values from -0.21875 to 0.21875
- avg_up: float32 [768, 3072], P(('seq', 'dp')), may hold values from -0.21875 to 0.21875
- avg_down: float32 [3072, 768], P(('seq', 'dp')), may hold values from -0.109375 to 0.109375
- avg_gains: float32 [768, 2], P(('seq', 'dp')), may hold values from 0.5 to 1.5
Outputs:
- output: bfloat16 [16, 1024, 768], P('dp', 'seq')
- input_grad: float32 [16, 1024, 768], P('dp', 'seq')
- new_query: float32 [768, 768], P(('seq', 'dp'))
- new_key: float32 [768, 768], P(('seq', 'dp'))
- new_value: float32 [768, 768], P(('seq', 'dp'))
- new_output: float32 [768, 768], P(('seq', 'dp'))
- new_gate: float32 [768, 3072], P(('seq', 'dp'))
- new_up: float32 [768, 3072], P(('seq', 'dp'))
- new_down: float32 [3072, 768], P(('seq', 'dp'))
- new_gains: float32 [768, 2], P(('seq', 'dp'))
- moment_query: float32 [768, 768], P(('seq', 'dp'))
- moment_key: float32 [768, 768], P(('seq', 'dp'))
- moment_value: float32 [768, 768], P(('seq', 'dp'))
- moment_output: float32 [768, 768], P(('seq', 'dp'))
- moment_gate: float32 [768, 3072], P(('seq', 'dp'))
- moment_up: float32 [768, 3072], P(('seq', 'dp'))
- moment_down: float32 [3072, 768], P(('seq', 'dp'))
- moment_gains: float32 [768, 2], P(('seq', 'dp'))
- mean_query: float32 [768, 768], P(('seq', 'dp'))
- mean_key: float32 [768, 768], P(('seq', 'dp'))
- mean_value: float32 [768, 768], P(('seq', 'dp'))
- mean_output: float32 [768, 768], P(('seq', 'dp'))
- mean_gate: float32 [768, 3072], P(('seq', 'dp'))
- mean_up: float32 [768, 3072], P(('seq', 'dp'))
- mean_down: float32 [3072, 768], P(('seq', 'dp'))
- mean_gains: float32 [768, 2], P(('seq', 'dp'))
- copy_query: bfloat16 [768, 768], P(('seq', 'dp'))
- copy_key: bfloat16 [768, 768], P(('seq', 'dp'))
- copy_value: bfloat16 [768, 768], P(('seq', 'dp'))
- copy_output: bfloat16 [768, 768], P(('seq', 'dp'))
- copy_gate: bfloat16 [768, 3072], P(('seq', 'dp'))
- copy_up: bfloat16 [768, 3072], P(('seq', 'dp'))
- copy_down: bfloat16 [3072, 768], P(('seq', 'dp'))
- copy_gains: bfloat16 [768, 2], P(('seq', 'dp'))
The draws below stay inside these ranges and needn't reach their ends.
Inputs may be any that keep to these rules, and one draw needn't show every extreme that they name: `doc_ids`: ids never fall along a sequence and start at 0; in every sequence one document begins within the first device's block of 128 tokens and ends within the last one's.
All inputs are finite; a program needn't handle non-finite values.
Results may differ from the reference program's by a relative error of at most 0.02.
Values may be sent and summed in bfloat16 or wider, within the bound.
No kernel may reach another device: no remote copies, remote signals or barrier semaphores. Data moves between devices by JAX's collectives and lax.ppermute only.
A program may use at most 192 MiB of HBM per device.

```python
import math
import jax
import jax.numpy as jnp
from jax import lax

D = 768
H = 12
KV = 12
HD = 64
FF = 3072
LENGTH = 1024
SPAN = 128
SEQS = 16
TOKENS = 16384


def draw_doc_ids(key, part):
    key = jax.random.fold_in(key, 11)
    keys = jax.random.split(key, 4)
    half = SPAN // 2
    first_cut = jax.random.randint(keys[0], (SEQS, 1), 1, half)
    open_doc = first_cut + jax.random.randint(keys[1], (SEQS, 1), 1, half)
    close_doc = LENGTH - SPAN + jax.random.randint(keys[2], (SEQS, 1), 1, half)
    last_cut = close_doc + jax.random.randint(keys[3], (SEQS, 1), 1, half)
    places = jnp.arange(LENGTH, dtype=jnp.int32)[None, :]
    ids = (places >= first_cut).astype(jnp.int32) + (places >= open_doc).astype(jnp.int32)
    ids = ids + (places >= close_doc).astype(jnp.int32) + (places >= last_cut).astype(jnp.int32)
    return ids.astype(jnp.int32)


def steps_of(own_key, extent, cuts, smallest, top_value):
    factor_of = 1.0
    for position, shards_of in cuts:
        heights = jax.random.uniform(jax.random.fold_in(jax.random.fold_in(own_key, 6), position), (shards_of,), jnp.float32, smallest / len(cuts), top_value / len(cuts))
        factor_of = factor_of * jnp.repeat(jnp.exp(heights), extent[position] // shards_of).reshape((-1,) + (1,) * (len(extent) - 1 - position))
    return factor_of


def centred(stream_key, dims, deviation, bound, pieces=(), kind=jnp.bfloat16):
    loudness = steps_of(stream_key, dims, pieces, -0.22, 0.18) if pieces else 1.0
    drawn = jax.random.normal(stream_key, dims, jnp.float32) * deviation * loudness
    return jnp.minimum(jnp.maximum(drawn, -bound), bound).astype(kind)


def setup_inputs(seed: int = 0) -> dict:
    streams_of = jax.random.split(jax.random.key(seed), 28)
    return {
        "inputs": centred(streams_of[0], (SEQS, LENGTH, D), 1.0, 6.0, ((0, 16), (1, 8))),
        "doc_ids": draw_doc_ids(jax.random.fold_in(streams_of[27], 71), 0),
        "cotangent": centred(streams_of[2], (SEQS, LENGTH, D), 1.0, 6.0, ((0, 16), (1, 8))),
        "w_query": centred(streams_of[3], (D, H * HD), D ** -0.5, 0.21875, ((0, 128),), jnp.float32),
        "w_key": centred(streams_of[4], (D, KV * HD), D ** -0.5, 0.21875, ((0, 128),), jnp.float32),
        "w_value": centred(streams_of[5], (D, KV * HD), D ** -0.5, 0.21875, ((0, 128),), jnp.float32),
        "w_output": centred(streams_of[6], (H * HD, D), (max(1, H * HD * 4 // LENGTH)) ** -0.5, 3.5, ((0, 128),), jnp.float32),
        "w_gate": centred(streams_of[7], (D, FF), D ** -0.5, 0.21875, ((0, 128),), jnp.float32),
        "w_up": centred(streams_of[8], (D, FF), D ** -0.5, 0.21875, ((0, 128),), jnp.float32),
        "w_down": centred(streams_of[9], (FF, D), FF ** -0.5, 0.109375, ((0, 128),), jnp.float32),
        "norm_gains": jnp.clip(1.0 + 0.1 * jax.random.normal(streams_of[10], (D, 2), jnp.float32), 0.5, 1.5),
        "mom_query": centred(streams_of[11], (D, H * HD), (0.1 * TOKENS ** 0.5), 80.0, ((0, 128),), jnp.float32),
        "mom_key": centred(streams_of[12], (D, KV * HD), (0.1 * TOKENS ** 0.5), 80.0, ((0, 128),), jnp.float32),
        "mom_value": centred(streams_of[13], (D, KV * HD), (0.1 * TOKENS ** 0.5), 80.0, ((0, 128),), jnp.float32),
        "mom_output": centred(streams_of[14], (H * HD, D), (0.15 * SEQS ** 0.5), 3.5, ((0, 128),), jnp.float32),
        "mom_gate": centred(streams_of[15], (D, FF), (0.05 * TOKENS ** 0.5), 40.0, ((0, 128),), jnp.float32),
        "mom_up": centred(streams_of[16], (D, FF), (0.05 * TOKENS ** 0.5), 40.0, ((0, 128),), jnp.float32),
        "mom_down": centred(streams_of[17], (FF, D), (0.05 * TOKENS ** 0.5), 40.0, ((0, 128),), jnp.float32),
        "mom_gains": centred(streams_of[18], (D, 2), (0.1 * TOKENS ** 0.5), 80.0, ((0, 128),), jnp.float32),
        "avg_query": centred(streams_of[19], (D, H * HD), D ** -0.5, 0.21875, ((0, 128),), jnp.float32),
        "avg_key": centred(streams_of[20], (D, KV * HD), D ** -0.5, 0.21875, ((0, 128),), jnp.float32),
        "avg_value": centred(streams_of[21], (D, KV * HD), D ** -0.5, 0.21875, ((0, 128),), jnp.float32),
        "avg_output": centred(streams_of[22], (H * HD, D), (max(1, H * HD * 4 // LENGTH)) ** -0.5, 3.5, ((0, 128),), jnp.float32),
        "avg_gate": centred(streams_of[23], (D, FF), D ** -0.5, 0.21875, ((0, 128),), jnp.float32),
        "avg_up": centred(streams_of[24], (D, FF), D ** -0.5, 0.21875, ((0, 128),), jnp.float32),
        "avg_down": centred(streams_of[25], (FF, D), FF ** -0.5, 0.109375, ((0, 128),), jnp.float32),
        "avg_gains": jnp.clip(1.0 + 0.1 * jax.random.normal(streams_of[26], (D, 2), jnp.float32), 0.5, 1.5),
    }


@jax.custom_vjp
def low(v):
    return lax.optimization_barrier(v.astype(jnp.bfloat16)).astype(jnp.float32)

@jax.custom_vjp
def low_back(v):
    return v

def low_keep(v):
    return (low(v), None)

def low_pass(kept, grad):
    return (grad,)

def back_keep(v):
    return (v, None)

def back_low(kept, grad):
    return (low(grad),)
low.defvjp(low_keep, low_pass)
low_back.defvjp(back_keep, back_low)
EPS = 1e-05
MOMENTUM = 0.9
AVERAGE = 0.5
RATES = (0.01, 0.01, 0.01, 4.0, 0.02, 0.02, 0.015, 0.1)
MASKED = -1e+30
HIGH = lax.Precision.HIGHEST

def matmul(left, right):
    return jnp.dot(left, right, precision=HIGH)

def turn_angles(ids):
    starts = lax.optimization_barrier(jnp.sum((ids[None, :] < ids[:, None]).astype(jnp.int32), axis=1))
    places = jnp.arange(ids.shape[0], dtype=jnp.int32) - starts
    freq = 10000.0 ** (-jnp.arange(0, HD, 2, dtype=jnp.float32) / HD)
    theta = places.astype(jnp.float32)[:, None] * freq[None, :]
    theta = jnp.concatenate([theta, theta], axis=-1)
    return (jnp.cos(theta), jnp.sin(theta))

def rotate(vecs, cosine, sine):
    half = vecs.shape[-1] // 2
    turned = jnp.concatenate([-vecs[..., half:], vecs[..., :half]], axis=-1)
    return vecs * cosine[:, None, :] + turned * sine[:, None, :]

def normed(values, gain):
    scale = lax.rsqrt(lax.optimization_barrier(jnp.mean(values * values, axis=-1, keepdims=True)) + EPS)
    return values * scale * gain

def layer(x, ids, weights):
    wq, wk, wv, wo, wg, wu, wd, gains = weights
    length = x.shape[0]
    group = H // KV
    cosine, sine = turn_angles(ids)
    h1 = low(normed(x, gains[:, 0]))
    q = low_back(matmul(h1, wq)).reshape(length, H, HD)
    k = low_back(matmul(h1, wk)).reshape(length, KV, HD)
    v = low(low_back(matmul(h1, wv))).reshape(length, KV, HD)
    q = low(rotate(q, cosine, sine)).reshape(length, KV, group, HD)
    k = low(rotate(k, cosine, sine))
    scores = jnp.einsum('qkgd,skd->kgqs', q, k, precision=HIGH) * HD ** (-0.5)
    scores = low_back(scores)
    index = jnp.arange(length, dtype=jnp.int32)
    allowed = (ids[:, None] == ids[None, :]) & (index[None, :] <= index[:, None])
    scores = jnp.where(allowed[None, None], scores, MASKED)
    probs = low(jax.nn.softmax(scores, axis=-1))
    mixed = jnp.einsum('kgqs,skd->qkgd', probs, v, precision=HIGH).reshape(length, H * HD)
    mixed = low(low_back(mixed))
    resid = x + low_back(matmul(mixed, wo))
    h2 = low(normed(resid, gains[:, 1]))
    gate = low_back(matmul(h2, wg))
    up = low_back(matmul(h2, wu))
    hidden = low(jax.nn.silu(gate) * up)
    return resid + matmul(hidden, wd)

def update(master, moment, average, grad, rate):
    moment_new = MOMENTUM * moment + grad
    weight_new = master - rate * (grad + MOMENTUM * moment_new)
    mean_new = AVERAGE * average + (1.0 - AVERAGE) * weight_new
    return (weight_new, moment_new, mean_new, weight_new.astype(jnp.bfloat16))

def reference(inputs, doc_ids, cotangent, w_query, w_key, w_value, w_output, w_gate, w_up, w_down, norm_gains, mom_query, mom_key, mom_value, mom_output, mom_gate, mom_up, mom_down, mom_gains, avg_query, avg_key, avg_value, avg_output, avg_gate, avg_up, avg_down, avg_gains):
    masters = (w_query, w_key, w_value, w_output, w_gate, w_up, w_down, norm_gains)
    moments = (mom_query, mom_key, mom_value, mom_output, mom_gate, mom_up, mom_down, mom_gains)
    averages = (avg_query, avg_key, avg_value, avg_output, avg_gate, avg_up, avg_down, avg_gains)

    def forward(values, weights):
        used = tuple((low(w) for w in weights))

        def step(carry, item):
            return (carry, jax.checkpoint(layer)(item[0], item[1], used))
        _, outs = lax.scan(step, jnp.zeros((), jnp.float32), (values, doc_ids))
        return outs
    values = inputs.astype(jnp.float32)
    weights = tuple((w.astype(jnp.float32) for w in masters))
    result, pullback = jax.vjp(forward, values, weights)
    input_grad, grads = pullback(cotangent.astype(jnp.float32))
    base = 1.0 / math.sqrt(TOKENS)
    done = [update(masters[i], moments[i], averages[i], grads[i], RATES[i] * base) for i in range(8)]
    news = [item[0] for item in done]
    moms = [item[1] for item in done]
    means = [item[2] for item in done]
    copies = [item[3] for item in done]
    return (result.astype(jnp.bfloat16), input_grad, news[0], news[1], news[2], news[3], news[4], news[5], news[6], news[7], moms[0], moms[1], moms[2], moms[3], moms[4], moms[5], moms[6], moms[7], means[0], means[1], means[2], means[3], means[4], means[5], means[6], means[7], copies[0], copies[1], copies[2], copies[3], copies[4], copies[5], copies[6], copies[7])
```

```python
import math

import jax
import jax.numpy as jnp
import numpy as np
from jax import lax
from jax.experimental import pallas as pl
from jax.experimental.pallas import tpu as pltpu
from jax.sharding import Mesh
from jax.sharding import PartitionSpec as P


BF = jnp.bfloat16
F32 = jnp.float32
HD = 64
D = 768
FF = 3072
HALF = 384
PACK = 1024
TOK = 256
LEN = 1024
HEADS = 6
EPS = 1e-05
MOMENTUM = 0.9
AVERAGE = 0.5
RATES = (0.01, 0.01, 0.01, 4.0, 0.02, 0.02, 0.015, 0.1)
MASKED = -1e30
AXES = ("z", "core", "y", "x")
VMEM_LIMIT = 60 * 1024 * 1024


def params():
    return pltpu.CompilerParams(vmem_limit_bytes=VMEM_LIMIT)


def device_pairs(move):
    pairs = []
    for z in range(4):
        for c in range(2):
            for y in range(4):
                for x in range(4):
                    to = move(z, c, y, x)
                    pairs.append((((z * 2 + c) * 4 + y) * 4 + x, ((to[0] * 2 + to[1]) * 4 + to[2]) * 4 + to[3]))
    return pairs


CORE_PAIRS = device_pairs(lambda z, c, y, x: (z, 1 - c, y, x))


def z_shift(k):
    return device_pairs(lambda z, c, y, x: ((z + k) % 4, c, y, x))


def halving_pairs(axis, first):
    def move(z, c, y, x):
        flip = 3 if (c == 0) == first else 1
        at = [z, c, y, x]
        at[axis] ^= flip
        return tuple(at)

    return device_pairs(move)


AXIS = {"z": 0, "y": 2, "x": 3}
ORDERS = (("x", "y", "z"), ("y", "z", "x"), ("z", "x", "y"))
LAST = ("x", "y", "z")


def permute(value, pairs):
    return lax.ppermute(value, AXES, pairs)


def chip_of_place(me, core):
    place = np.arange(64)
    rows = []
    for order in ORDERS:
        first = {axis: (place >> (5 - k)) & 1 for k, axis in enumerate(order)}
        second = {axis: (place >> (2 - k)) & 1 for k, axis in enumerate(LAST)}
        at = {}
        for axis in "zyx":
            one, two = jnp.asarray(first[axis]), jnp.asarray(second[axis])
            high = jnp.where(core == 0, one, two)
            low = jnp.where(core == 0, two, one)
            mine = me[axis]
            high = high ^ (mine >> 1)
            low = low ^ ((mine >> 1) ^ (mine & 1))
            at[axis] = high * 2 + (high ^ low)
        rows.append(at["z"] * 16 + at["y"] * 4 + at["x"])
    return jnp.stack(rows).astype(jnp.int32)


def spread_matrix():
    feature = lax.broadcasted_iota(jnp.int32, (HALF, 512), 0)
    place = lax.broadcasted_iota(jnp.int32, (HALF, 512), 1)
    z, rest = place // 256, place % 256
    yx, core, row = rest // 16, (rest // 8) % 2, rest % 8
    want = ((z * 2 + core) * 16 + yx) * 6 + row
    return ((feature == want) & (row < 6)).astype(BF)


def dot(left, right):
    return jnp.dot(left, right, preferred_element_type=F32)


def dot_nt(left, right):
    return lax.dot_general(left, right, (((1,), (1,)), ((), ())), preferred_element_type=F32)


def dot_tn(left, right):
    return lax.dot_general(left, right, (((0,), (0,)), ((), ())), preferred_element_type=F32)


def spread(values, e2):
    return jnp.concatenate([dot(values[:, :HALF], e2), dot(values[:, HALF:], e2)], axis=1).astype(BF)


def gather_back(values, e2):
    high = values.astype(BF)
    low = (values - high.astype(F32)).astype(BF)
    return jnp.concatenate(
        [dot_nt(high[:, k : k + 512], e2) + dot_nt(low[:, k : k + 512], e2) for k in (0, 512)], axis=1
    )


def swap_halves(tile):
    lane = lax.broadcasted_iota(jnp.int32, tile.shape, 1)
    return jnp.where(lane % HD < HD // 2, pltpu.roll(tile, 96, 1), pltpu.roll(tile, 32, 1))


def lanes_of(tile, odd):
    lane = lax.broadcasted_iota(jnp.int32, tile.shape, 1)
    return jnp.where((lane >= HD) == bool(odd), tile, jnp.zeros_like(tile))


def join_lanes(even, odd):
    lane = lax.broadcasted_iota(jnp.int32, even.shape, 1)
    return jnp.where(lane < HD, even, odd)


def pack_kernel(scal, wq, wk, wv, wo, wg, wu, wd, gains, keep, send, down):
    core = scal[1]
    k = 0
    for w in (wq, wk, wv, wo, wg, wu):
        count = w.shape[1] // D
        for part in range(count):
            halves = [w[:, part * D + h * HALF : part * D + (h + 1) * HALF] for h in range(2)]
            keep[k, 0:6, :] = jnp.where(core == 0, halves[0], halves[1])
            send[k, 0:6, :] = jnp.where(core == 0, halves[1], halves[0])
            keep[k, 6:8, :] = jnp.zeros((2, HALF), F32)
            send[k, 6:8, :] = jnp.zeros((2, HALF), F32)
            k += 1
    lane = lax.broadcasted_iota(jnp.int32, (6, HALF), 1)
    row = lax.broadcasted_iota(jnp.int32, (6, HALF), 0)
    here = lane == row + core * 8
    for col in range(2):
        line = jnp.sum(jnp.where(here, gains[:, col : col + 1], 0.0), axis=0, keepdims=True)
        keep[0, 6 + col : 7 + col, :] = line
        send[0, 6 + col : 7 + col, :] = line
    for j in range(3):
        rows = wd[8 * j : 8 * j + 8, :]
        down[j] = jnp.concatenate([rows[:, :HALF], rows[:, HALF:]], axis=0).astype(BF)


def attn_forward_kernel(
    scal, xp, gq, gk, gv, cosine, sine, start, e2, q_all, k_all, v_all, h1_own, probs, o_out, g1_out, g2_out, h1p, bias
):
    z = scal[0]
    own = pl.multiple_of(z * TOK, TOK)
    held = gq[:, 0, :, 0:128].astype(F32)
    rows = lax.broadcasted_iota(jnp.int32, held.shape, 1)
    lane = lax.broadcasted_iota(jnp.int32, held.shape, 2)
    chip = lax.broadcasted_iota(jnp.int32, (64, PACK), 0)
    place = lax.broadcasted_iota(jnp.int32, (64, PACK), 1)
    take = lax.broadcasted_iota(jnp.int32, (128, PACK), 0)
    fold = (take == lax.broadcasted_iota(jnp.int32, (128, PACK), 1) % 16).astype(BF)
    lines = []
    for k in range(2):
        wanted = (rows == jnp.where(lane < 8, 6 + k, 14 + k)) & (lane < 16)
        table = jnp.sum(jnp.where(wanted, held, 0.0), axis=1).astype(BF)
        wide = dot(table, fold)
        lines.append(jnp.sum(jnp.where(place // 16 == chip, wide, 0.0), axis=0, keepdims=True))
    g1 = lines[0]
    g1_out[...] = jnp.broadcast_to(g1, (8, PACK))
    g2 = jnp.broadcast_to(lines[1], (8, PACK)).astype(BF)
    g2_out[...] = jnp.concatenate([dot_nt(g2[:, :512], e2[...]), dot_nt(g2[:, 512:], e2[...])], axis=1)

    wq, wk, wv = (w[...].reshape(PACK, HALF) for w in (gq, gk, gv))

    def block(b, carry):
        at = pl.ds(pl.multiple_of(b * TOK, TOK), TOK)
        x = xp[at, :].astype(F32)
        scale = lax.rsqrt(jnp.sum(x * x, axis=1, keepdims=True) * (1.0 / D) + EPS)
        h1 = (x * scale * g1).astype(BF)
        h1p[at, :] = h1
        cs, sn = cosine[at, :], sine[at, :]
        for w, out, factor in ((wq, q_all, 0.125), (wk, k_all, 1.0)):
            raw = dot(h1, w)
            for t in range(3):
                u = raw[:, 128 * t : 128 * t + 128]
                turned = (u * cs + swap_halves(u) * sn).astype(BF)
                out[at, 128 * t : 128 * t + 128] = turned * BF(factor)
        v_all[at, :] = dot(h1, wv).astype(BF)
        return carry

    lax.fori_loop(0, 4, block, 0)
    h1_own[...] = h1p[pl.ds(own, TOK), :]

    key = lax.broadcasted_iota(jnp.int32, (TOK, LEN), 1).astype(F32)
    query = (lax.broadcasted_iota(jnp.int32, (TOK, LEN), 0) + own).astype(F32)
    first = start[pl.ds(own, TOK), :]
    bias[...] = jnp.where((key >= first) & (key <= query), 0.0, MASKED)
    lane = lax.broadcasted_iota(jnp.int32, (TOK, 128), 1)
    logs = jnp.zeros((TOK, 128), F32)
    for t in range(3):
        cols = slice(128 * t, 128 * t + 128)
        q_tile = q_all[pl.ds(own, TOK), cols]
        k_tile = k_all[:, cols]
        v_tile = v_all[:, cols]
        mixed = []
        for odd in range(2):
            h = 2 * t + odd
            s = dot_nt(lanes_of(q_tile, odd), k_tile) + bias[...]
            top = jnp.max(s, axis=1, keepdims=True)
            expo = jnp.exp(s - top)
            total = jnp.sum(expo, axis=1, keepdims=True)
            pb = (expo * (1.0 / total)).astype(BF)
            probs[h] = pb
            mixed.append(dot(pb, v_tile))
            logs = jnp.where(lane == h, top + jnp.log(total), logs)
        o_out[:, cols] = join_lanes(mixed[0], mixed[1]).astype(BF)
    high = logs.astype(BF).astype(F32)
    mid = (logs - high).astype(BF).astype(F32)
    low = logs - high - mid
    packed = jnp.where(lane < 8, high, jnp.where(lane < 16, pltpu.roll(mid, 8, 1), pltpu.roll(low, 16, 1)))
    o_out[:, HALF:] = jnp.where(lane < 24, packed, 0.0).astype(BF)


def attn_out_kernel(scal, o, wo_keep, wo_other, e2, part):
    core = scal[1]
    spread_o = dot(o[:, :HALF], e2[...]).astype(BF)
    mine = dot(spread_o, wo_keep[...].reshape(512, HALF))
    other = dot(spread_o, wo_other[...].reshape(512, HALF))
    part[:, :HALF] = jnp.where(core == 0, mine, other)
    part[:, HALF:] = jnp.where(core == 0, other, mine)


def ffn_kernel(
    scal,
    chips,
    x,
    part_a,
    part_b,
    dy,
    e2,
    g2,
    wg,
    wu,
    wd,
    out_keep,
    out_send,
    dh2_out,
    resid,
    gg2,
    keep_g,
    send_g,
    keep_u,
    send_u,
    keep_d,
    send_d,
    h2p,
    h2p_t,
    acc_out,
    acc_dh2,
    grad,
    grad_d,
):
    core = scal[1]
    j = pl.program_id(0)

    @pl.when(j == 0)
    def _():
        r = x[...].astype(F32) + (part_a[...] + part_b[...])
        resid[...] = r
        scale = lax.rsqrt(jnp.mean(r * r, axis=1, keepdims=True) + EPS)
        h2 = (r * scale * g2[0:1, :]).astype(BF)
        packed = spread(h2, e2[...])
        h2p[...] = packed
        h2p_t[...] = packed.T
        acc_out[...] = jnp.zeros_like(acc_out)
        acc_dh2[...] = jnp.zeros_like(acc_dh2)

    w_gate = wg[...].reshape(PACK, HALF)
    w_up = wu[...].reshape(PACK, HALF)
    blocks = wd[...].astype(F32)
    w_down = jnp.concatenate(
        [blocks[:, :, 0:8, :].reshape(HALF, HALF), blocks[:, :, 8:16, :].reshape(HALF, HALF)], axis=1
    ).astype(BF)
    h2 = h2p[...]
    gate = dot(h2, w_gate)
    up = dot(h2, w_up)
    sig = jax.nn.sigmoid(gate)
    hidden = (gate * sig * up).astype(BF)
    acc_out[...] += dot(hidden, w_down)
    dhid = dot_nt(dy[...], w_down)
    dgate = (dhid * up * sig * (1.0 + gate * (1.0 - sig))).astype(BF)
    dup = (dhid * gate * sig).astype(BF)
    acc_dh2[...] += dot_nt(dgate, w_gate) + dot_nt(dup, w_up)

    for part, value, keep, send in ((0, dgate, keep_g, send_g), (1, dup, keep_u, send_u)):
        grad[...] = dot(h2p_t[...], value)

        def write(w, carry, part=part, keep=keep, send=send):
            a = pl.multiple_of(chips[part, w] * 16, 16)
            b = pl.multiple_of(chips[part, w + 32] * 16, 16)
            keep[w, 0] = grad[pl.ds(a, 16), :].astype(BF)
            send[w, 0] = grad[pl.ds(b, 16), :].astype(BF)
            return carry

        lax.fori_loop(0, 32, write, 0)
    grad_d[pl.ds(pl.multiple_of(j * HALF, HALF), HALF), :] = dot_tn(hidden, dy[...])

    @pl.when(j == 3)
    def _():
        mine = pl.multiple_of(core * 128, 128)
        other = pl.multiple_of((1 - core) * 128, 128)
        out_keep[...] = acc_out[pl.ds(mine, 128), :]
        out_send[...] = acc_out[pl.ds(other, 128), :]
        dh2 = gather_back(acc_dh2[...], e2[...])
        dh2_out[...] = dh2
        r = resid[...]
        scale = lax.rsqrt(jnp.mean(r * r, axis=1, keepdims=True) + EPS)
        gg2[...] = jnp.broadcast_to(jnp.sum(dh2 * r * scale, axis=0, keepdims=True), (8, D))

        def write(w, carry):
            for at, out in ((w, keep_d), (w + 32, send_d)):
                base = chips[2, at] * 24
                for k in range(3):
                    rows = grad_d[pl.ds(pl.multiple_of(base + 8 * k, 8), 8), :]
                    out[w, k] = jnp.concatenate([rows[:, :HALF], rows[:, HALF:]], axis=0).astype(BF)
            return carry

        lax.fori_loop(0, 32, write, 0)


def resid_backward_kernel(scal, resid, dh2_a, dh2_b, g2, dy, wo_keep, wo_other, e2, dres_out, dresb_out, do_out):
    core = scal[1]
    r = resid[...]
    dh2 = dh2_a[...] + dh2_b[...]
    scale = lax.rsqrt(jnp.mean(r * r, axis=1, keepdims=True) + EPS)
    weighted = dh2 * g2[0:1, :]
    inner = jnp.mean(weighted * r, axis=1, keepdims=True)
    dres = dy[...].astype(F32) + (scale * weighted - r * (scale * scale * scale) * inner)
    mine = pl.multiple_of(core * 128, 128)
    dresb = dres.astype(BF)
    dresb_out[...] = dresb
    d_mine = jnp.where(core == 0, dresb[:, :HALF], dresb[:, HALF:])
    d_other = jnp.where(core == 0, dresb[:, HALF:], dresb[:, :HALF])
    do = dot_nt(d_mine, wo_keep[...].reshape(512, HALF)) + dot_nt(d_other, wo_other[...].reshape(512, HALF))
    do_out[...] = dot_nt(do.astype(BF), e2[...]).astype(BF)
    resid_rows = dres
    dres_out[0] = resid_rows[0:128, :]
    dres_out[1] = resid_rows[128:256, :]
    del mine


def attn_query_kernel(scal, probs, do, o, k_all, v_all, cosine, sine, dq_out):
    own = pl.multiple_of(scal[0] * TOK, TOK)
    cs, sn = cosine[pl.ds(own, TOK), :], sine[pl.ds(own, TOK), :]
    for t in range(3):
        cols = slice(128 * t, 128 * t + 128)
        do_tile = do[:, cols]
        product = do_tile.astype(F32) * o[:, cols].astype(F32)
        k_tile, v_tile = k_all[:, cols], v_all[:, cols]
        both = []
        for odd in range(2):
            inner = jnp.sum(lanes_of(product, odd), axis=1, keepdims=True)
            dp = dot_nt(lanes_of(do_tile, odd), v_tile)
            ds = (probs[2 * t + odd].astype(F32) * (dp - inner)).astype(BF)
            both.append(dot(ds, k_tile))
        u = join_lanes(both[0], both[1]) * 0.125
        dq_out[:, cols] = (u * cs - swap_halves(u) * sn).astype(BF)


def attn_key_kernel(
    scal, q_all, k_all, v_all, do0, do1, do2, do3, o0, o1, o2, o3, start, cosine, sine, dk_out, dv_out, dk_acc, dv_acc
):
    z = scal[0]
    own = pl.multiple_of(z * TOK, TOK)
    head = lax.broadcasted_iota(jnp.int32, (8, 128), 0)
    lane = lax.broadcasted_iota(jnp.int32, (8, 128), 1)
    pick = ((lane < 24) & (lane % 8 == head)).astype(BF)
    head_of = (
        lax.broadcasted_iota(jnp.int32, (8, HALF), 1) // HD == lax.broadcasted_iota(jnp.int32, (8, HALF), 0)
    ).astype(F32)
    dk_acc[...] = jnp.zeros_like(dk_acc)
    dv_acc[...] = jnp.zeros_like(dv_acc)
    key = (lax.broadcasted_iota(jnp.int32, (TOK, TOK), 0) + own).astype(F32)
    for k, (do, o) in enumerate(((do0, o0), (do1, o1), (do2, o2), (do3, o3))):
        zq = lax.rem(z + 4 - k, 4)

        @pl.when(zq >= z)
        def _(do=do, o=o, zq=zq):
            at = pl.multiple_of(zq * TOK, TOK)
            logs = dot_nt(pick, o[:, HALF:])
            inner = lax.dot_general(
                head_of,
                do[...].astype(F32) * o[:, :HALF].astype(F32),
                (((1,), (1,)), ((), ())),
                precision=lax.Precision.HIGHEST,
                preferred_element_type=F32,
            )
            query = (lax.broadcasted_iota(jnp.int32, (TOK, TOK), 1) + at).astype(F32)
            seen = (key >= start[0:1, pl.ds(at, TOK)]) & (key <= query)
            bias = jnp.where(seen, 0.0, MASKED)
            for t in range(3):
                cols = slice(128 * t, 128 * t + 128)
                q_tile, do_tile = q_all[pl.ds(at, TOK), cols], do[:, cols]
                k_tile, v_tile = k_all[pl.ds(own, TOK), cols], v_all[pl.ds(own, TOK), cols]
                dks, dvs = [], []
                for odd in range(2):
                    h = 2 * t + odd
                    s = dot_nt(lanes_of(k_tile, odd), q_tile) + bias
                    p = jnp.exp(s - logs[h : h + 1, :])
                    dvs.append(dot(p.astype(BF), do_tile))
                    dp = dot_nt(lanes_of(v_tile, odd), do_tile)
                    ds = (p * (dp - inner[h : h + 1, :])).astype(BF)
                    dks.append(dot(ds, q_tile))
                dk_acc[:, cols] += join_lanes(dks[0], dks[1])
                dv_acc[:, cols] += join_lanes(dvs[0], dvs[1])

    cs, sn = cosine[pl.ds(own, TOK), :], sine[pl.ds(own, TOK), :]
    for t in range(3):
        cols = slice(128 * t, 128 * t + 128)
        u = dk_acc[:, cols]
        dk_out[:, cols] = (u * cs - swap_halves(u) * sn).astype(BF)
    dv_out[...] = dv_acc[...].astype(BF)


def attn_grads_kernel(
    scal,
    chips,
    dq,
    dk,
    dv,
    xp,
    h1,
    o_mine,
    o_other,
    dresb,
    gg2,
    gq,
    gk,
    gv,
    e2,
    dh1_keep,
    dh1_send,
    k0,
    k1,
    k2,
    s0,
    s1,
    s2,
    grad,
    grad_o,
    lines,
    dh1,
):
    core = scal[1]
    own = pl.multiple_of(scal[0] * TOK, TOK)
    e = e2[...]
    wq, wk, wv = (w[...].reshape(PACK, HALF) for w in (gq, gk, gv))
    dh1[...] = dot_nt(dq[...], wq) + dot_nt(dk[...], wk) + dot_nt(dv[...], wv)
    dh1_keep[...] = dh1[pl.ds(pl.multiple_of(core * 128, 128), 128), :]
    dh1_send[...] = dh1[pl.ds(pl.multiple_of((1 - core) * 128, 128), 128), :]
    x = xp[pl.ds(own, TOK), :].astype(F32)
    scale = lax.rsqrt(jnp.sum(x * x, axis=1, keepdims=True) * (1.0 / D) + EPS)
    gg1 = jnp.sum(dh1[...] * x * scale, axis=0, keepdims=True)
    g2_wide = spread(gg2[...].astype(BF), e).astype(F32)[0:1, :]
    chip = lax.broadcasted_iota(jnp.int32, (64, PACK), 0)
    place = lax.broadcasted_iota(jnp.int32, (64, PACK), 1)
    fold = (
        lax.broadcasted_iota(jnp.int32, (128, PACK), 0) == lax.broadcasted_iota(jnp.int32, (128, PACK), 1) % 16
    ).astype(BF)
    for k, line in enumerate((gg1, g2_wide)):
        lines[k] = dot_nt(jnp.where(place // 16 == chip, line, 0.0).astype(BF), fold)

    h1_t = h1[...].T
    for p, value in enumerate((dq, dk, dv)):
        grad[p] = dot(h1_t, value[...])
    o_a, o_b = o_mine[:, :HALF], o_other[:, :HALF]
    o_full = jnp.concatenate(
        [dot(jnp.where(core == 0, o_a, o_b), e), dot(jnp.where(core == 0, o_b, o_a), e)], axis=1
    ).astype(BF)
    d_mine = jnp.where(core == 0, dresb[:, :HALF], dresb[:, HALF:])
    grad_o[...] = dot_tn(o_full, d_mine)

    row = lax.broadcasted_iota(jnp.int32, (16, 128), 0)
    lane = lax.broadcasted_iota(jnp.int32, (16, 128), 1)
    row_one = row == jnp.where(lane < 8, 6, 14)
    row_two = row == jnp.where(lane < 8, 7, 15)
    used = lane < 16

    def write(w, carry):
        for p, (keep, send) in enumerate(((k0, s0), (k1, s1), (k2, s2))):
            for at, out in ((w, keep), (w + 32, send)):
                i = chips[p, at]
                base = pl.multiple_of(i * 16, 16)
                block = grad[p, pl.ds(base, 16), :]
                if p == 0:
                    tile = block[:, :128]
                    tile = jnp.where(used & row_one, lines[0, pl.ds(i, 1), :], tile)
                    tile = jnp.where(used & row_two, lines[1, pl.ds(i, 1), :], tile)
                    out[w, :, 0:128] = tile.astype(BF)
                    out[w, :, 128:HALF] = block[:, 128:].astype(BF)
                else:
                    out[w, :, 0:HALF] = block.astype(BF)
                out[w, :, HALF:512] = grad_o[pl.ds(base, 16), 128 * p : 128 * p + 128].astype(BF)
        return carry

    lax.fori_loop(0, 32, write, 0)


def token_outputs_kernel(scal, xp, dh1_a, dh1_b, g1, dres, e2, resid, out_a, out_b, output, input_grad):
    core = scal[1]
    at = pl.multiple_of(scal[0] * TOK + core * 128, 128)
    x = xp[pl.ds(at, 128), :].astype(F32)
    scale = lax.rsqrt(jnp.sum(x * x, axis=1, keepdims=True) * (1.0 / D) + EPS)
    weighted = (dh1_a[...] + dh1_b[...]) * g1[0:1, :]
    inner = jnp.sum(weighted * x, axis=1, keepdims=True) * (1.0 / D)
    dx = scale * weighted - x * (scale * scale * scale) * inner
    input_grad[...] = dres[core] + gather_back(dx, e2[...])
    mine = pl.ds(pl.multiple_of(core * 128, 128), 128)
    output[...] = (resid[mine, :] + (out_a[...] + out_b[...])).astype(BF)


def update_kernel(scal, attn_a, attn_b, ff_a, ff_b, *refs):
    core = scal[1]
    masters, moments, averages = refs[0:8], refs[8:16], refs[16:24]
    news, moms, means, copies = refs[24:32], refs[32:40], refs[40:48], refs[48:56]
    base = 1.0 / math.sqrt(16384)

    def step(k, at, grad):
        rate = RATES[k] * base
        moment = MOMENTUM * moments[k][at] + grad
        new = masters[k][at] - rate * (grad + MOMENTUM * moment)
        news[k][at] = new
        moms[k][at] = moment
        means[k][at] = AVERAGE * averages[k][at] + (1.0 - AVERAGE) * new
        copies[k][at] = new.astype(BF)

    def halves(a, b):
        return (jnp.where(core == 0, a, b), jnp.where(core == 0, b, a))

    for p in range(3):
        lo = 512 * p
        for h, grad in enumerate(halves(attn_a[0:6, lo : lo + HALF], attn_b[0:6, lo : lo + HALF])):
            step(p, (slice(0, 6), slice(h * HALF, (h + 1) * HALF)), grad)
        lo = 512 * p + HALF
        for h, grad in enumerate(halves(attn_a[0:6, lo : lo + 128], attn_b[0:6, lo : lo + 128])):
            at = h * HALF + 128 * p
            step(3, (slice(0, 6), slice(at, at + 128)), grad)
    for k in range(2):
        for j in range(4):
            for h, grad in enumerate(halves(ff_a[4 * k + j, 0:6, :], ff_b[4 * k + j, 0:6, :])):
                at = j * D + h * HALF
                step(4 + k, (slice(0, 6), slice(at, at + HALF)), grad)
    for j in range(3):
        for h in range(2):
            grad = ff_a[8 + j, 8 * h : 8 * h + 8, :]
            step(6, (slice(8 * j, 8 * j + 8), slice(h * HALF, (h + 1) * HALF)), grad)
    both = attn_a[6:8, 0:128] + attn_b[6:8, 0:128]
    row = lax.broadcasted_iota(jnp.int32, (6, 128), 0)
    lane = lax.broadcasted_iota(jnp.int32, (6, 128), 1)
    here = lane == row + 8 * core
    for col in range(2):
        grad = jnp.sum(jnp.where(here, both[col : col + 1, :], 0.0), axis=1, keepdims=True)
        step(7, (slice(0, 6), slice(col, col + 1)), grad)


def whole():
    return pl.BlockSpec(memory_space=pltpu.VMEM)


def scalars():
    return pl.BlockSpec(memory_space=pltpu.SMEM)


def call(kernel, out_shape, operands, scratch=(), smem=1, name=None):
    specs = [scalars() if k < smem else whole() for k in range(len(operands))]
    return pl.pallas_call(
        kernel,
        out_shape=out_shape,
        in_specs=specs,
        out_specs=jax.tree.map(lambda _: whole(), out_shape),
        scratch_shapes=list(scratch),
        compiler_params=params(),
        name=name,
    )(*operands)


def shape(dims, kind):
    return jax.ShapeDtypeStruct(dims, kind)


def halving(keep, send, steps):
    for k, (axis, first) in enumerate(steps):
        got = permute(send, halving_pairs(AXIS[axis], first))
        count = keep.shape[0] // 2
        total = keep.astype(F32) + got.astype(F32)
        if count == 0 or k == len(steps) - 1:
            return total
        total = total.astype(BF)
        keep, send = total[:count], total[count:]
    return keep


def reduce_parts(parts, join_axis):
    thirds = []
    for order, (keep, send) in zip(ORDERS, parts):
        thirds.append(halving(keep, send, [(axis, True) for axis in order]))
    joined = jnp.concatenate([t.astype(BF) for t in thirds], axis=join_axis)
    return halving(joined[:4], joined[4:], [(axis, False) for axis in LAST])[0]


def shards(inputs, doc_ids, cotangent, *state):
    masters, moments, averages = state[0:8], state[8:16], state[16:24]
    z, core = lax.axis_index("z"), lax.axis_index("core")
    y, x_at = lax.axis_index("y"), lax.axis_index("x")
    scal = jnp.stack([z, core]).astype(jnp.int32)
    chips = chip_of_place({"z": z, "y": y, "x": x_at}, core)
    e2 = spread_matrix()

    def by_core(mine, other, axis):
        return jnp.where(
            core == 0, jnp.concatenate([mine, other], axis=axis), jnp.concatenate([other, mine], axis=axis)
        )

    keep, send, down = call(
        pack_kernel,
        (shape((12, 8, HALF), F32), shape((12, 8, HALF), F32), shape((3, 16, HALF), BF)),
        (scal, *masters),
        name="pack_weights",
    )
    packed = by_core(keep, permute(send, CORE_PAIRS), 1).astype(BF)
    packed = jnp.concatenate([packed, down], axis=0)
    gathered = lax.all_gather(packed, ("z", "y", "x"), axis=0, tiled=False)

    ids_row = jnp.zeros((16, D), BF).at[0, :128].set(doc_ids[0].astype(BF))
    block = jnp.concatenate([inputs[0], ids_row], axis=0)
    ring = [block] + [permute(block, z_shift(k)) for k in (1, 2, 3)]
    ring = jnp.stack(ring)
    both = by_core(ring[:, None], permute(ring, CORE_PAIRS)[:, None], 1)
    both = jnp.roll(both[::-1], z + 1, axis=0)
    x_all = both[:, :, :128].reshape(LEN, D)
    ids = both[:, :, 128, :128].reshape(LEN).astype(F32)
    dy = by_core(cotangent[0], permute(cotangent[0], CORE_PAIRS), 0)
    starts = jnp.sum((ids[None, :] < ids[:, None]).astype(jnp.int32), axis=1)
    places = (jnp.arange(LEN, dtype=jnp.int32) - starts).astype(F32)
    freq = 10000.0 ** (-jnp.arange(0, HD, 2, dtype=F32) / HD)
    theta = places[:, None] * freq[None, :]
    cosine, sine = jnp.cos(theta), jnp.sin(theta)
    cosine = jnp.concatenate([cosine] * 4, axis=1)
    sine = jnp.concatenate([-sine, sine, -sine, sine], axis=1)
    start_col = starts.astype(F32)[:, None]
    start_row = jnp.broadcast_to(starts.astype(F32)[None, :], (8, LEN))
    xp = jnp.concatenate(
        [jnp.dot(x_all[:, :HALF], e2, preferred_element_type=F32), jnp.dot(x_all[:, HALF:], e2, preferred_element_type=F32)],
        axis=1,
    ).astype(BF)
    x_chip = lax.dynamic_slice_in_dim(x_all, z * TOK, TOK, 0)

    def chunk(k):
        return pl.BlockSpec((64, 1, 16, HALF), lambda i, k=k: (0, k, 0, 0))

    def full(dims):
        return pl.BlockSpec(dims, lambda i, n=len(dims): (0,) * n)

    forward_out = (
        shape((LEN, HALF), BF),
        shape((LEN, HALF), BF),
        shape((LEN, HALF), BF),
        shape((TOK, PACK), BF),
        shape((HEADS, TOK, LEN), BF),
        shape((TOK, 512), BF),
        shape((8, PACK), F32),
        shape((8, D), F32),
    )
    q_all, k_all, v_all, h1_own, probs, o, g1, g2 = pl.pallas_call(
        attn_forward_kernel,
        out_shape=forward_out,
        grid=(1,),
        in_specs=[
            scalars(),
            full((LEN, PACK)),
            chunk(0),
            chunk(1),
            chunk(2),
            full((LEN, 128)),
            full((LEN, 128)),
            full((LEN, 1)),
            full((HALF, 512)),
        ],
        out_specs=tuple(full(s.shape) for s in forward_out),
        scratch_shapes=[pltpu.VMEM((LEN, PACK), BF), pltpu.VMEM((TOK, LEN), F32)],
        compiler_params=params(),
        name="attention_forward",
    )(scal, xp, gathered, gathered, gathered, cosine, sine, start_col, e2)

    wo_keep = lax.dynamic_slice_in_dim(gathered, core * 32, 32, 0)[:, 3]
    wo_send = lax.dynamic_slice_in_dim(gathered, (1 - core) * 32, 32, 0)[:, 3]
    wo_other = permute(wo_send, CORE_PAIRS)
    part = call(attn_out_kernel, shape((TOK, D), F32), (scal, o, wo_keep, wo_other, e2), name="attention_output")
    part_other = permute(part, CORE_PAIRS)

    ffn_out = (
        shape((128, D), F32),
        shape((128, D), F32),
        shape((TOK, D), F32),
        shape((TOK, D), F32),
        shape((8, D), F32),
    ) + tuple(shape((32, 4, 16, HALF), BF) for _ in range(4)) + tuple(shape((32, 3, 16, HALF), BF) for _ in range(2))
    column = pl.BlockSpec((32, 1, 16, HALF), lambda j: (0, j, 0, 0))
    out_keep, out_send, dh2, resid, gg2, kg, sg, ku, su, kd, sd = pl.pallas_call(
        ffn_kernel,
        out_shape=ffn_out,
        grid=(4,),
        in_specs=[
            scalars(),
            scalars(),
            full((TOK, D)),
            full((TOK, D)),
            full((TOK, D)),
            full((TOK, D)),
            full((HALF, 512)),
            full((8, D)),
            pl.BlockSpec((64, 1, 16, HALF), lambda j: (0, 4 + j, 0, 0)),
            pl.BlockSpec((64, 1, 16, HALF), lambda j: (0, 8 + j, 0, 0)),
            pl.BlockSpec((16, 3, 16, HALF), lambda j: (j, 4, 0, 0)),
        ],
        out_specs=tuple(full(s.shape) for s in ffn_out[:5])
        + (column,) * 4
        + tuple(full(s.shape) for s in ffn_out[9:]),
        scratch_shapes=[
            pltpu.VMEM((TOK, PACK), BF),
            pltpu.VMEM((PACK, TOK), BF),
            pltpu.VMEM((TOK, D), F32),
            pltpu.VMEM((TOK, PACK), F32),
            pltpu.VMEM((PACK, HALF), F32),
            pltpu.VMEM((FF // 2, D), F32),
        ],
        compiler_params=params(),
        name="feed_forward",
    )(scal, chips, x_chip, part, part_other, dy, e2, g2, gathered, gathered, gathered)

    dh2_other = permute(dh2, CORE_PAIRS)
    out_other = permute(out_send, CORE_PAIRS)
    o_other = permute(o, CORE_PAIRS)
    o_ring = [o] + [permute(o, z_shift(k)) for k in (1, 2, 3)]
    ff_block = reduce_parts(((kg, sg), (ku, su), (kd, sd)), 1)

    dres, dresb, do = call(
        resid_backward_kernel,
        (shape((2, 128, D), F32), shape((TOK, D), BF), shape((TOK, HALF), BF)),
        (scal, resid, dh2, dh2_other, g2, dy, wo_keep, wo_other, e2),
        name="residual_backward",
    )
    do_ring = [do] + [permute(do, z_shift(k)) for k in (1, 2, 3)]
    dq = call(
        attn_query_kernel,
        shape((TOK, HALF), BF),
        (scal, probs, do, o, k_all, v_all, cosine, sine),
        name="attention_query_gradient",
    )
    dk, dv = call(
        attn_key_kernel,
        (shape((TOK, HALF), BF), shape((TOK, HALF), BF)),
        (scal, q_all, k_all, v_all, *do_ring, *o_ring, start_row, cosine, sine),
        scratch=(pltpu.VMEM((TOK, HALF), F32), pltpu.VMEM((TOK, HALF), F32)),
        name="attention_key_gradient",
    )
    grads_out = (shape((128, PACK), F32),) * 2 + (shape((32, 16, 512), BF),) * 6
    dh1, dh1_send, k0, k1, k2, s0, s1, s2 = pl.pallas_call(
        attn_grads_kernel,
        out_shape=grads_out,
        grid=(1,),
        in_specs=[
            scalars(),
            scalars(),
            full((TOK, HALF)),
            full((TOK, HALF)),
            full((TOK, HALF)),
            full((LEN, PACK)),
            full((TOK, PACK)),
            full((TOK, 512)),
            full((TOK, 512)),
            full((TOK, D)),
            full((8, D)),
            chunk(0),
            chunk(1),
            chunk(2),
            full((HALF, 512)),
        ],
        out_specs=tuple(full(s.shape) for s in grads_out),
        scratch_shapes=[
            pltpu.VMEM((3, PACK, HALF), F32),
            pltpu.VMEM((PACK, HALF), F32),
            pltpu.VMEM((2, 64, 128), F32),
            pltpu.VMEM((TOK, PACK), F32),
        ],
        compiler_params=params(),
        name="attention_weight_gradients",
    )(scal, chips, dq, dk, dv, xp, h1_own, o, o_other, dresb, gg2, gathered, gathered, gathered, e2)
    dh1_other = permute(dh1_send, CORE_PAIRS)
    attn_block = reduce_parts(((k0, s0), (k1, s1), (k2, s2)), 2)

    output, input_grad = call(
        token_outputs_kernel,
        (shape((128, D), BF), shape((128, D), F32)),
        (scal, xp, dh1, dh1_other, g1, dres, e2, resid, out_keep, out_other),
        name="token_outputs",
    )

    attn_rows = attn_block.reshape(2, 8, 3 * 512)
    ff_rows = ff_block[:8].reshape(8, 2, 8, HALF)
    attn_mine = lax.dynamic_index_in_dim(attn_rows, core, 0, False)
    attn_theirs = permute(lax.dynamic_index_in_dim(attn_rows, 1 - core, 0, False), CORE_PAIRS)
    ff_mine = lax.dynamic_index_in_dim(ff_rows, core, 1, False)
    ff_theirs = permute(lax.dynamic_index_in_dim(ff_rows, 1 - core, 1, False), CORE_PAIRS)
    pad = jnp.zeros((8, 8, HALF), F32)
    ff_mine = jnp.concatenate([jnp.concatenate([ff_mine, pad], axis=1), ff_block[8:]], axis=0)
    shapes = tuple(shape(m.shape, F32) for m in masters)
    outs = call(
        update_kernel,
        shapes * 3 + tuple(shape(m.shape, BF) for m in masters),
        (scal, attn_mine, attn_theirs, ff_mine, ff_theirs, *masters, *moments, *averages),
        name="update",
    )
    return (output[None], input_grad[None], *outs)


def solution(mesh):
    fine = Mesh(mesh.devices.reshape(4, 2, 4, 4), AXES)
    tokens = P(("y", "x"), ("z", "core"), None)
    rows = P(("z", "core", "y", "x"), None)
    return jax.shard_map(
        shards,
        mesh=fine,
        in_specs=(tokens, P(("y", "x"), ("z", "core")), tokens) + (rows,) * 24,
        out_specs=(tokens, tokens) + (rows,) * 32,
        check_vma=False,
    )
```

```python
import math

import jax
import jax.numpy as jnp
import numpy as np
from jax import lax
from jax.experimental import pallas as pl
from jax.experimental.pallas import tpu as pltpu
from jax.sharding import Mesh
from jax.sharding import PartitionSpec as P


BF = jnp.bfloat16
F32 = jnp.float32
HD = 64
D = 768
FF = 3072
HALF = 384
TOK = 256
LEN = 1024
HEADS = 6
EPS = 1e-05
MOMENTUM = 0.9
AVERAGE = 0.5
RATES = (0.01, 0.01, 0.01, 4.0, 0.02, 0.02, 0.015, 0.1)
MASKED = -1e30
AXES = ("z", "core", "y", "x")


def params(mib=60):
    return pltpu.CompilerParams(vmem_limit_bytes=mib * 1024 * 1024)


def cost(micros):
    return pl.CostEstimate(flops=1 + int(micros * 1e3), bytes_accessed=1, transcendentals=0)


def device_pairs(move):
    pairs = []
    for z in range(4):
        for c in range(2):
            for y in range(4):
                for x in range(4):
                    to = move(z, c, y, x)
                    pairs.append((((z * 2 + c) * 4 + y) * 4 + x, ((to[0] * 2 + to[1]) * 4 + to[2]) * 4 + to[3]))
    return pairs


CORE_PAIRS = device_pairs(lambda z, c, y, x: (z, 1 - c, y, x))


def z_shift(k):
    return device_pairs(lambda z, c, y, x: ((z + k) % 4, c, y, x))


def halving_pairs(axis, first):
    def move(z, c, y, x):
        flip = 3 if (c == 0) == first else 1
        at = [z, c, y, x]
        at[axis] ^= flip
        return tuple(at)

    return device_pairs(move)


AXIS = {"z": 0, "y": 2, "x": 3}
ORDERS = (("x", "y", "z"), ("y", "z", "x"), ("z", "x", "y"))


def permute(value, pairs):
    return lax.ppermute(value, AXES, pairs)


def cube_groups():
    groups = {}
    for z in range(4):
        for c in range(2):
            for y in range(4):
                for x in range(4):
                    key = (c,) + tuple((v >> 1) if c == 0 else (v >> 1) ^ (v & 1) for v in (z, y, x))
                    groups.setdefault(key, []).append(((z * 2 + c) * 4 + y) * 4 + x)
    return list(groups.values())


def exchange(blocks):
    return lax.all_to_all(blocks, AXES, 0, 0, tiled=True, axis_index_groups=cube_groups())


def chip_of_place(me, core):
    place = np.arange(64)
    rows = []
    for order in ORDERS:
        away = {axis: (place >> (5 - k)) & 1 for k, axis in enumerate(order)}
        inside = {axis: (place >> (2 - k)) & 1 for k, axis in enumerate("zyx")}
        at = {}
        for axis in "zyx":
            one, two = jnp.asarray(away[axis]), jnp.asarray(inside[axis])
            mine = me[axis]
            zero = ((one ^ (mine >> 1)) << 1) | two
            low = one ^ ((mine >> 1) ^ (mine & 1))
            at[axis] = jnp.where(core == 0, zero, (two << 1) | (two ^ low))
        rows.append(at["z"] * 16 + at["y"] * 4 + at["x"])
    return jnp.stack(rows).astype(jnp.int32)


def placed_matrix(chips):
    row = jnp.arange(12, dtype=jnp.int32)[None, :]
    chip = chips[:, None]
    wanted = (((chip // 16) * 2 + row // 6) * 16 + chip % 16) * 6 + row % 6
    return (lax.broadcasted_iota(jnp.int32, (D, D), 0) == wanted.reshape(1, D)).astype(BF)


def dot(left, right):
    return jnp.dot(left, right, preferred_element_type=F32)


def dot_nt(left, right):
    return lax.dot_general(left, right, (((1,), (1,)), ((), ())), preferred_element_type=F32)


def dot_tn(left, right):
    return lax.dot_general(left, right, (((0,), (0,)), ((), ())), preferred_element_type=F32)


def swap_halves(tile):
    lane = lax.broadcasted_iota(jnp.int32, tile.shape, 1)
    return jnp.where(lane % HD < HD // 2, pltpu.roll(tile, 96, 1), pltpu.roll(tile, 32, 1))


def lanes_of(tile, odd):
    lane = lax.broadcasted_iota(jnp.int32, tile.shape, 1)
    return jnp.where((lane >= HD) == bool(odd), tile, jnp.zeros_like(tile))


def join_lanes(even, odd):
    lane = lax.broadcasted_iota(jnp.int32, even.shape, 1)
    return jnp.where(lane < HD, even, odd)


def pack_kernel(scal, wq, wk, wv, wo, wg, wu, wd, gains, keep, send, down, lines):
    core = scal[1]
    chunks = []
    for w in (wq, wk, wg, wv, wu):
        for part in range(w.shape[1] // D):
            halves = [w[:, part * D + h * HALF : part * D + (h + 1) * HALF] for h in range(2)]
            chunks.append((jnp.where(core == 0, halves[0], halves[1]), jnp.where(core == 0, halves[1], halves[0])))
    chunks += [(wo[:, :HALF],) * 2, (wo[:, HALF:],) * 2]
    for k, (mine, other) in enumerate(chunks):
        keep[k, 0:6, :] = mine
        send[k, 0:6, :] = other
        keep[k, 6:8, :] = jnp.zeros((2, HALF), F32)
        send[k, 6:8, :] = jnp.zeros((2, HALF), F32)
    lines[...] = jnp.zeros_like(lines)
    lines[0:2, 0:6] = gains[...]
    moved = jnp.where(core == 0, lines[...], pltpu.roll(lines[...], 8, 1))
    keep[0, 6:8, 0:128] = moved[0:2, :]
    send[0, 6:8, 0:128] = moved[0:2, :]
    for j in range(3):
        rows = wd[8 * j : 8 * j + 8, :]
        down[j] = jnp.concatenate([rows[:, :HALF], rows[:, HALF:]], axis=0).astype(BF)


def merge_kernel(scal, keep, other, down, out):
    core = scal[1]
    for k in range(16):
        if k >= 13:
            block = down[k - 13]
        else:
            low = jnp.where(core == 0, keep[k], other[k])
            high = jnp.where(core == 0, other[k], keep[k])
            block = jnp.concatenate([low, high], axis=0).astype(BF)
        for copy in range(8):
            out[copy, k] = block


def dense_rows():
    to = lax.broadcasted_iota(jnp.int32, (96, 128), 0)
    at = lax.broadcasted_iota(jnp.int32, (96, 128), 1)
    row = to % 12
    return (at == (to // 12) * 16 + (row // 6) * 8 + row % 6).astype(BF)


def dense_kernel(blocks, m0, m1, m2):
    pick = dense_rows()

    def rows(k):
        return blocks[:, k].reshape(128, HALF)

    at = 0
    for k in range(6):
        m0[0, 96 * k : 96 * k + 96, :] = dot(pick, rows(k)).astype(BF)
    m1[0, 0:96, :] = dot(pick, rows(6)).astype(BF)
    to = lax.broadcasted_iota(jnp.int32, (16, 128), 0)
    at = lax.broadcasted_iota(jnp.int32, (16, 128), 1)
    gains = ((at // 16 == to % 8) & (at % 8 == 6 + to // 8)).astype(BF)
    m1[0, 96:112, :] = dot(gains, rows(0)).astype(BF)
    for k in range(4):
        m1[0, 112 + 96 * k : 208 + 96 * k, :] = dot(pick, rows(7 + k)).astype(BF)
    for k in range(2):
        m2[0, 96 * k : 96 * k + 96, :] = dot(pick, rows(11 + k)).astype(BF)
    m2[0, 192:, :] = blocks[:, 13:16].reshape(HALF, HALF)


def split_kernel(x0, y0, x1, y1, x2, y2, a0, f0, a1, f1, a2, f2):
    for x, y, a, f in ((x0, y0, a0, f0), (x1, y1, a1, f1), (x2, y2, a2, f2)):
        rows = a.shape[1]
        for k, source in ((0, x), (1, y)):
            a[k] = source[0, :rows, :]
            f[k] = source[0, rows:, :]


def stacked(low, high, start):
    return jnp.concatenate([half[:, start : start + 96, :].reshape(HALF, HALF) for half in (low, high)], axis=0)


def attn_forward_kernel(
    scal,
    ring,
    other,
    cosine,
    sine,
    start,
    p0,
    p1,
    p2,
    a0_low,
    a0_high,
    a1_low,
    a1_high,
    a2_low,
    a2_high,
    q,
    k_all,
    v_all,
    h_qk,
    h_v,
    x_chip,
    probs,
    o_out,
    part,
    g1_out,
    g2_out,
    bias,
):
    z, core = scal[0], scal[1]
    own = pl.ds(pl.multiple_of(z * TOK, TOK), TOK)
    held = jnp.concatenate([half[f, 96:112, 0:128].astype(F32) for half in (a1_low, a1_high) for f in range(4)], axis=0)
    held = held.reshape(8, 2, 8, 128)
    block = lax.broadcasted_iota(jnp.int32, (64, D), 0)
    place = lax.broadcasted_iota(jnp.int32, (64, D), 1)
    lane = lax.broadcasted_iota(jnp.int32, (128, D), 0)
    row = lax.broadcasted_iota(jnp.int32, (128, D), 1) % 12
    fold = (lane == (row // 6) * 8 + row % 6).astype(BF)
    for k, out in ((0, g1_out), (1, g2_out)):
        wide = dot(held[:, k].reshape(64, 128).astype(BF), fold)
        line = jnp.sum(jnp.where(place // 12 == block, wide, 0.0), axis=0, keepdims=True)
        out[...] = dot_nt(jnp.broadcast_to(line, (8, D)).astype(BF), p1[...])
    g1 = g1_out[0:1, :]

    wq, wk, wv = stacked(a0_low, a0_high, 0), stacked(a0_low, a0_high, 96), stacked(a1_low, a1_high, 0)

    def turn(raw, at, t):
        u = raw[:, 128 * t : 128 * t + 128]
        return (u * cosine[at, :] + swap_halves(u) * sine[at, :]).astype(BF)

    for b in range(4):
        at = slice(b * TOK, (b + 1) * TOK)
        mine, theirs = ring[b, 0:128, :], other[b, 0:128, :]
        x16 = jnp.concatenate([jnp.where(core == 0, mine, theirs), jnp.where(core == 0, theirs, mine)], axis=0)
        x = x16.astype(F32)
        scale = lax.rsqrt(jnp.mean(x * x, axis=1, keepdims=True) + EPS)
        h1 = (x * scale * g1).astype(BF)
        for_qk = dot(h1, p0[...]).astype(BF)
        for_v = dot(h1, p1[...]).astype(BF)
        h_qk[at, :] = for_qk
        h_v[at, :] = for_v
        raw = dot(for_qk, wk)
        for t in range(3):
            k_all[at, 128 * t : 128 * t + 128] = turn(raw, at, t)
        v_all[at, :] = dot(for_v, wv).astype(BF)

        @pl.when(z == b)
        def _(x16=x16):
            x_chip[...] = x16

    raw = dot(h_qk[own, :], wq)
    for t in range(3):
        q[:, 128 * t : 128 * t + 128] = turn(raw, own, t) * BF(0.125)

    key = lax.broadcasted_iota(jnp.int32, (LEN, TOK), 0).astype(F32)
    query = (lax.broadcasted_iota(jnp.int32, (LEN, TOK), 1) + z * TOK).astype(F32)
    bias[...] = jnp.where((key >= start[0:1, own]) & (key <= query), 0.0, MASKED)
    sub = lax.broadcasted_iota(jnp.int32, (128, TOK), 0)
    for t in range(3):
        cols = slice(128 * t, 128 * t + 128)
        q_tile, k_tile = q[:, cols], k_all[:, cols]
        v_t = v_all[:, cols].T
        mixed = []
        for odd in range(2):
            s = dot_nt(k_tile, lanes_of(q_tile, odd)) + bias[...]
            top = jnp.max(s, axis=0, keepdims=True)
            expo = jnp.exp(s - top)
            total = jnp.sum(expo, axis=0, keepdims=True)
            pb = (expo * (1.0 / total)).astype(BF)
            probs[2 * t + odd] = pb
            mixed.append(dot(v_t, pb))
        o_out[:, cols] = jnp.where(sub < HD, mixed[0], mixed[1]).T.astype(BF)
    placed = dot(o_out[...], p2[pl.ds(pl.multiple_of(core * HALF, HALF), HALF), :]).astype(BF)
    part[:, :HALF] = dot(placed, stacked(a2_low, a2_high, 0))
    part[:, HALF:] = dot(placed, stacked(a2_low, a2_high, 96))


def ffn_kernel(
    scal,
    chips,
    x,
    part_a,
    part_b,
    cot,
    cot_other,
    p0,
    p1,
    g2,
    wg_low,
    wg_high,
    wu_low,
    wu_high,
    wd_low,
    wd_high,
    out_keep,
    out_send,
    dh2_out,
    resid,
    keep_g,
    send_g,
    keep_u,
    send_u,
    keep_d,
    send_d,
    h2p,
    h2p_t,
    down,
    dy,
    acc_out,
    acc_dh2,
    grad_d,
):
    core = scal[1]
    j = pl.program_id(0)

    @pl.when(j == 0)
    def _():
        r = x[...].astype(F32) + (part_a[...] + part_b[...])
        resid[...] = r
        scale = lax.rsqrt(jnp.mean(r * r, axis=1, keepdims=True) + EPS)
        h2 = (r * scale * g2[0:1, :]).astype(BF)
        for k, p in ((0, p0), (1, p1)):
            placed = dot(h2, p[...]).astype(BF)
            h2p[k] = placed
            h2p_t[k] = placed.T
        dy[pl.ds(pl.multiple_of(core * 128, 128), 128), :] = cot[...]
        dy[pl.ds(pl.multiple_of((1 - core) * 128, 128), 128), :] = cot_other[...]
        acc_out[...] = jnp.zeros_like(acc_out)
        acc_dh2[...] = jnp.zeros_like(acc_dh2)

        def move(w, carry):
            down[chips[2, w]] = wd_low[w]
            down[chips[2, w + 32]] = wd_high[w]
            return carry

        lax.fori_loop(0, 32, move, 0, unroll=2)

    halves = ((slice(0, HALF), wg_low, wu_low), (slice(HALF, D), wg_high, wu_high))
    gate, up = 0.0, 0.0
    for at, wg, wu in halves:
        gate += dot(h2p[0, :, at], wg[...].reshape(HALF, HALF))
        up += dot(h2p[1, :, at], wu[...].reshape(HALF, HALF))
    blocks = down[pl.ds(j * 16, 16)].astype(F32)
    w_down = jnp.concatenate(
        [blocks[:, :, 0:8, :].reshape(HALF, HALF), blocks[:, :, 8:16, :].reshape(HALF, HALF)], axis=1
    ).astype(BF)
    sig = jax.nn.sigmoid(gate)
    hidden = (gate * sig * up).astype(BF)
    acc_out[...] += dot(hidden, w_down)
    dhid = dot_nt(dy[...], w_down)
    dgate = (dhid * up * sig * (1.0 + gate * (1.0 - sig))).astype(BF)
    dup = (dhid * gate * sig).astype(BF)
    for at, wg, wu in halves:
        acc_dh2[0, :, at] += dot_nt(dgate, wg[...].reshape(HALF, HALF))
        acc_dh2[1, :, at] += dot_nt(dup, wu[...].reshape(HALF, HALF))

    for part, value, keep, send in ((0, dgate, keep_g, send_g), (1, dup, keep_u, send_u)):
        grad = dot(h2p_t[part], value).astype(BF).reshape(8, 96, HALF)
        keep[...] = grad[:4]
        send[...] = grad[4:]
    grad_d[pl.ds(pl.multiple_of(j * HALF, HALF), HALF), :] = dot_tn(hidden, dy[...])

    @pl.when(j == 3)
    def _():
        mine = pl.multiple_of(core * 128, 128)
        other = pl.multiple_of((1 - core) * 128, 128)
        out_keep[...] = acc_out[pl.ds(mine, 128), :]
        out_send[...] = acc_out[pl.ds(other, 128), :]
        dh2 = dot_nt(acc_dh2[0].astype(BF), p0[...]) + dot_nt(acc_dh2[1].astype(BF), p1[...])
        dh2_out[...] = dh2.astype(BF)

        def write(w, carry):
            for at, out in ((w, keep_d), (w + 32, send_d)):
                base = chips[2, at] * 24
                for k in range(3):
                    rows = grad_d[pl.ds(pl.multiple_of(base + 8 * k, 8), 8), :]
                    out[w, k] = jnp.concatenate([rows[:, :HALF], rows[:, HALF:]], axis=0).astype(BF)
            return carry

        lax.fori_loop(0, 32, write, 0, unroll=2)


def resid_backward_kernel(
    scal, resid, dh2_a, dh2_b, g2, cot, cot_other, a2_low, a2_high, p2, dres_out, dresb_out, do_out
):
    core = scal[1]
    r = resid[...]
    dh2 = dh2_a[...].astype(F32) + dh2_b[...].astype(F32)
    scale = lax.rsqrt(jnp.mean(r * r, axis=1, keepdims=True) + EPS)
    weighted = dh2 * g2[0:1, :]
    inner = jnp.mean(weighted * r, axis=1, keepdims=True)
    mine, theirs = cot[...].astype(F32), cot_other[...].astype(F32)
    dy = jnp.concatenate([jnp.where(core == 0, mine, theirs), jnp.where(core == 0, theirs, mine)], axis=0)
    dres = dy + (scale * weighted - r * (scale * scale * scale) * inner)
    dresb = dres.astype(BF)
    dresb_out[...] = dresb
    do = dot_nt(dresb[:, :HALF], stacked(a2_low, a2_high, 0)) + dot_nt(dresb[:, HALF:], stacked(a2_low, a2_high, 96))
    do_out[...] = dot_nt(do.astype(BF), p2[pl.ds(pl.multiple_of(core * HALF, HALF), HALF), :]).astype(BF)
    dres_out[0] = dres[0:128, :]
    dres_out[1] = dres[128:256, :]


def attn_backward_kernel(scal, probs, do, o, q, k_all, v_all, cosine, sine, dq_out, dk_out, dv_out):
    own = pl.ds(pl.multiple_of(scal[0] * TOK, TOK), TOK)
    head_of = (
        lax.broadcasted_iota(jnp.int32, (8, HALF), 1) // HD == lax.broadcasted_iota(jnp.int32, (8, HALF), 0)
    ).astype(F32)
    inner = lax.dot_general(
        head_of,
        do[...].astype(F32) * o[...].astype(F32),
        (((1,), (1,)), ((), ())),
        precision=lax.Precision.HIGHEST,
        preferred_element_type=F32,
    )
    sub = lax.broadcasted_iota(jnp.int32, (128, TOK), 0)
    for t in range(3):
        cols = slice(128 * t, 128 * t + 128)
        q_tile, do_tile = q[:, cols], do[:, cols]
        k_tile, v_tile = k_all[:, cols], v_all[:, cols]
        k_t = k_tile.T
        dqs, dks, dvs = [], [], []
        for odd in range(2):
            h = 2 * t + odd
            pb = probs[h]
            dp = dot_nt(v_tile, lanes_of(do_tile, odd))
            ds = (pb.astype(F32) * (dp - inner[h : h + 1, :])).astype(BF)
            dks.append(dot(ds, q_tile))
            dvs.append(dot(pb, do_tile))
            dqs.append(dot(k_t, ds))
        u = jnp.where(sub < HD, dqs[0], dqs[1]).T * 0.125
        dq_out[:, cols] = (u * cosine[own, :] - swap_halves(u) * sine[own, :]).astype(BF)
        u = join_lanes(dks[0], dks[1])
        dk_out[:, cols] = (u * cosine[...] - swap_halves(u) * sine[...]).astype(BF)
        dv_out[:, cols] = join_lanes(dvs[0], dvs[1]).astype(BF)


def attn_grads_kernel(scal, dq, dk, dv, h_qk, h_v, o_mine, o_other, dresb, p2, k0, k1, k2, s0, s1, s2):
    core = scal[1]
    own = pl.ds(pl.multiple_of(scal[0] * TOK, TOK), TOK)

    def write(keep, send, at, grad):
        grad = grad.astype(BF).reshape(8, 96, HALF)
        keep[:, at : at + 96, :] = grad[:4]
        send[:, at : at + 96, :] = grad[4:]

    o_a, o_b = o_mine[...], o_other[...]
    o_full = jnp.concatenate([jnp.where(core == 0, o_a, o_b), jnp.where(core == 0, o_b, o_a)], axis=1)
    d_mine = jnp.where(core == 0, dresb[:, :HALF], dresb[:, HALF:])
    write(k2, s2, 0, dot_tn(dot(o_full, p2[...]).astype(BF), d_mine))
    write(k0, s0, 0, dot_tn(h_qk[own, :], dq[...]))
    write(k0, s0, 96, dot(h_qk[...].T, dk[...]))
    write(k1, s1, 0, dot(h_v[...].T, dv[...]))


def dh1_kernel(scal, dq, dk, dv, a0_low, a0_high, a1_low, a1_high, p0, p1, keep, send):
    z, core = scal[0], scal[1]
    wq, wk, wv = stacked(a0_low, a0_high, 0), stacked(a0_low, a0_high, 96), stacked(a1_low, a1_high, 0)
    for k in range(4):
        at = pl.ds(pl.multiple_of(lax.rem(z + k, 4) * TOK, TOK), TOK)
        first = dot_nt(dk[at, :], wk)
        if k == 0:
            first = first + dot_nt(dq[...], wq)
        second = dot_nt(dv[at, :], wv)
        total = (dot_nt(first.astype(BF), p0[...]) + dot_nt(second.astype(BF), p1[...])).astype(BF)
        keep[k] = jnp.where(core == 0, total[:128], total[128:])
        send[k] = jnp.where(core == 0, total[128:], total[:128])


def token_outputs_kernel(scal, x_ref, d0, d1, d2, d3, g1, dres, resid, out_a, out_b, output, input_grad):
    core = scal[1]
    x = x_ref[...].astype(F32)
    dh1 = (d0[...].astype(F32) + d1[...].astype(F32)) + (d2[...].astype(F32) + d3[...].astype(F32))
    scale = lax.rsqrt(jnp.mean(x * x, axis=1, keepdims=True) + EPS)
    weighted = dh1 * g1[0:1, :]
    inner = jnp.mean(weighted * x, axis=1, keepdims=True)
    input_grad[...] = dres[core] + (scale * weighted - x * (scale * scale * scale) * inner)
    mine = pl.ds(pl.multiple_of(core * 128, 128), 128)
    output[...] = (resid[mine, :] + (out_a[...] + out_b[...])).astype(BF)


def padded_kernel(x0, y0, x1, y1, x2, y2, out):
    pick = dense_rows()
    for x, y, units, at in ((x0, y0, 6, 0), (x1, y1, 5, 6), (x2, y2, 0, 11)):
        total = (x[0].astype(F32) + y[0].astype(F32)).astype(BF)
        for k in range(units):
            out[:, at + k] = dot_tn(pick, total[96 * k : 96 * k + 96]).astype(BF).reshape(8, 16, HALF)
        if units == 0:
            out[:, 11:14] = total[:HALF].reshape(8, 3, 16, HALF)
            out[:, 14] = dot_tn(pick, total[HALF:]).astype(BF).reshape(8, 16, HALF)


def sum_kernel(scal, blocks, total, other):
    core = scal[1]
    for k in range(15):
        value = blocks[0, k].astype(F32)
        for b in range(1, 8):
            value += blocks[b, k].astype(F32)
        total[k] = value
        other[k] = jnp.where(core == 0, value[8:16], value[0:8])


def update_kernel(scal, mine, theirs, *refs):
    core = scal[1]
    masters, moments, averages = refs[0:8], refs[8:16], refs[16:24]
    news, moms, means, copies = refs[24:32], refs[32:40], refs[40:48], refs[48:56]
    base = 1.0 / math.sqrt(16384)

    def step(k, at, grad):
        rate = RATES[k] * base
        moment = MOMENTUM * moments[k][at] + grad
        new = masters[k][at] - rate * (grad + MOMENTUM * moment)
        news[k][at] = new
        moms[k][at] = moment
        means[k][at] = AVERAGE * averages[k][at] + (1.0 - AVERAGE) * new
        copies[k][at] = new.astype(BF)

    def halves(a, b):
        return (jnp.where(core == 0, a, b), jnp.where(core == 0, b, a))

    gain_sums = [jnp.zeros((6, 128), F32), jnp.zeros((6, 128), F32)]

    def weigh(which, k, at, grad):
        product = masters[k][at].astype(BF).astype(F32) * grad
        for c in range(0, product.shape[1], 128):
            gain_sums[which] += product[:, c : c + 128]

    own = pl.ds(pl.multiple_of(core * 8, 8), 8)

    def chunk(k):
        a, b = mine[k, own, :][0:6, :], theirs[k][0:6, :]
        return (jnp.where(core == 0, a, b), jnp.where(core == 0, b, a))

    for k, weight, offset, gain in (
        (4, 0, 0, 0),
        (5, 1, 0, 0),
        (10, 2, 0, 0),
        (14, 3, 0, None),
        (0, 4, 0, 1),
        (1, 4, D, 1),
        (2, 4, 2 * D, 1),
        (3, 4, 3 * D, 1),
        (6, 5, 0, 1),
        (7, 5, D, 1),
        (8, 5, 2 * D, 1),
        (9, 5, 3 * D, 1),
    ):
        for h, grad in enumerate(chunk(k)):
            at = (slice(0, 6), slice(offset + h * HALF, offset + (h + 1) * HALF))
            step(weight, at, grad)
            if gain is not None:
                weigh(gain, weight, at, grad)
    for j in range(3):
        for h in range(2):
            grad = mine[11 + j, 8 * h : 8 * h + 8, :]
            step(6, (slice(8 * j, 8 * j + 8), slice(h * HALF, (h + 1) * HALF)), grad)
    row = lax.broadcasted_iota(jnp.int32, (6, 128), 0)
    lane = lax.broadcasted_iota(jnp.int32, (6, 128), 1)
    for k in range(2):
        column = jnp.sum(gain_sums[k], axis=1, keepdims=True)
        line = jnp.sum(jnp.where(lane == row, column, 0.0), axis=0, keepdims=True)[:, 0:6]
        at = (slice(k, k + 1), slice(0, 6))
        step(7, at, line / masters[7][at].astype(BF).astype(F32))


def whole():
    return pl.BlockSpec(memory_space=pltpu.VMEM)


def scalars():
    return pl.BlockSpec(memory_space=pltpu.SMEM)


def call(kernel, out_shape, operands, scratch=(), smem=1, name=None, micros=1.0, mib=60):
    specs = [scalars() if k < smem else whole() for k in range(len(operands))]
    return pl.pallas_call(
        kernel,
        out_shape=out_shape,
        in_specs=specs,
        out_specs=jax.tree.map(lambda _: whole(), out_shape),
        scratch_shapes=list(scratch),
        compiler_params=params(mib),
        cost_estimate=cost(micros),
        name=name,
    )(*operands)


def shape(dims, kind):
    return jax.ShapeDtypeStruct(dims, kind)


def add(a, b):
    return (a.astype(F32) + b.astype(F32)).astype(BF)


def halve(keep, send, axis):
    return add(keep, permute(send, halving_pairs(AXIS[axis], True)))


def reduce_blocks(ffn, attn):
    ffn = [halve(keep, send, order[0]) for order, (keep, send) in zip(ORDERS, ffn)]
    ffn, attn = lax.optimization_barrier((ffn, attn))
    attn = [halve(keep, send, order[0]) for order, (keep, send) in zip(ORDERS, attn)]
    terms = []
    for order, a, b in zip(ORDERS, ffn, attn):
        keep = jnp.concatenate([a[:2], b[:2]], axis=1)
        send = jnp.concatenate([a[2:], b[2:]], axis=1)
        both = halve(keep, send, order[1])
        terms += [both[:1], permute(both[1:], halving_pairs(AXIS[order[2]], True))]
    return terms


def fetch(block, axis):
    return permute(block, halving_pairs(AXIS[axis], True))


def gather_parts(blocks):
    merged = call(
        dense_kernel,
        (shape((1, 576, HALF), BF), shape((1, 496, HALF), BF), shape((1, 576, HALF), BF)),
        (blocks,),
        smem=0,
        name="dense_rows",
    )
    merged = [half for m, order in zip(merged, ORDERS) for half in (m, fetch(m, order[2]))]
    sizes = (192, 112, 192)
    split = call(
        split_kernel,
        tuple(shape((2, rows, HALF), BF) for a in sizes for rows in (a, HALF)),
        merged,
        smem=0,
        name="split_rows",
    )
    found = []
    for kind in range(2):
        parts = []
        for value, order in zip(split[kind::2], ORDERS):
            value = jnp.concatenate([value, fetch(value, order[1])], axis=0)
            parts += [value, fetch(value, order[0])]
        found.append(parts)
    return found


def shards(inputs, doc_ids, cotangent, *state):
    state = tuple(v.T if k % 8 == 7 else v for k, v in enumerate(state))
    masters, moments, averages = state[0:8], state[8:16], state[16:24]
    z, core = lax.axis_index("z"), lax.axis_index("core")
    y, x_at = lax.axis_index("y"), lax.axis_index("x")
    scal = jnp.stack([z, core]).astype(jnp.int32)
    chips = chip_of_place({"z": z, "y": y, "x": x_at}, core)

    keep, send, down = call(
        pack_kernel,
        (shape((13, 8, HALF), F32), shape((13, 8, HALF), F32), shape((3, 16, HALF), BF)),
        (scal, *masters),
        scratch=(pltpu.VMEM((8, 128), F32),),
        name="pack_weights",
    )
    blocks = call(
        merge_kernel,
        shape((8, 16, 16, HALF), BF),
        (scal, keep, permute(send, CORE_PAIRS), down),
        name="merge_weights",
    )
    blocks, inputs, cotangent = lax.optimization_barrier((blocks, inputs, cotangent))
    blocks = exchange(blocks)
    places = [placed_matrix(chips[k]) for k in range(3)]
    ids_row = jnp.zeros((16, D), BF).at[0, :128].set(doc_ids[0].astype(BF))
    block = jnp.concatenate([inputs[0], ids_row], axis=0)
    ring = jnp.broadcast_to(block[None], (4, 144, D))
    blocks, ring, places = lax.optimization_barrier((blocks, ring, places))
    attn_w, ffn_w = gather_parts(blocks)

    ring = lax.all_to_all(ring, "z", 0, 0, tiled=True)
    other = permute(jnp.concatenate([ring.reshape(576, D), cotangent[0]], axis=0), CORE_PAIRS)
    cot_other = other[576:]
    other = other[:576].reshape(4, 144, D)
    ids = jnp.stack([ring[:, 128, :128], other[:, 128, :128]], axis=1)
    ids = jnp.where(core == 0, ids, ids[:, ::-1]).reshape(LEN).astype(F32)
    starts = jnp.sum((ids[None, :] < ids[:, None]).astype(jnp.int32), axis=1)
    freq = 10000.0 ** (-jnp.arange(0, HD, 2, dtype=F32) / HD)
    spot = (jnp.arange(LEN, dtype=jnp.int32) - starts).astype(F32)
    theta = spot[:, None] * jnp.tile(freq, 4)[None, :]
    sign = jnp.tile(jnp.repeat(jnp.array([-1.0, 1.0], F32), HD // 2), 2)
    cosine, sine = jnp.cos(theta), jnp.sin(theta) * sign[None, :]
    start_row = jnp.broadcast_to(starts.astype(F32)[None, :], (8, LEN))

    q, k_all, v_all, h_qk, h_v, x_chip, probs, o, part, g1, g2 = call(
        attn_forward_kernel,
        (
            shape((TOK, HALF), BF),
            shape((LEN, HALF), BF),
            shape((LEN, HALF), BF),
            shape((LEN, D), BF),
            shape((LEN, D), BF),
            shape((TOK, D), BF),
            shape((HEADS, LEN, TOK), BF),
            shape((TOK, HALF), BF),
            shape((TOK, D), F32),
            shape((8, D), F32),
            shape((8, D), F32),
        ),
        (scal, ring, other, cosine, sine, start_row, *places, *attn_w),
        scratch=(pltpu.VMEM((LEN, TOK), F32),),
        name="attention_forward",
        mib=40,
    )
    part_other = permute(part, CORE_PAIRS)

    def full(dims):
        return pl.BlockSpec(dims, lambda i, n=len(dims): (0,) * n)

    ffn_out = (
        shape((128, D), F32),
        shape((128, D), F32),
        shape((TOK, D), BF),
        shape((TOK, D), F32),
    ) + tuple(shape((4, HALF, HALF), BF) for _ in range(4)) + tuple(shape((32, 3, 16, HALF), BF) for _ in range(2))
    column = pl.BlockSpec((4, 96, HALF), lambda j: (0, j, 0))
    out_keep, out_send, dh2, resid, kg, sg, ku, su, kd, sd = pl.pallas_call(
        ffn_kernel,
        out_shape=ffn_out,
        grid=(4,),
        in_specs=[
            scalars(),
            scalars(),
            full((TOK, D)),
            full((TOK, D)),
            full((TOK, D)),
            full((128, D)),
            full((128, D)),
            full((D, D)),
            full((D, D)),
            full((8, D)),
            column,
            column,
            column,
            column,
            full((32, 3, 16, HALF)),
            full((32, 3, 16, HALF)),
        ],
        out_specs=tuple(full(s.shape) for s in ffn_out[:4])
        + (column,) * 4
        + tuple(full(s.shape) for s in ffn_out[8:]),
        scratch_shapes=[
            pltpu.VMEM((2, TOK, D), BF),
            pltpu.VMEM((2, D, TOK), BF),
            pltpu.VMEM((64, 3, 16, HALF), BF),
            pltpu.VMEM((TOK, D), BF),
            pltpu.VMEM((TOK, D), F32),
            pltpu.VMEM((2, TOK, D), F32),
            pltpu.VMEM((FF // 2, D), F32),
        ],
        compiler_params=params(36),
        cost_estimate=cost(4),
        name="feed_forward",
    )(
        scal,
        chips,
        x_chip,
        part,
        part_other,
        cotangent[0],
        cot_other,
        places[0],
        places[1],
        g2,
        *ffn_w[:4],
        *(half.reshape(32, 3, 16, HALF) for half in ffn_w[4:]),
    )

    dh2_other = permute(dh2, CORE_PAIRS)
    out_other = permute(out_send, CORE_PAIRS)
    o_other = permute(o, CORE_PAIRS)

    dres, dresb, do = call(
        resid_backward_kernel,
        (shape((2, 128, D), F32), shape((TOK, D), BF), shape((TOK, HALF), BF)),
        (scal, resid, dh2, dh2_other, g2, cotangent[0], cot_other, *attn_w[4:], places[2]),
        name="residual_backward",
        mib=16,
    )
    dq, dk, dv = call(
        attn_backward_kernel,
        (shape((TOK, HALF), BF), shape((LEN, HALF), BF), shape((LEN, HALF), BF)),
        (scal, probs, do, o, q, k_all, v_all, cosine, sine),
        name="attention_backward",
        mib=24,
    )
    terms = tuple(shape((4, rows, HALF), BF) for rows in (192, 96, 96))
    k0, k1, k2, s0, s1, s2 = call(
        attn_grads_kernel,
        terms * 2,
        (scal, dq, dk, dv, h_qk, h_v, o, o_other, dresb, places[2]),
        name="attention_weight_gradients",
        mib=32,
    )
    dh1, dh1_send = call(
        dh1_kernel,
        (shape((4, 128, D), BF), shape((4, 128, D), BF)),
        (scal, dq, dk, dv, *attn_w[:4], places[0], places[1]),
        name="attention_input_gradient",
    )
    dh1 = (dh1.astype(F32) + permute(dh1_send, CORE_PAIRS).astype(F32)).astype(BF)
    dh1 = [dh1[0]] + [permute(dh1[k], z_shift(k)) for k in (1, 2, 3)]
    kd, sd = kd.reshape(4, HALF, HALF), sd.reshape(4, HALF, HALF)
    terms = reduce_blocks(((kg, sg), (ku, su), (kd, sd)), ((k0, s0), (k1, s1), (k2, s2)))
    blocks = call(padded_kernel, shape((8, 15, 16, HALF), BF), terms, smem=0, name="padded_rows")
    blocks, out_other, *dh1 = lax.optimization_barrier((blocks, out_other, *dh1))
    blocks = exchange(blocks)
    output, input_grad = call(
        token_outputs_kernel,
        (shape((128, D), BF), shape((128, D), F32)),
        (scal, inputs[0], *dh1, g1, dres, resid, out_keep, out_other),
        name="token_outputs",
    )

    grads, theirs = call(
        sum_kernel, (shape((15, 16, HALF), F32), shape((15, 8, HALF), F32)), (scal, blocks), name="sum_blocks"
    )
    theirs = permute(theirs, CORE_PAIRS)
    shapes = tuple(shape(m.shape, F32) for m in masters)
    outs = call(
        update_kernel,
        shapes * 3 + tuple(shape(m.shape, BF) for m in masters),
        (scal, grads, theirs, *masters, *moments, *averages),
        name="update",
    )
    outs = tuple(v.T if k % 8 == 7 else v for k, v in enumerate(outs))
    return (output[None], input_grad[None], *outs)


def solution(mesh):
    fine = Mesh(mesh.devices.reshape(4, 2, 4, 4), AXES)
    tokens = P(("y", "x"), ("z", "core"), None)
    rows = P(("z", "core", "y", "x"), None)
    return jax.shard_map(
        shards,
        mesh=fine,
        in_specs=(tokens, P(("y", "x"), ("z", "core")), tokens) + (rows,) * 24,
        out_specs=(tokens, tokens) + (rows,) * 32,
        check_vma=False,
    )
```

```python
import functools
import math

import jax
import jax.numpy as jnp
import numpy as np
from jax import lax
from jax.experimental import pallas as pl
from jax.experimental.pallas import tpu as pltpu
from jax.sharding import Mesh
from jax.sharding import PartitionSpec as P


BF = jnp.bfloat16
F32 = jnp.float32
HD = 64
D = 768
FF = 3072
HALF = 384
TOK = 256
LEN = 1024
HEADS = 6
EPS = 1e-05
MOMENTUM = 0.9
AVERAGE = 0.5
RATES = (0.01, 0.01, 0.01, 4.0, 0.02, 0.02, 0.015, 0.1)
MASKED = -1e30
AXES = ("z", "core", "y", "x")


def params(mib=60):
    return pltpu.CompilerParams(vmem_limit_bytes=mib * 1024 * 1024)


def cost(micros):
    return pl.CostEstimate(flops=1 + int(micros * 1e3), bytes_accessed=1, transcendentals=0)


def device_pairs(move):
    pairs = []
    for z in range(4):
        for c in range(2):
            for y in range(4):
                for x in range(4):
                    to = move(z, c, y, x)
                    pairs.append((((z * 2 + c) * 4 + y) * 4 + x, ((to[0] * 2 + to[1]) * 4 + to[2]) * 4 + to[3]))
    return pairs


CORE_PAIRS = device_pairs(lambda z, c, y, x: (z, 1 - c, y, x))


AXIS = {"z": 0, "y": 2, "x": 3}
FLIPS = (0, 1, 3, 2)
ORDERS = (("x", "y", "z"), ("y", "z", "x"), ("z", "x", "y"))


def flip_pairs(axis, flip):
    def move(z, c, y, x):
        at = [z, c, y, x]
        at[AXIS[axis]] = (((at[AXIS[axis]] + c) % 4 ^ flip) - c) % 4
        return tuple(at)

    return device_pairs(move)


def permute(value, pairs):
    return lax.ppermute(value, AXES, pairs)


def cube_groups(flip):
    groups = {}
    for z in range(4):
        for c in range(2):
            for y in range(4):
                for x in range(4):
                    u = [(v + c) % 4 for v in (z, y, x)]
                    key = (c,) + tuple(min(v, v ^ flip) for v in u)
                    place = sum((v & 1 if flip == 1 else v >> 1) << (2 - k) for k, v in enumerate(u))
                    groups.setdefault(key, [None] * 8)[place] = ((z * 2 + c) * 4 + y) * 4 + x
    return list(groups.values())


def exchange(blocks, flip):
    return lax.all_to_all(blocks, AXES, 0, 0, tiled=True, axis_index_groups=cube_groups(flip))


def chip_of_place(me, core):
    place = np.arange(64)
    rows = []
    for order in ORDERS + (None,):
        at = {}
        for k, axis in enumerate("zyx"):
            low = jnp.asarray((place >> (2 - k)) & 1)
            high = jnp.asarray((place >> (5 - (order.index(axis) if order else k))) & 1)
            if order:
                high = high ^ (((me[axis] + core) % 4) >> 1)
            at[axis] = (high * 2 + low - core) % 4
        rows.append(at["z"] * 16 + at["y"] * 4 + at["x"])
    return jnp.stack(rows).astype(jnp.int32)


def spread_matrix():
    place = jnp.arange(512, dtype=jnp.int32)
    chip, core, row = place // 16, (place // 8) % 2, place % 8
    wanted = jnp.where(row < 6, ((chip // 16 * 2 + core) * 16 + chip % 16) * 6 + row, -1)
    return (lax.broadcasted_iota(jnp.int32, (HALF, 512), 0) == wanted[None, :]).astype(BF)


def placed_features(chips):
    row = jnp.arange(12, dtype=jnp.int32)[None, None, :]
    chip = chips[:, :, None]
    wanted = (((chip // 16) * 2 + row // 6) * 16 + chip % 16) * 6 + row % 6
    return jnp.pad(wanted.reshape(4, D), ((0, 4), (0, 0)))


def placed_matrix(wanted):
    return (lax.broadcasted_iota(jnp.int32, (D, D), 0) == wanted).astype(BF)


def dot(left, right):
    return jnp.dot(left, right, preferred_element_type=F32)


def dot_nt(left, right):
    return lax.dot_general(left, right, (((1,), (1,)), ((), ())), preferred_element_type=F32)


def dot_tn(left, right):
    return lax.dot_general(left, right, (((0,), (0,)), ((), ())), preferred_element_type=F32)


def swap_halves(tile):
    lane = lax.broadcasted_iota(jnp.int32, tile.shape, 1)
    return jnp.where(lane % HD < HD // 2, pltpu.roll(tile, 96, 1), pltpu.roll(tile, 32, 1))


def lanes_of(tile, odd):
    lane = lax.broadcasted_iota(jnp.int32, tile.shape, 1)
    return jnp.where((lane >= HD) == bool(odd), tile, jnp.zeros_like(tile))


def join_lanes(even, odd):
    lane = lax.broadcasted_iota(jnp.int32, even.shape, 1)
    return jnp.where(lane < HD, even, odd)


def put_halves(core, w, keep, send, at):
    for part in range(w.shape[1] // D):
        halves = [w[:, part * D + h * HALF : part * D + (h + 1) * HALF] for h in range(2)]
        keep[at + part, 0:6, :] = jnp.where(core == 0, halves[0], halves[1])
        send[at + part, 0:6, :] = jnp.where(core == 0, halves[1], halves[0])
        keep[at + part, 6:8, :] = jnp.zeros((2, HALF), F32)
        send[at + part, 6:8, :] = jnp.zeros((2, HALF), F32)


def pack_ffn_kernel(scal, wg, wu, keep, send):
    put_halves(scal[1], wg, keep, send, 0)
    put_halves(scal[1], wu, keep, send, 4)


def pack_attn_kernel(scal, wq, wk, wv, wo, gains, keep, send, lines):
    core = scal[1]
    for k, w in enumerate((wq, wk, wv)):
        put_halves(core, w, keep, send, k)
    for h in range(2):
        for out in (keep, send):
            out[3 + h, 0:6, :] = wo[:, h * HALF : (h + 1) * HALF]
            out[3 + h, 6:8, :] = jnp.zeros((2, HALF), F32)
    lines[...] = jnp.zeros_like(lines)
    lines[0:2, 0:6] = gains[...]
    moved = jnp.where(core == 0, lines[...], pltpu.roll(lines[...], 8, 1))
    keep[0, 6:8, 0:128] = moved[0:2, :]
    send[0, 6:8, 0:128] = moved[0:2, :]


def both_cores(core, keep, other):
    low = jnp.where(core == 0, keep, other)
    high = jnp.where(core == 0, other, keep)
    return jnp.concatenate([low, high], axis=0).astype(BF)


def merge_ffn_kernel(scal, keep, other, wd, ffn):
    for k in range(8):
        ffn[k] = both_cores(scal[1], keep[k], other[k])
    for j in range(3):
        rows = wd[8 * j : 8 * j + 8, :]
        ffn[8 + j] = jnp.concatenate([rows[:, :HALF], rows[:, HALF:]], axis=0).astype(BF)


def merge_attn_kernel(scal, keep, other, attn):
    for k in range(5):
        value = both_cores(scal[1], keep[k], other[k])
        for copy in range(8):
            attn[copy, k] = value


def dense_rows():
    to = lax.broadcasted_iota(jnp.int32, (96, 128), 0)
    at = lax.broadcasted_iota(jnp.int32, (96, 128), 1)
    row = to % 12
    return (at == (to // 12) * 16 + (row // 6) * 8 + row % 6).astype(BF)


def dense_kernel(blocks, attn):
    pick = dense_rows()
    to = lax.broadcasted_iota(jnp.int32, (32, 128), 0)
    at = lax.broadcasted_iota(jnp.int32, (32, 128), 1)
    gains = ((at // 16 == to % 8) & (at % 8 == 6 + to // 8) & (to < 16)).astype(BF)
    rows = [blocks[:, k].reshape(128, HALF) for k in range(5)]
    found = [dot(pick, value).astype(BF) for value in rows] + [dot(gains, rows[0]).astype(BF)]
    for copy in range(8):
        for k, value in enumerate(found):
            attn[copy, 96 * k : 96 * k + value.shape[0], :] = value


def weight_at(attn, k):
    return attn[:, 96 * k : 96 * k + 96, :].reshape(D, HALF)


def attn_forward_kernel(
    scal,
    seq,
    seq_other,
    cosine,
    sine,
    start,
    wanted,
    attn,
    q,
    k_all,
    v_all,
    h_all,
    h_t,
    x_chip,
    probs,
    po,
    g1_out,
    g2_out,
    x_all,
    bias,
    pa,
):
    z, core = scal[0], scal[1]
    own = pl.ds(pl.multiple_of(z * TOK, TOK), TOK)
    pa[...] = placed_matrix(wanted[3:4, :])
    held = attn[:, 480:496, 0:128].astype(F32).reshape(8, 2, 8, 128)
    block = lax.broadcasted_iota(jnp.int32, (64, D), 0)
    place = lax.broadcasted_iota(jnp.int32, (64, D), 1)
    lane = lax.broadcasted_iota(jnp.int32, (128, D), 0)
    row = lax.broadcasted_iota(jnp.int32, (128, D), 1) % 12
    fold = (lane == (row // 6) * 8 + row % 6).astype(BF)
    for k, out in ((0, g1_out), (1, g2_out)):
        wide = dot(held[:, k].reshape(64, 128).astype(BF), fold)
        line = jnp.sum(jnp.where(place // 12 == block, wide, 0.0), axis=0, keepdims=True)
        out[...] = dot_nt(jnp.broadcast_to(line, (8, D)).astype(BF), pa[...])
    g1 = g1_out[0:1, :]
    wq, wk, wv = (weight_at(attn, k) for k in range(3))

    def turn(raw, at, t):
        u = raw[:, 128 * t : 128 * t + 128]
        return (u * cosine[at, :] + swap_halves(u) * sine[at, :]).astype(BF)

    for c, blocks in ((core, seq), (1 - core, seq_other)):
        for k, flip in enumerate(FLIPS):
            at = (((z + c) % 4 ^ flip) + 4 - c) % 4 * TOK + c * 128
            x_all[pl.ds(pl.multiple_of(at, 128), 128), :] = blocks[k, 0:128, :]
    x_chip[...] = x_all[own, :]
    for b in range(4):
        at = slice(b * TOK, (b + 1) * TOK)
        x16 = x_all[at, :]
        x = x16.astype(F32)
        scale = lax.rsqrt(jnp.mean(x * x, axis=1, keepdims=True) + EPS)
        h1 = dot((x * scale * g1).astype(BF), pa[...]).astype(BF)
        h_all[at, :] = h1
        raw = dot(h1, wk)
        for t in range(3):
            k_all[at, 128 * t : 128 * t + 128] = turn(raw, at, t)
        v_all[at, :] = dot(h1, wv).astype(BF)

    raw = dot(h_all[own, :], wq)
    for t in range(3):
        q[:, 128 * t : 128 * t + 128] = turn(raw, own, t) * BF(0.125)

    key = lax.broadcasted_iota(jnp.int32, (LEN, TOK), 0).astype(F32)
    query = (lax.broadcasted_iota(jnp.int32, (LEN, TOK), 1) + z * TOK).astype(F32)
    bias[...] = jnp.where((key >= start[0:1, own]) & (key <= query), 0.0, MASKED)
    sub = lax.broadcasted_iota(jnp.int32, (128, TOK), 0)
    for t in range(3):
        cols = slice(128 * t, 128 * t + 128)
        q_tile, k_tile = q[:, cols], k_all[:, cols]
        v_t = v_all[:, cols].T
        mixed = []
        for odd in range(2):
            s = dot_nt(k_tile, lanes_of(q_tile, odd)) + bias[...]
            top = jnp.max(s, axis=0, keepdims=True)
            expo = jnp.exp(s - top)
            total = jnp.sum(expo, axis=0, keepdims=True)
            pb = (expo * (1.0 / total)).astype(BF)
            probs[2 * t + odd] = pb
            mixed.append(dot(v_t, pb))
        po[:, D + 128 * t : D + 128 * t + 128] = jnp.where(sub < HD, mixed[0], mixed[1]).T.astype(BF)
    h_t[...] = h_all[...].T
    half = pl.ds(pl.multiple_of(core * HALF, HALF), HALF)
    placed = dot(po[:, D:], pa[half, :]).astype(BF)
    po[:, :HALF] = dot(placed, weight_at(attn, 3)).astype(BF)
    po[:, HALF:D] = dot(placed, weight_at(attn, 4)).astype(BF)


def ffn_kernel(
    scal,
    chips,
    x,
    part_a,
    part_b,
    cot,
    cot_other,
    wanted,
    e2,
    g2,
    wg,
    wu,
    wd0,
    wd1,
    wd2,
    out_keep,
    dh2_out,
    resid,
    keep_g,
    send_g,
    keep_u,
    send_u,
    keep_d,
    send_d,
    h2p,
    h2p_t,
    dy,
    acc_out,
    acc_dh2,
    grad_d,
):
    core = scal[1]
    j = pl.program_id(0)

    @pl.when(j == 0)
    def _():
        r = x[...].astype(F32) + (part_a[...].astype(F32) + part_b[...].astype(F32))
        resid[...] = r
        scale = lax.rsqrt(jnp.mean(r * r, axis=1, keepdims=True) + EPS)
        h2 = (r * scale * g2[0:1, :]).astype(BF)
        h2p[:, :512] = dot(h2[:, :HALF], e2[...]).astype(BF)
        h2p[:, 512:] = dot(h2[:, HALF:], e2[...]).astype(BF)
        for k in range(2):
            h2p_t[k] = dot(h2, placed_matrix(wanted[k : k + 1, :])).astype(BF).T
        dy[pl.ds(pl.multiple_of(core * 128, 128), 128), :] = cot[...]
        dy[pl.ds(pl.multiple_of((1 - core) * 128, 128), 128), :] = cot_other[...]
        acc_out[...] = jnp.zeros_like(acc_out)
        acc_dh2[...] = jnp.zeros_like(acc_dh2)

    w_gate, w_up = wg[...].reshape(1024, HALF), wu[...].reshape(1024, HALF)
    gate, up = dot(h2p[...], w_gate), dot(h2p[...], w_up)
    blocks = jnp.concatenate([wd0[...], wd1[...], wd2[...]], axis=1).astype(F32)
    w_down = jnp.concatenate(
        [blocks[:, :, 0:8, :].reshape(HALF, HALF), blocks[:, :, 8:16, :].reshape(HALF, HALF)], axis=1
    ).astype(BF)
    sig = jax.nn.sigmoid(gate)
    hidden = (gate * sig * up).astype(BF)
    acc_out[...] += dot(hidden, w_down)
    dhid = dot_nt(dy[...], w_down)
    dgate = (dhid * up * sig * (1.0 + gate * (1.0 - sig))).astype(BF)
    dup = (dhid * gate * sig).astype(BF)
    acc_dh2[...] += dot_nt(dgate, w_gate) + dot_nt(dup, w_up)

    for part, value, keep, send in ((0, dgate, keep_g, send_g), (1, dup, keep_u, send_u)):
        grad = dot(h2p_t[part], value).astype(BF).reshape(8, 96, HALF)
        keep[...] = grad[:4]
        send[...] = grad[4:]
    grad_d[pl.ds(pl.multiple_of(j * HALF, HALF), HALF), :] = dot_tn(hidden, dy[...])

    @pl.when(j == 3)
    def _():
        mine = pl.multiple_of(core * 128, 128)
        other = pl.multiple_of((1 - core) * 128, 128)
        out_keep[...] = acc_out[pl.ds(mine, 128), :]
        dh2 = acc_dh2[...].astype(BF)
        dh2_out[:TOK, :HALF] = dot_nt(dh2[:, :512], e2[...]).astype(BF)
        dh2_out[:TOK, HALF:] = dot_nt(dh2[:, 512:], e2[...]).astype(BF)
        dh2_out[TOK:, :] = acc_out[pl.ds(other, 128), :].astype(BF)

        def write(w, carry):
            for at, out in ((w, keep_d), (w + 32, send_d)):
                base = chips[2, at] * 24
                for k in range(3):
                    rows = grad_d[pl.ds(pl.multiple_of(base + 8 * k, 8), 8), :]
                    out[w, k] = jnp.concatenate([rows[:, :HALF], rows[:, HALF:]], axis=0).astype(BF)
            return carry

        lax.fori_loop(0, 32, write, 0, unroll=2)


def attn_backward_kernel(
    scal,
    resid,
    dh2_a,
    dh2_b,
    g2,
    cot,
    cot_other,
    wo_a,
    wo_b,
    wanted,
    probs,
    o_mine,
    o_other,
    q,
    k_all,
    v_all,
    h_t,
    cosine,
    sine,
    dres_out,
    dq_out,
    dk_out,
    dv_out,
    grads,
    do,
    inner,
    grad_o,
    pa,
):
    core = scal[1]
    own = pl.ds(pl.multiple_of(scal[0] * TOK, TOK), TOK)
    step = pl.program_id(0)

    @pl.when(step == 0)
    def _():
        pa[...] = placed_matrix(wanted[3:4, :])
        r = resid[...]
        dh2 = dh2_a[...].astype(F32) + dh2_b[...].astype(F32)
        scale = lax.rsqrt(jnp.mean(r * r, axis=1, keepdims=True) + EPS)
        weighted = dh2 * g2[0:1, :]
        mean = jnp.mean(weighted * r, axis=1, keepdims=True)
        mine, theirs = cot[...].astype(F32), cot_other[...].astype(F32)
        dy = jnp.concatenate([jnp.where(core == 0, mine, theirs), jnp.where(core == 0, theirs, mine)], axis=0)
        dres = dy + (scale * weighted - r * (scale * scale * scale) * mean)
        dresb = dres.astype(BF)
        placed = dot_nt(dresb[:, :HALF], wo_a[...].reshape(D, HALF)) + dot_nt(dresb[:, HALF:], wo_b[...].reshape(D, HALF))
        half = pl.ds(pl.multiple_of(core * HALF, HALF), HALF)
        found = dot_nt(placed.astype(BF), pa[half, :]).astype(BF)
        head_of = (
            lax.broadcasted_iota(jnp.int32, (8, HALF), 1) // HD == lax.broadcasted_iota(jnp.int32, (8, HALF), 0)
        ).astype(F32)
        o_a, o_b = o_mine[...], o_other[...]
        inner[...] = lax.dot_general(
            head_of,
            found.astype(F32) * o_a.astype(F32),
            (((1,), (1,)), ((), ())),
            precision=lax.Precision.HIGHEST,
            preferred_element_type=F32,
        )
        o_full = jnp.concatenate([jnp.where(core == 0, o_a, o_b), jnp.where(core == 0, o_b, o_a)], axis=1)
        d_mine = jnp.where(core == 0, dresb[:, :HALF], dresb[:, HALF:])
        found_o = dot_tn(dot(o_full, pa[...]).astype(BF), d_mine).astype(BF)
        for t in range(3):
            do[t] = found[:, 128 * t : 128 * t + 128]
            grad_o[t] = found_o[:, 128 * t : 128 * t + 128].reshape(8, 96, 128)
        dres_out[0] = dres[0:128, :]
        dres_out[1] = dres[128:256, :]

    @pl.when(step > 0)
    def _():
        t = step - 1
        sub = lax.broadcasted_iota(jnp.int32, (128, TOK), 0)
        q_tile, do_tile, v_tile = q[...], do[t], v_all[...]
        k_t = k_all[...].T
        dqs, dks, dvs = [], [], []
        for odd in range(2):
            pb = probs[odd]
            dp = dot_nt(v_tile, lanes_of(do_tile, odd))
            ds = (pb.astype(F32) * (dp - inner[pl.ds(2 * t + odd, 1), :])).astype(BF)
            dks.append(dot(ds, q_tile))
            dvs.append(dot(pb, do_tile))
            dqs.append(dot(k_t, ds))
        u = jnp.where(sub < HD, dqs[0], dqs[1]).T * 0.125
        dq = (u * cosine[own, :] - swap_halves(u) * sine[own, :]).astype(BF)
        u = join_lanes(dks[0], dks[1])
        dk = (u * cosine[...] - swap_halves(u) * sine[...]).astype(BF)
        dv = join_lanes(dvs[0], dvs[1]).astype(BF)
        dq_out[...] = dq
        dk_out[...] = dk
        dv_out[...] = dv
        both = dot(h_t[...], jnp.concatenate([dk, dv], axis=1)).astype(BF)
        grads[:, 0:96, :] = dot(h_t[:, own], dq).astype(BF).reshape(8, 96, 128)
        grads[:, 96:192, :] = both[:, :128].reshape(8, 96, 128)
        grads[:, 192:288, :] = both[:, 128:].reshape(8, 96, 128)
        grads[:, 288:384, :] = grad_o[t]


def dh1_kernel(scal, dq, dk, dv, attn, wanted, out, pa):
    @pl.when(pl.program_id(0) == 0)
    def _():
        pa[...] = placed_matrix(wanted[3:4, :])

    wq, wk, wv = (weight_at(attn, k) for k in range(3))
    mine = jnp.where(scal[0] == pl.program_id(0), dq[...], jnp.zeros_like(dq))
    total = dot_nt(dk[...], wk) + dot_nt(dv[...], wv) + dot_nt(mine, wq)
    out[...] = dot_nt(total.astype(BF), pa[...]).astype(BF)


def terms_kernel(*refs):
    for k in range(3):
        total = (refs[2 * k][...].astype(F32) + refs[2 * k + 1][...].astype(F32)).astype(BF)
        half = total.shape[0] // 2
        refs[6 + 2 * k][...] = total[:half]
        refs[7 + 2 * k][...] = total[half:]


def padded_kernel(x0, y0, x1, y1, x2, y2, attn, out):
    pick = dense_rows()

    def write(at, rows):
        out[:, at] = dot_tn(pick, rows).astype(BF).reshape(8, 16, HALF)

    for at, x, y in ((0, x0, y0), (4, x1, y1)):
        total = (x[0].astype(F32) + y[0].astype(F32)).astype(BF)
        for k in range(4):
            write(at + k, total[96 * k : 96 * k + 96])
    out[:, 12:15] = (x2[0].astype(F32) + y2[0].astype(F32)).astype(BF).reshape(8, 3, 16, HALF)
    for k in range(4):
        rows = slice(96 * k, 96 * k + 96)
        total = attn[0, rows, :].astype(F32)
        for b in range(1, 8):
            total += attn[b, rows, :].astype(F32)
        write(8 + k, total.astype(BF))


def sum_kernel(scal, blocks, total, other):
    core = scal[1]
    for k in range(15):
        value = blocks[0, k].astype(F32)
        for b in range(1, 8):
            value += blocks[b, k].astype(F32)
        total[k] = value
        other[k] = jnp.where(core == 0, value[8:16], value[0:8])


def update_kernel(scal, mine, theirs, x_ref, dh1_ref, g1, dres, resid, out_a, out_b, *refs):
    core = scal[1]
    output, input_grad = refs[56:58]
    x = x_ref[...].astype(F32)
    dh1 = dh1_ref[...].astype(F32)
    scale = lax.rsqrt(jnp.mean(x * x, axis=1, keepdims=True) + EPS)
    weighted = dh1 * g1[0:1, :]
    inner = jnp.mean(weighted * x, axis=1, keepdims=True)
    input_grad[...] = dres[core] + (scale * weighted - x * (scale * scale * scale) * inner)
    tokens = pl.ds(pl.multiple_of(core * 128, 128), 128)
    output[...] = (resid[tokens, :] + (out_a[...] + out_b[TOK:, :].astype(F32))).astype(BF)
    masters, moments, averages = refs[0:8], refs[8:16], refs[16:24]
    news, moms, means, copies = refs[24:32], refs[32:40], refs[40:48], refs[48:56]
    base = 1.0 / math.sqrt(16384)

    def step(k, at, grad):
        rate = RATES[k] * base
        moment = MOMENTUM * moments[k][at] + grad
        new = masters[k][at] - rate * (grad + MOMENTUM * moment)
        news[k][at] = new
        moms[k][at] = moment
        means[k][at] = AVERAGE * averages[k][at] + (1.0 - AVERAGE) * new
        copies[k][at] = new.astype(BF)

    def halves(a, b):
        return (jnp.where(core == 0, a, b), jnp.where(core == 0, b, a))

    gain_sums = [jnp.zeros((6, 128), F32), jnp.zeros((6, 128), F32)]

    def weigh(which, k, at, grad):
        product = masters[k][at].astype(BF).astype(F32) * grad
        for c in range(0, product.shape[1], 128):
            gain_sums[which] += product[:, c : c + 128]

    own = pl.ds(pl.multiple_of(core * 8, 8), 8)

    def chunk(k):
        a, b = mine[k, own, :][0:6, :], theirs[k][0:6, :]
        return (jnp.where(core == 0, a, b), jnp.where(core == 0, b, a))

    for k, weight, offset, gain in (
        (8, 0, 0, 0),
        (9, 1, 0, 0),
        (10, 2, 0, 0),
        (11, 3, 0, None),
        (0, 4, 0, 1),
        (1, 4, D, 1),
        (2, 4, 2 * D, 1),
        (3, 4, 3 * D, 1),
        (4, 5, 0, 1),
        (5, 5, D, 1),
        (6, 5, 2 * D, 1),
        (7, 5, 3 * D, 1),
    ):
        for h, grad in enumerate(chunk(k)):
            at = (slice(0, 6), slice(offset + h * HALF, offset + (h + 1) * HALF))
            step(weight, at, grad)
            if gain is not None:
                weigh(gain, weight, at, grad)
    for j in range(3):
        for h in range(2):
            grad = mine[12 + j, 8 * h : 8 * h + 8, :]
            step(6, (slice(8 * j, 8 * j + 8), slice(h * HALF, (h + 1) * HALF)), grad)
    row = lax.broadcasted_iota(jnp.int32, (6, 128), 0)
    lane = lax.broadcasted_iota(jnp.int32, (6, 128), 1)
    for k in range(2):
        column = jnp.sum(gain_sums[k], axis=1, keepdims=True)
        line = jnp.sum(jnp.where(lane == row, column, 0.0), axis=0, keepdims=True)[:, 0:6]
        at = (slice(k, k + 1), slice(0, 6))
        step(7, at, line / masters[7][at].astype(BF).astype(F32))


def whole():
    return pl.BlockSpec(memory_space=pltpu.VMEM)


def scalars():
    return pl.BlockSpec(memory_space=pltpu.SMEM)


def call(kernel, out_shape, operands, scratch=(), smem=1, name=None, micros=1.0, mib=60):
    specs = [scalars() if k < smem else whole() for k in range(len(operands))]
    return pl.pallas_call(
        kernel,
        out_shape=out_shape,
        in_specs=specs,
        out_specs=jax.tree.map(lambda _: whole(), out_shape),
        scratch_shapes=list(scratch),
        compiler_params=params(mib),
        cost_estimate=cost(micros),
        name=name,
    )(*operands)


def shape(dims, kind):
    return jax.ShapeDtypeStruct(dims, kind)


def add(a, b):
    return (a.astype(F32) + b.astype(F32)).astype(BF)


def fetch(block, axis):
    return permute(block, flip_pairs(axis, 3))


def first_terms(parts):
    return [fetch(send, order[0]) for order, (_, send) in reversed(list(zip(ORDERS, parts)))][::-1]


def next_terms(keeps, got):
    count, rows = keeps[0].shape[0], 96
    pair = [pl.BlockSpec((count // 2, rows, HALF), lambda j: (0, j, 0))] * 6
    out = pl.pallas_call(
        terms_kernel,
        out_shape=(shape((count // 2, HALF, HALF), BF),) * 6,
        grid=(HALF // rows,),
        in_specs=[pl.BlockSpec((count, rows, HALF), lambda j: (0, j, 0))] * 6,
        out_specs=tuple(pair),
        compiler_params=params(),
        cost_estimate=cost(1),
        name="next_terms",
    )(*(v for pair in zip(keeps, got) for v in pair))
    return out[::2], out[1::2]


def reduce_rows(parts, got, after):
    keeps, sents = next_terms([keep for keep, _ in parts], got)
    got = [fetch(sent, order[1]) for sent, order in zip(sents, ORDERS)]
    got, after = lax.optimization_barrier((got, after))
    keeps, sents = next_terms(keeps, got)
    got = [fetch(sent, order[2]) for sent, order in zip(sents, ORDERS)]
    return [term for pair in zip(keeps, got) for term in pair], after


def flipped(block, flip):
    return permute(block, flip_pairs("z", flip))


def shards(inputs, doc_ids, cotangent, *state):
    state = tuple(v.T if k % 8 == 7 else v for k, v in enumerate(state))
    masters, moments, averages = state[0:8], state[8:16], state[16:24]
    z, core = lax.axis_index("z"), lax.axis_index("core")
    y, x_at = lax.axis_index("y"), lax.axis_index("x")
    scal = jnp.stack([z, core]).astype(jnp.int32)
    chips = chip_of_place({"z": z, "y": y, "x": x_at}, core)

    halves = shape((8, 8, HALF), F32)
    wq, wk, wv, wo, wg, wu, wd, gains = masters
    keep, send = call(pack_ffn_kernel, (halves, halves), (scal, wg, wu), name="pack_feed_forward")
    ffn_w = call(
        merge_ffn_kernel,
        shape((11, 16, HALF), BF),
        (scal, keep, permute(send, CORE_PAIRS), wd),
        name="merge_feed_forward",
    )
    ffn_w, wq, wk, wv, wo, gains, inputs, doc_ids, cotangent = lax.optimization_barrier(
        (ffn_w, wq, wk, wv, wo, gains, inputs, doc_ids, cotangent)
    )
    ffn_w = lax.all_gather(ffn_w, ("z", "y", "x"), axis=0, tiled=False)
    halves = shape((5, 8, HALF), F32)
    keep, send = call(
        pack_attn_kernel,
        (halves, halves),
        (scal, wq, wk, wv, wo, gains),
        scratch=(pltpu.VMEM((8, 128), F32),),
        name="pack_attention",
    )
    theirs, cot_other = permute(send, CORE_PAIRS), permute(cotangent[0], CORE_PAIRS)
    theirs, cot_other = lax.optimization_barrier((theirs, cot_other))
    attn = call(merge_attn_kernel, shape((8, 5, 16, HALF), BF), (scal, keep, theirs), name="merge_attention")

    ids_row = jnp.zeros((16, D), BF).at[0, :128].set(doc_ids[0].astype(BF))
    block = jnp.concatenate([inputs[0], ids_row], axis=0)
    attn, block = lax.optimization_barrier((attn, block))
    attn = exchange(attn, 1)
    seq = [block, flipped(block, 1), flipped(block, 3)]
    e2 = spread_matrix()
    wanted = placed_features(chips)
    attn, wanted, chips, e2 = lax.optimization_barrier((attn, wanted, chips, e2))
    attn = call(dense_kernel, shape((8, 512, HALF), BF), (attn,), smem=0, name="dense_rows", mib=16)
    attn = exchange(attn, 3)
    seq.append(flipped(seq[1], 3))
    seq = jnp.stack(seq)
    seq_other = permute(seq, CORE_PAIRS)
    ids = jnp.concatenate([seq[:, 128, :128], seq_other[:, 128, :128]], axis=0).astype(F32)
    spots = [(((z + c) % 4 ^ flip) + 4 - c) % 4 * 2 + c for c in (core, 1 - core) for flip in FLIPS]
    here = jnp.stack(spots)[None, :] == jnp.arange(8)[:, None]
    ids = jnp.sum(jnp.where(here[:, :, None], ids[None], 0.0), axis=1).reshape(LEN)
    starts = jnp.sum((ids[None, :] < ids[:, None]).astype(jnp.int32), axis=1)
    freq = 10000.0 ** (-jnp.arange(0, HD, 2, dtype=F32) / HD)
    spot = (jnp.arange(LEN, dtype=jnp.int32) - starts).astype(F32)
    theta = spot[:, None] * jnp.tile(freq, 4)[None, :]
    sign = jnp.tile(jnp.repeat(jnp.array([-1.0, 1.0], F32), HD // 2), 2)
    cosine, sine = jnp.cos(theta), jnp.sin(theta) * sign[None, :]
    start_row = jnp.broadcast_to(starts.astype(F32)[None, :], (8, LEN))

    q, k_all, v_all, h_all, h_t, x_chip, probs, po, g1, g2 = call(
        attn_forward_kernel,
        (
            shape((TOK, HALF), BF),
            shape((LEN, HALF), BF),
            shape((LEN, HALF), BF),
            shape((LEN, D), BF),
            shape((D, LEN), BF),
            shape((TOK, D), BF),
            shape((HEADS, LEN, TOK), BF),
            shape((TOK, D + HALF), BF),
            shape((8, D), F32),
            shape((8, D), F32),
        ),
        (scal, seq, seq_other, cosine, sine, start_row, wanted, attn),
        scratch=(pltpu.VMEM((LEN, D), BF), pltpu.VMEM((LEN, TOK), F32), pltpu.VMEM((D, D), BF)),
        name="attention_forward",
        micros=1.3e7,
    )
    po_other = permute(po, CORE_PAIRS)

    def full(dims):
        return pl.BlockSpec(dims, lambda i, n=len(dims): (0,) * n)

    ffn_out = (
        shape((128, D), F32),
        shape((TOK + 128, D), BF),
        shape((TOK, D), F32),
    ) + tuple(shape((4, HALF, HALF), BF) for _ in range(4)) + tuple(shape((32, 3, 16, HALF), BF) for _ in range(2))
    column = pl.BlockSpec((4, 96, HALF), lambda j: (0, j, 0))
    out_keep, dh2, resid, kg, sg, ku, su, kd, sd = pl.pallas_call(
        ffn_kernel,
        out_shape=ffn_out,
        grid=(4,),
        in_specs=[
            scalars(),
            scalars(),
            full((TOK, D)),
            full((TOK, D)),
            full((TOK, D)),
            full((128, D)),
            full((128, D)),
            full((8, D)),
            full((HALF, 512)),
            full((8, D)),
            pl.BlockSpec((64, 1, 16, HALF), lambda j: (0, j, 0, 0)),
            pl.BlockSpec((64, 1, 16, HALF), lambda j: (0, 4 + j, 0, 0)),
            *(pl.BlockSpec((16, 1, 16, HALF), lambda j, k=k: (j, 8 + k, 0, 0)) for k in range(3)),
        ],
        out_specs=tuple(full(s.shape) for s in ffn_out[:3])
        + (column,) * 4
        + tuple(full(s.shape) for s in ffn_out[7:]),
        scratch_shapes=[
            pltpu.VMEM((TOK, 1024), BF),
            pltpu.VMEM((2, D, TOK), BF),
            pltpu.VMEM((TOK, D), BF),
            pltpu.VMEM((TOK, D), F32),
            pltpu.VMEM((TOK, 1024), F32),
            pltpu.VMEM((FF // 2, D), F32),
        ],
        compiler_params=params(),
        cost_estimate=cost(4),
        name="feed_forward",
    )(
        scal,
        chips,
        x_chip,
        po,
        po_other,
        cotangent[0],
        cot_other,
        wanted,
        e2,
        g2,
        *((ffn_w,) * 5),
    )

    dh2_other = permute(dh2, CORE_PAIRS)
    dh2_other, kg, sg, ku, su, kd, sd = lax.optimization_barrier((dh2_other, kg, sg, ku, su, kd, sd))
    at_tile = lambda i: jnp.maximum(i - 1, 0)
    short = pl.BlockSpec((TOK, 128), lambda i: (0, at_tile(i)))
    long = pl.BlockSpec((LEN, 128), lambda i: (0, at_tile(i)))
    dres, dq, dk, dv, grads = pl.pallas_call(
        attn_backward_kernel,
        out_shape=(
            shape((2, 128, D), F32),
            shape((TOK, HALF), BF),
            shape((LEN, HALF), BF),
            shape((LEN, HALF), BF),
            shape((8, HALF, HALF), BF),
        ),
        grid=(4,),
        in_specs=[
            scalars(),
            full((TOK, D)),
            full((TOK, D)),
            full((TOK, D)),
            full((8, D)),
            full((128, D)),
            full((128, D)),
            pl.BlockSpec((8, 96, HALF), lambda i: (0, 3, 0)),
            pl.BlockSpec((8, 96, HALF), lambda i: (0, 4, 0)),
            full((8, D)),
            pl.BlockSpec((2, LEN, TOK), lambda i: (at_tile(i), 0, 0)),
            pl.BlockSpec((TOK, HALF), lambda i: (0, 2)),
            pl.BlockSpec((TOK, HALF), lambda i: (0, 2)),
            short,
            long,
            long,
            full((D, LEN)),
            full((LEN, 128)),
            full((LEN, 128)),
        ],
        out_specs=(
            full((2, 128, D)),
            short,
            long,
            long,
            pl.BlockSpec((8, HALF, 128), lambda i: (0, 0, at_tile(i))),
        ),
        scratch_shapes=[
            pltpu.VMEM((3, TOK, 128), BF),
            pltpu.VMEM((8, TOK), F32),
            pltpu.VMEM((3, 8, 96, 128), BF),
            pltpu.VMEM((D, D), BF),
        ],
        compiler_params=params(),
        cost_estimate=cost(1),
        name="attention_backward",
    )(
        scal,
        resid,
        dh2,
        dh2_other,
        g2,
        cotangent[0],
        cot_other,
        attn,
        attn,
        wanted,
        probs,
        po,
        po_other,
        q,
        k_all,
        v_all,
        h_t,
        cosine,
        sine,
    )
    parts = [(kg, sg), (ku, su), (kd.reshape(4, HALF, HALF), sd.reshape(4, HALF, HALF))]
    got = first_terms(parts)
    grads, dq, dk, dv, got = lax.optimization_barrier((grads, dq, dk, dv, got))
    grads = exchange(grads, 3)
    dh1 = pl.pallas_call(
        dh1_kernel,
        out_shape=shape((LEN, D), BF),
        grid=(4,),
        in_specs=[
            scalars(),
            full((TOK, HALF)),
            pl.BlockSpec((TOK, HALF), lambda b: (b, 0)),
            pl.BlockSpec((TOK, HALF), lambda b: (b, 0)),
            pl.BlockSpec((8, 288, HALF), lambda b: (0, 0, 0)),
            full((8, D)),
        ],
        out_specs=pl.BlockSpec((TOK, D), lambda b: (b, 0)),
        scratch_shapes=[pltpu.VMEM((D, D), BF)],
        compiler_params=params(),
        cost_estimate=cost(1),
        name="attention_input_gradient",
    )(scal, dq, dk, dv, attn, wanted)
    terms, dh1 = reduce_rows(parts, got, dh1)
    dh1 = lax.psum_scatter(dh1, ("z", "core"), scatter_dimension=0, tiled=True)
    blocks = call(padded_kernel, shape((8, 15, 16, HALF), BF), (*terms, grads), smem=0, name="padded_rows")
    blocks = exchange(blocks, 1)

    grads, theirs = call(
        sum_kernel, (shape((15, 16, HALF), F32), shape((15, 8, HALF), F32)), (scal, blocks), name="sum_blocks", mib=16
    )
    theirs = permute(theirs, CORE_PAIRS)
    shapes = tuple(shape(m.shape, F32) for m in masters)
    outs = call(
        update_kernel,
        shapes * 3 + tuple(shape(m.shape, BF) for m in masters) + (shape((128, D), BF), shape((128, D), F32)),
        (scal, grads, theirs, inputs[0], dh1, g1, dres, resid, out_keep, dh2_other, *masters, *moments, *averages),
        name="update",
    )
    outs, output, input_grad = outs[:32], *outs[32:]
    outs = tuple(v.T if k % 8 == 7 else v for k, v in enumerate(outs))
    return (output[None], input_grad[None], *outs)


def solution(mesh):
    fine = Mesh(mesh.devices.reshape(4, 2, 4, 4), AXES)
    tokens = P(("y", "x"), ("z", "core"), None)
    rows = P(("z", "core", "y", "x"), None)
    return jax.shard_map(
        shards,
        mesh=fine,
        in_specs=(tokens, P(("y", "x"), ("z", "core")), tokens) + (rows,) * 24,
        out_specs=(tokens, tokens) + (rows,) * 32,
        check_vma=False,
    )
```

```python
import functools
import math

import jax
import jax.numpy as jnp
import numpy as np
from jax import lax
from jax.experimental import pallas as pl
from jax.experimental.pallas import tpu as pltpu
from jax.sharding import Mesh
from jax.sharding import PartitionSpec as P


BF = jnp.bfloat16
F32 = jnp.float32
HD = 64
D = 768
FF = 3072
HALF = 384
TOK = 256
LEN = 1024
HEADS = 6
EPS = 1e-05
MOMENTUM = 0.9
AVERAGE = 0.5
RATES = (0.01, 0.01, 0.01, 4.0, 0.02, 0.02, 0.015, 0.1)
MASKED = -1e30
AXES = ("z", "core", "y", "x")


def params(mib=60):
    return pltpu.CompilerParams(vmem_limit_bytes=mib * 1024 * 1024)


def cost(micros):
    return pl.CostEstimate(flops=1 + int(micros * 1e3), bytes_accessed=1, transcendentals=0)


def device_pairs(move):
    pairs = []
    for z in range(4):
        for c in range(2):
            for y in range(4):
                for x in range(4):
                    to = move(z, c, y, x)
                    pairs.append((((z * 2 + c) * 4 + y) * 4 + x, ((to[0] * 2 + to[1]) * 4 + to[2]) * 4 + to[3]))
    return pairs


CORE_PAIRS = device_pairs(lambda z, c, y, x: (z, 1 - c, y, x))


AXIS = {"z": 0, "y": 2, "x": 3}
FLIPS = (0, 1, 3, 2)
ORDERS = (("x", "y", "z"), ("y", "z", "x"), ("z", "x", "y"))


def flip_pairs(axis, flip):
    def move(z, c, y, x):
        at = [z, c, y, x]
        at[AXIS[axis]] = (((at[AXIS[axis]] + c) % 4 ^ flip) - c) % 4
        return tuple(at)

    return device_pairs(move)


def permute(value, pairs):
    return lax.ppermute(value, AXES, pairs)


def cube_groups(flip):
    groups = {}
    for z in range(4):
        for c in range(2):
            for y in range(4):
                for x in range(4):
                    u = [(v + c) % 4 for v in (z, y, x)]
                    key = (c,) + tuple(min(v, v ^ flip) for v in u)
                    place = sum((v & 1 if flip == 1 else v >> 1) << (2 - k) for k, v in enumerate(u))
                    groups.setdefault(key, [None] * 8)[place] = ((z * 2 + c) * 4 + y) * 4 + x
    return list(groups.values())


def exchange(blocks, flip):
    return lax.all_to_all(blocks, AXES, 0, 0, tiled=True, axis_index_groups=cube_groups(flip))


def chip_of_place(me, core):
    place = np.arange(64)
    rows = []
    for order in ORDERS + (None,):
        at = {}
        for k, axis in enumerate("zyx"):
            low = jnp.asarray((place >> (2 - k)) & 1)
            high = jnp.asarray((place >> (5 - (order.index(axis) if order else k))) & 1)
            if order:
                high = high ^ (((me[axis] + core) % 4) >> 1)
            at[axis] = (high * 2 + low - core) % 4
        rows.append(at["z"] * 16 + at["y"] * 4 + at["x"])
    return jnp.stack(rows).astype(jnp.int32)


def placed_features(chips):
    chips = jnp.concatenate([chips, jnp.arange(64, dtype=jnp.int32)[None, :]], axis=0)
    row = jnp.arange(12, dtype=jnp.int32)[None, None, :]
    chip = chips[:, :, None]
    wanted = (((chip // 16) * 2 + row // 6) * 16 + chip % 16) * 6 + row % 6
    return jnp.pad(wanted.reshape(5, D), ((0, 3), (0, 0)))


def placed_matrix(wanted):
    return (lax.broadcasted_iota(jnp.int32, (D, D), 0) == wanted).astype(BF)


def dot(left, right):
    return jnp.dot(left, right, preferred_element_type=F32)


def dot_nt(left, right):
    return lax.dot_general(left, right, (((1,), (1,)), ((), ())), preferred_element_type=F32)


def dot_tn(left, right):
    return lax.dot_general(left, right, (((0,), (0,)), ((), ())), preferred_element_type=F32)


def swap_halves(tile):
    lane = lax.broadcasted_iota(jnp.int32, tile.shape, 1)
    return jnp.where(lane % HD < HD // 2, pltpu.roll(tile, 96, 1), pltpu.roll(tile, 32, 1))


def lanes_of(tile, odd):
    lane = lax.broadcasted_iota(jnp.int32, tile.shape, 1)
    return jnp.where((lane >= HD) == bool(odd), tile, jnp.zeros_like(tile))


def join_lanes(even, odd):
    lane = lax.broadcasted_iota(jnp.int32, even.shape, 1)
    return jnp.where(lane < HD, even, odd)


def put_halves(core, w, keep, send, at):
    for part in range(w.shape[1] // D):
        halves = [w[:, part * D + h * HALF : part * D + (h + 1) * HALF] for h in range(2)]
        keep[at + part, 0:6, :] = jnp.where(core == 0, halves[0], halves[1])
        send[at + part, 0:6, :] = jnp.where(core == 0, halves[1], halves[0])
        keep[at + part, 6:8, :] = jnp.zeros((2, HALF), F32)
        send[at + part, 6:8, :] = jnp.zeros((2, HALF), F32)


def pack_ffn_kernel(scal, wg, wu, keep, send):
    put_halves(scal[1], wg, keep, send, 0)
    put_halves(scal[1], wu, keep, send, 4)


def pack_attn_kernel(scal, wq, wk, wv, wo, gains, keep, send, lines):
    core = scal[1]
    for k, w in enumerate((wq, wk, wv)):
        put_halves(core, w, keep, send, k)
    for h in range(2):
        for out in (keep, send):
            out[3 + h, 0:6, :] = wo[:, h * HALF : (h + 1) * HALF]
            out[3 + h, 6:8, :] = jnp.zeros((2, HALF), F32)
    lines[...] = jnp.zeros_like(lines)
    lines[0:2, 0:6] = gains[...]
    moved = jnp.where(core == 0, lines[...], pltpu.roll(lines[...], 8, 1))
    keep[0, 6:8, 0:128] = moved[0:2, :]
    send[0, 6:8, 0:128] = moved[0:2, :]


def both_cores(core, keep, other):
    low = jnp.where(core == 0, keep, other)
    high = jnp.where(core == 0, other, keep)
    return jnp.concatenate([low, high], axis=0).astype(BF)


def merge_ffn_kernel(scal, keep, other, wd, ffn):
    to = lax.broadcasted_iota(jnp.int32, (48, 64), 0)
    at = lax.broadcasted_iota(jnp.int32, (48, 64), 1)
    row = to % 12
    pick = (at == (to // 12) * 16 + (row // 6) * 8 + row % 6).astype(BF)
    for w in range(2):
        blocks = [both_cores(scal[1], keep[4 * w + k], other[4 * w + k]) for k in range(4)]
        ffn[48 * w : 48 * w + 48, :] = dot(pick, jnp.concatenate(blocks, axis=0)).astype(BF)
    for j in range(3):
        rows = wd[8 * j : 8 * j + 8, :]
        ffn[96 + 16 * j : 112 + 16 * j, :] = jnp.concatenate([rows[:, :HALF], rows[:, HALF:]], axis=0).astype(BF)


def merge_attn_kernel(scal, keep, other, attn):
    for k in range(5):
        value = both_cores(scal[1], keep[k], other[k])
        for copy in range(8):
            attn[copy, k] = value


def dense_rows():
    to = lax.broadcasted_iota(jnp.int32, (96, 128), 0)
    at = lax.broadcasted_iota(jnp.int32, (96, 128), 1)
    row = to % 12
    return (at == (to // 12) * 16 + (row // 6) * 8 + row % 6).astype(BF)


def dense_kernel(blocks, attn):
    pick = dense_rows()
    to = lax.broadcasted_iota(jnp.int32, (32, 128), 0)
    at = lax.broadcasted_iota(jnp.int32, (32, 128), 1)
    gains = ((at // 16 == to % 8) & (at % 8 == 6 + to // 8) & (to < 16)).astype(BF)
    rows = [blocks[:, k].reshape(128, HALF) for k in range(5)]
    found = [dot(pick, value).astype(BF) for value in rows] + [dot(gains, rows[0]).astype(BF)]
    for copy in range(8):
        for k, value in enumerate(found):
            attn[copy, 96 * k : 96 * k + value.shape[0], :] = value


def weight_at(attn, k):
    return attn[:, 96 * k : 96 * k + 96, :].reshape(D, HALF)


def attn_forward_kernel(
    scal,
    seq,
    seq_other,
    cosine,
    sine,
    start,
    wanted,
    attn,
    q,
    k_all,
    v_all,
    h_all,
    h_t,
    x_chip,
    probs,
    po,
    g1_out,
    g2_out,
    x_all,
    bias,
    pa,
):
    z, core = scal[0], scal[1]
    own = pl.ds(pl.multiple_of(z * TOK, TOK), TOK)
    pa[...] = placed_matrix(wanted[3:4, :])
    held = attn[:, 480:496, 0:128].astype(F32).reshape(8, 2, 8, 128)
    block = lax.broadcasted_iota(jnp.int32, (64, D), 0)
    place = lax.broadcasted_iota(jnp.int32, (64, D), 1)
    lane = lax.broadcasted_iota(jnp.int32, (128, D), 0)
    row = lax.broadcasted_iota(jnp.int32, (128, D), 1) % 12
    fold = (lane == (row // 6) * 8 + row % 6).astype(BF)
    for k, out in ((0, g1_out), (1, g2_out)):
        wide = dot(held[:, k].reshape(64, 128).astype(BF), fold)
        line = jnp.sum(jnp.where(place // 12 == block, wide, 0.0), axis=0, keepdims=True)
        out[...] = dot_nt(jnp.broadcast_to(line, (8, D)).astype(BF), pa[...])
    g1 = g1_out[0:1, :]
    wq, wk, wv = (weight_at(attn, k) for k in range(3))

    def turn(raw, at, t):
        u = raw[:, 128 * t : 128 * t + 128]
        return (u * cosine[at, :] + swap_halves(u) * sine[at, :]).astype(BF)

    for c, blocks in ((core, seq), (1 - core, seq_other)):
        for k, flip in enumerate(FLIPS):
            at = (((z + c) % 4 ^ flip) + 4 - c) % 4 * TOK + c * 128
            x_all[pl.ds(pl.multiple_of(at, 128), 128), :] = blocks[k, 0:128, :]
    x_chip[...] = x_all[own, :]
    for b in range(4):
        at = slice(b * TOK, (b + 1) * TOK)
        x16 = x_all[at, :]
        x = x16.astype(F32)
        scale = lax.rsqrt(jnp.mean(x * x, axis=1, keepdims=True) + EPS)
        h1 = dot((x * scale * g1).astype(BF), pa[...]).astype(BF)
        h_all[at, :] = h1
        raw = dot(h1, wk)
        for t in range(3):
            k_all[at, 128 * t : 128 * t + 128] = turn(raw, at, t)
        v_all[at, :] = dot(h1, wv).astype(BF)

    raw = dot(h_all[own, :], wq)
    for t in range(3):
        q[:, 128 * t : 128 * t + 128] = turn(raw, own, t) * BF(0.125)

    key = lax.broadcasted_iota(jnp.int32, (LEN, TOK), 0).astype(F32)
    query = (lax.broadcasted_iota(jnp.int32, (LEN, TOK), 1) + z * TOK).astype(F32)
    bias[...] = jnp.where((key >= start[0:1, own]) & (key <= query), 0.0, MASKED)
    sub = lax.broadcasted_iota(jnp.int32, (128, TOK), 0)
    for t in range(3):
        cols = slice(128 * t, 128 * t + 128)
        q_tile, k_tile = q[:, cols], k_all[:, cols]
        v_t = v_all[:, cols].T
        mixed = []
        for odd in range(2):
            s = dot_nt(k_tile, lanes_of(q_tile, odd)) + bias[...]
            top = jnp.max(s, axis=0, keepdims=True)
            expo = jnp.exp(s - top)
            total = jnp.sum(expo, axis=0, keepdims=True)
            pb = (expo * (1.0 / total)).astype(BF)
            probs[2 * t + odd] = pb
            mixed.append(dot(v_t, pb))
        po[:, D + 128 * t : D + 128 * t + 128] = jnp.where(sub < HD, mixed[0], mixed[1]).T.astype(BF)
    h_t[...] = h_all[...].T
    half = pl.ds(pl.multiple_of(core * HALF, HALF), HALF)
    placed = dot(po[:, D:], pa[half, :]).astype(BF)
    po[:, :HALF] = dot(placed, weight_at(attn, 3)).astype(BF)
    po[:, HALF:D] = dot(placed, weight_at(attn, 4)).astype(BF)


def ffn_kernel(
    scal,
    chips,
    x,
    part_a,
    part_b,
    cot,
    cot_other,
    wanted,
    g2,
    wg,
    wu,
    wd,
    out_keep,
    dh2_out,
    resid,
    keep_g,
    send_g,
    keep_u,
    send_u,
    keep_d,
    send_d,
    pn,
    dense,
    h2p,
    h2p_t,
    dy,
    acc_out,
    acc_dh2,
    grad_d,
):
    core = scal[1]
    j = pl.program_id(0)

    @pl.when(j == 0)
    def _():
        r = x[...].astype(F32) + (part_a[...].astype(F32) + part_b[...].astype(F32))
        resid[...] = r
        scale = lax.rsqrt(jnp.mean(r * r, axis=1, keepdims=True) + EPS)
        h2 = (r * scale * g2[0:1, :]).astype(BF)
        pn[...] = placed_matrix(wanted[4:5, :])
        to = lax.broadcasted_iota(jnp.int32, (HALF, HALF), 0)
        at = (to % 96 // 12) * 48 + 12 * (to // 96) + to % 12
        pick = (lax.broadcasted_iota(jnp.int32, (HALF, HALF), 1) == at).astype(BF)
        for k, w in ((0, wg), (1, wu)):
            for q in range(8):
                rows = dot(pick, w[8 * q : 8 * q + 8].reshape(HALF, HALF)).astype(BF)
                dense[k, :, 96 * q : 96 * q + 96, :] = rows.reshape(4, 96, HALF)
        h2p[...] = dot(h2, pn[...]).astype(BF)
        for k in range(2):
            h2p_t[k] = dot(h2, placed_matrix(wanted[k : k + 1, :])).astype(BF).T
        dy[pl.ds(pl.multiple_of(core * 128, 128), 128), :] = cot[...]
        dy[pl.ds(pl.multiple_of((1 - core) * 128, 128), 128), :] = cot_other[...]
        acc_out[...] = jnp.zeros_like(acc_out)
        acc_dh2[...] = jnp.zeros_like(acc_dh2)

    w_gate, w_up = dense[0, j], dense[1, j]
    gate, up = dot(h2p[...], w_gate), dot(h2p[...], w_up)
    blocks = wd[...].reshape(16, 3, 16, HALF).astype(F32)
    w_down = jnp.concatenate(
        [blocks[:, :, 0:8, :].reshape(HALF, HALF), blocks[:, :, 8:16, :].reshape(HALF, HALF)], axis=1
    ).astype(BF)
    sig = jax.nn.sigmoid(gate)
    hidden = (gate * sig * up).astype(BF)
    acc_out[...] += dot(hidden, w_down)
    dhid = dot_nt(dy[...], w_down)
    dgate = (dhid * up * sig * (1.0 + gate * (1.0 - sig))).astype(BF)
    dup = (dhid * gate * sig).astype(BF)
    acc_dh2[...] += dot_nt(dgate, w_gate) + dot_nt(dup, w_up)

    for part, value, keep, send in ((0, dgate, keep_g, send_g), (1, dup, keep_u, send_u)):
        grad = dot(h2p_t[part], value).astype(BF).reshape(8, 96, HALF)
        keep[...] = grad[:4]
        send[...] = grad[4:]
    grad_d[pl.ds(pl.multiple_of(j * HALF, HALF), HALF), :] = dot_tn(hidden, dy[...])

    @pl.when(j == 3)
    def _():
        mine = pl.multiple_of(core * 128, 128)
        other = pl.multiple_of((1 - core) * 128, 128)
        out_keep[...] = acc_out[pl.ds(mine, 128), :]
        dh2_out[:TOK, :] = dot_nt(acc_dh2[...].astype(BF), pn[...]).astype(BF)
        dh2_out[TOK:, :] = acc_out[pl.ds(other, 128), :].astype(BF)

        def write(w, carry):
            for at, out in ((w, keep_d), (w + 32, send_d)):
                base = chips[2, at] * 24
                for k in range(3):
                    rows = grad_d[pl.ds(pl.multiple_of(base + 8 * k, 8), 8), :]
                    out[w, k] = jnp.concatenate([rows[:, :HALF], rows[:, HALF:]], axis=0).astype(BF)
            return carry

        lax.fori_loop(0, 32, write, 0, unroll=2)


def attn_backward_kernel(
    scal,
    resid,
    dh2_a,
    dh2_b,
    g2,
    cot,
    cot_other,
    wo_a,
    wo_b,
    wanted,
    probs,
    o_mine,
    o_other,
    q,
    k_all,
    v_all,
    h_t_in,
    cosine_in,
    sine_in,
    dres_out,
    dq_out,
    dk_out,
    dv_out,
    grads,
    do,
    inner,
    grad_o,
    pa,
    h_t,
    cosine,
    sine,
    sems,
):
    core = scal[1]
    own = pl.ds(pl.multiple_of(scal[0] * TOK, TOK), TOK)
    step = pl.program_id(0)
    copies = [
        pltpu.make_async_copy(source, target, sems.at[k])
        for k, (source, target) in enumerate(((h_t_in, h_t), (cosine_in, cosine), (sine_in, sine)))
    ]

    @pl.when(step == 0)
    def _():
        for copy in copies:
            copy.start()
        pa[...] = placed_matrix(wanted[3:4, :])
        r = resid[...]
        dh2 = dh2_a[...].astype(F32) + dh2_b[...].astype(F32)
        scale = lax.rsqrt(jnp.mean(r * r, axis=1, keepdims=True) + EPS)
        weighted = dh2 * g2[0:1, :]
        mean = jnp.mean(weighted * r, axis=1, keepdims=True)
        mine, theirs = cot[...].astype(F32), cot_other[...].astype(F32)
        dy = jnp.concatenate([jnp.where(core == 0, mine, theirs), jnp.where(core == 0, theirs, mine)], axis=0)
        dres = dy + (scale * weighted - r * (scale * scale * scale) * mean)
        dresb = dres.astype(BF)
        placed = dot_nt(dresb[:, :HALF], wo_a[...].reshape(D, HALF)) + dot_nt(dresb[:, HALF:], wo_b[...].reshape(D, HALF))
        half = pl.ds(pl.multiple_of(core * HALF, HALF), HALF)
        found = dot_nt(placed.astype(BF), pa[half, :]).astype(BF)
        head_of = (
            lax.broadcasted_iota(jnp.int32, (8, HALF), 1) // HD == lax.broadcasted_iota(jnp.int32, (8, HALF), 0)
        ).astype(F32)
        o_a, o_b = o_mine[...], o_other[...]
        inner[...] = lax.dot_general(
            head_of,
            found.astype(F32) * o_a.astype(F32),
            (((1,), (1,)), ((), ())),
            precision=lax.Precision.HIGHEST,
            preferred_element_type=F32,
        )
        o_full = jnp.concatenate([jnp.where(core == 0, o_a, o_b), jnp.where(core == 0, o_b, o_a)], axis=1)
        d_mine = jnp.where(core == 0, dresb[:, :HALF], dresb[:, HALF:])
        found_o = dot_tn(dot(o_full, pa[...]).astype(BF), d_mine).astype(BF)
        for t in range(3):
            do[t] = found[:, 128 * t : 128 * t + 128]
            grad_o[t] = found_o[:, 128 * t : 128 * t + 128].reshape(8, 96, 128)
        dres_out[0] = dres[0:128, :]
        dres_out[1] = dres[128:256, :]

    @pl.when(step == 1)
    def _():
        for copy in copies:
            copy.wait()

    @pl.when(step > 0)
    def _():
        t = step - 1
        sub = lax.broadcasted_iota(jnp.int32, (128, TOK), 0)
        q_tile, do_tile, v_tile = q[...], do[t], v_all[...]
        k_t = k_all[...].T
        dqs, dks, dvs = [], [], []
        for odd in range(2):
            pb = probs[odd]
            dp = dot_nt(v_tile, lanes_of(do_tile, odd))
            ds = (pb.astype(F32) * (dp - inner[pl.ds(2 * t + odd, 1), :])).astype(BF)
            dks.append(dot(ds, q_tile))
            dvs.append(dot(pb, do_tile))
            dqs.append(dot(k_t, ds))
        u = jnp.where(sub < HD, dqs[0], dqs[1]).T * 0.125
        dq = (u * cosine[own, :] - swap_halves(u) * sine[own, :]).astype(BF)
        u = join_lanes(dks[0], dks[1])
        dk = (u * cosine[...] - swap_halves(u) * sine[...]).astype(BF)
        dv = join_lanes(dvs[0], dvs[1]).astype(BF)
        dq_out[...] = dq
        dk_out[...] = dk
        dv_out[...] = dv
        both = dot(h_t[...], jnp.concatenate([dk, dv], axis=1)).astype(BF)
        grads[:, 0:96, :] = dot(h_t[:, own], dq).astype(BF).reshape(8, 96, 128)
        grads[:, 96:192, :] = both[:, :128].reshape(8, 96, 128)
        grads[:, 192:288, :] = both[:, 128:].reshape(8, 96, 128)
        grads[:, 288:384, :] = grad_o[t]


def dh1_kernel(scal, dq, dk, dv, attn, wanted, out, pa, total):
    @pl.when(pl.program_id(0) == 0)
    def _():
        pa[...] = placed_matrix(wanted[3:4, :])

    total[...] = dot_nt(dk[...], weight_at(attn, 1)) + dot_nt(dv[...], weight_at(attn, 2))

    @pl.when(scal[0] == pl.program_id(0))
    def _():
        total[...] += dot_nt(dq[...], weight_at(attn, 0))

    out[...] = dot_nt(total[...].astype(BF), pa[...]).astype(BF)


def terms_kernel(*refs):
    for k in range(3):
        total = (refs[2 * k][...].astype(F32) + refs[2 * k + 1][...].astype(F32)).astype(BF)
        half = total.shape[0] // 2
        refs[6 + 2 * k][...] = total[:half]
        refs[7 + 2 * k][...] = total[half:]


def padded_kernel(x0, y0, x1, y1, x2, y2, attn, out):
    pick = dense_rows()

    def write(at, rows):
        out[:, at] = dot_tn(pick, rows).astype(BF).reshape(8, 16, HALF)

    for at, x, y in ((0, x0, y0), (4, x1, y1)):
        total = (x[0].astype(F32) + y[0].astype(F32)).astype(BF)
        for k in range(4):
            write(at + k, total[96 * k : 96 * k + 96])
    out[:, 12:15] = (x2[0].astype(F32) + y2[0].astype(F32)).astype(BF).reshape(8, 3, 16, HALF)
    for k in range(4):
        rows = slice(96 * k, 96 * k + 96)
        total = attn[0, rows, :].astype(F32)
        for b in range(1, 8):
            total += attn[b, rows, :].astype(F32)
        write(8 + k, total.astype(BF))


def sum_kernel(scal, blocks, total, other):
    core = scal[1]
    for k in range(15):
        value = blocks[0, k].astype(F32)
        for b in range(1, 8):
            value += blocks[b, k].astype(F32)
        total[k] = value
        other[k] = jnp.where(core == 0, value[8:16], value[0:8])


def update_kernel(scal, mine, theirs, x_ref, dh1_ref, g1, dres, resid, out_a, out_b, *refs):
    core = scal[1]
    output, input_grad = refs[56:58]
    x = x_ref[...].astype(F32)
    dh1 = dh1_ref[...].astype(F32)
    scale = lax.rsqrt(jnp.mean(x * x, axis=1, keepdims=True) + EPS)
    weighted = dh1 * g1[0:1, :]
    inner = jnp.mean(weighted * x, axis=1, keepdims=True)
    input_grad[...] = dres[core] + (scale * weighted - x * (scale * scale * scale) * inner)
    tokens = pl.ds(pl.multiple_of(core * 128, 128), 128)
    output[...] = (resid[tokens, :] + (out_a[...] + out_b[TOK:, :].astype(F32))).astype(BF)
    masters, moments, averages = refs[0:8], refs[8:16], refs[16:24]
    news, moms, means, copies = refs[24:32], refs[32:40], refs[40:48], refs[48:56]
    base = 1.0 / math.sqrt(16384)

    def step(k, at, grad):
        rate = RATES[k] * base
        moment = MOMENTUM * moments[k][at] + grad
        new = masters[k][at] - rate * (grad + MOMENTUM * moment)
        news[k][at] = new
        moms[k][at] = moment
        means[k][at] = AVERAGE * averages[k][at] + (1.0 - AVERAGE) * new
        copies[k][at] = new.astype(BF)

    def halves(a, b):
        return (jnp.where(core == 0, a, b), jnp.where(core == 0, b, a))

    gain_sums = [jnp.zeros((6, 128), F32), jnp.zeros((6, 128), F32)]

    def weigh(which, k, at, grad):
        product = masters[k][at].astype(BF).astype(F32) * grad
        for c in range(0, product.shape[1], 128):
            gain_sums[which] += product[:, c : c + 128]

    own = pl.ds(pl.multiple_of(core * 8, 8), 8)

    def chunk(k):
        a, b = mine[k, own, :][0:6, :], theirs[k][0:6, :]
        return (jnp.where(core == 0, a, b), jnp.where(core == 0, b, a))

    for k, weight, offset, gain in (
        (8, 0, 0, 0),
        (9, 1, 0, 0),
        (10, 2, 0, 0),
        (11, 3, 0, None),
        (0, 4, 0, 1),
        (1, 4, D, 1),
        (2, 4, 2 * D, 1),
        (3, 4, 3 * D, 1),
        (4, 5, 0, 1),
        (5, 5, D, 1),
        (6, 5, 2 * D, 1),
        (7, 5, 3 * D, 1),
    ):
        for h, grad in enumerate(chunk(k)):
            at = (slice(0, 6), slice(offset + h * HALF, offset + (h + 1) * HALF))
            step(weight, at, grad)
            if gain is not None:
                weigh(gain, weight, at, grad)
    for j in range(3):
        for h in range(2):
            grad = mine[12 + j, 8 * h : 8 * h + 8, :]
            step(6, (slice(8 * j, 8 * j + 8), slice(h * HALF, (h + 1) * HALF)), grad)
    row = lax.broadcasted_iota(jnp.int32, (6, 128), 0)
    lane = lax.broadcasted_iota(jnp.int32, (6, 128), 1)
    for k in range(2):
        column = jnp.sum(gain_sums[k], axis=1, keepdims=True)
        line = jnp.sum(jnp.where(lane == row, column, 0.0), axis=0, keepdims=True)[:, 0:6]
        at = (slice(k, k + 1), slice(0, 6))
        step(7, at, line / masters[7][at].astype(BF).astype(F32))


def whole():
    return pl.BlockSpec(memory_space=pltpu.VMEM)


def scalars():
    return pl.BlockSpec(memory_space=pltpu.SMEM)


def call(kernel, out_shape, operands, scratch=(), smem=1, name=None, micros=1.0, mib=60):
    specs = [scalars() if k < smem else whole() for k in range(len(operands))]
    return pl.pallas_call(
        kernel,
        out_shape=out_shape,
        in_specs=specs,
        out_specs=jax.tree.map(lambda _: whole(), out_shape),
        scratch_shapes=list(scratch),
        compiler_params=params(mib),
        cost_estimate=cost(micros),
        name=name,
    )(*operands)


def shape(dims, kind):
    return jax.ShapeDtypeStruct(dims, kind)


def add(a, b):
    return (a.astype(F32) + b.astype(F32)).astype(BF)


def fetch(block, axis):
    return permute(block, flip_pairs(axis, 3))


def first_terms(parts):
    return [fetch(send, order[0]) for order, (_, send) in reversed(list(zip(ORDERS, parts)))][::-1]


def next_terms(keeps, got):
    count, rows = keeps[0].shape[0], 192
    pair = [pl.BlockSpec((count // 2, rows, HALF), lambda j: (0, j, 0))] * 6
    out = pl.pallas_call(
        terms_kernel,
        out_shape=(shape((count // 2, HALF, HALF), BF),) * 6,
        grid=(HALF // rows,),
        in_specs=[pl.BlockSpec((count, rows, HALF), lambda j: (0, j, 0))] * 6,
        out_specs=tuple(pair),
        compiler_params=params(54),
        cost_estimate=cost(1),
        name="next_terms",
    )(*(v for pair in zip(keeps, got) for v in pair))
    return out[::2], out[1::2]


def reduce_rows(parts, got, after):
    keeps, sents = next_terms([keep for keep, _ in parts], got)
    got = [fetch(sent, order[1]) for sent, order in zip(sents, ORDERS)]
    got, after = lax.optimization_barrier((got, after))
    keeps, sents = next_terms(keeps, got)
    got = [fetch(sent, order[2]) for sent, order in zip(sents, ORDERS)]
    return [term for pair in zip(keeps, got) for term in pair], after


def flipped(block, flip):
    return permute(block, flip_pairs("z", flip))


def shards(inputs, doc_ids, cotangent, *state):
    state = tuple(v.T if k % 8 == 7 else v for k, v in enumerate(state))
    masters, moments, averages = state[0:8], state[8:16], state[16:24]
    z, core = lax.axis_index("z"), lax.axis_index("core")
    y, x_at = lax.axis_index("y"), lax.axis_index("x")
    scal = jnp.stack([z, core]).astype(jnp.int32)
    chips = chip_of_place({"z": z, "y": y, "x": x_at}, core)

    halves = shape((8, 8, HALF), F32)
    wq, wk, wv, wo, wg, wu, wd, gains = masters
    keep, send = call(pack_ffn_kernel, (halves, halves), (scal, wg, wu), name="pack_feed_forward")
    ffn_w = call(
        merge_ffn_kernel,
        shape((144, HALF), BF),
        (scal, keep, permute(send, CORE_PAIRS), wd),
        name="merge_feed_forward",
        mib=56,
    )
    ffn_w, wq, wk, wv, wo, gains, inputs, doc_ids, cotangent = lax.optimization_barrier(
        (ffn_w, wq, wk, wv, wo, gains, inputs, doc_ids, cotangent)
    )
    ffn_w = lax.all_gather(ffn_w, ("z", "y", "x"), axis=0, tiled=False)
    halves = shape((5, 8, HALF), F32)
    keep, send = call(
        pack_attn_kernel,
        (halves, halves),
        (scal, wq, wk, wv, wo, gains),
        scratch=(pltpu.VMEM((8, 128), F32),),
        name="pack_attention",
    )
    theirs, cot_other = permute(send, CORE_PAIRS), permute(cotangent[0], CORE_PAIRS)
    theirs, cot_other = lax.optimization_barrier((theirs, cot_other))
    attn = call(merge_attn_kernel, shape((8, 5, 16, HALF), BF), (scal, keep, theirs), name="merge_attention", mib=56)

    ids_row = jnp.zeros((16, D), BF).at[0, :128].set(doc_ids[0].astype(BF))
    block = jnp.concatenate([inputs[0], ids_row], axis=0)
    attn, block = lax.optimization_barrier((attn, block))
    attn = exchange(attn, 1)
    seq = [block, flipped(block, 1), flipped(block, 3)]
    wanted = placed_features(chips)
    attn, wanted, chips = lax.optimization_barrier((attn, wanted, chips))
    attn = call(dense_kernel, shape((8, 512, HALF), BF), (attn,), smem=0, name="dense_rows", mib=16)
    attn = exchange(attn, 3)
    seq.append(flipped(seq[1], 3))
    seq = jnp.stack(seq)
    seq_other = permute(seq, CORE_PAIRS)
    ids = jnp.concatenate([seq[:, 128, :128], seq_other[:, 128, :128]], axis=0).astype(F32)
    spots = [(((z + c) % 4 ^ flip) + 4 - c) % 4 * 2 + c for c in (core, 1 - core) for flip in FLIPS]
    here = jnp.stack(spots)[None, :] == jnp.arange(8)[:, None]
    ids = jnp.sum(jnp.where(here[:, :, None], ids[None], 0.0), axis=1).reshape(LEN)
    starts = jnp.sum((ids[None, :] < ids[:, None]).astype(jnp.int32), axis=1)
    freq = 10000.0 ** (-jnp.arange(0, HD, 2, dtype=F32) / HD)
    spot = (jnp.arange(LEN, dtype=jnp.int32) - starts).astype(F32)
    theta = spot[:, None] * jnp.tile(freq, 4)[None, :]
    sign = jnp.tile(jnp.repeat(jnp.array([-1.0, 1.0], F32), HD // 2), 2)
    cosine, sine = jnp.cos(theta), jnp.sin(theta) * sign[None, :]
    start_row = jnp.broadcast_to(starts.astype(F32)[None, :], (8, LEN))

    q, k_all, v_all, h_all, h_t, x_chip, probs, po, g1, g2 = call(
        attn_forward_kernel,
        (
            shape((TOK, HALF), BF),
            shape((LEN, HALF), BF),
            shape((LEN, HALF), BF),
            shape((LEN, D), BF),
            shape((D, LEN), BF),
            shape((TOK, D), BF),
            shape((HEADS, LEN, TOK), BF),
            shape((TOK, D + HALF), BF),
            shape((8, D), F32),
            shape((8, D), F32),
        ),
        (scal, seq, seq_other, cosine, sine, start_row, wanted, attn),
        scratch=(pltpu.VMEM((LEN, D), BF), pltpu.VMEM((LEN, TOK), F32), pltpu.VMEM((D, D), BF)),
        name="attention_forward",
        mib=54,
        micros=1.3e7,
    )
    po_other = permute(po, CORE_PAIRS)

    def full(dims):
        return pl.BlockSpec(dims, lambda i, n=len(dims): (0,) * n)

    ffn_out = (
        shape((128, D), F32),
        shape((TOK + 128, D), BF),
        shape((TOK, D), F32),
    ) + tuple(shape((4, HALF, HALF), BF) for _ in range(4)) + tuple(shape((32, 3, 16, HALF), BF) for _ in range(2))
    column = pl.BlockSpec((4, 96, HALF), lambda j: (0, j, 0))
    out_keep, dh2, resid, kg, sg, ku, su, kd, sd = pl.pallas_call(
        ffn_kernel,
        out_shape=ffn_out,
        grid=(4,),
        in_specs=[
            scalars(),
            scalars(),
            full((TOK, D)),
            full((TOK, D)),
            full((TOK, D)),
            full((128, D)),
            full((128, D)),
            full((8, D)),
            full((8, D)),
            pl.BlockSpec((64, 48, HALF), lambda j: (0, 0, 0)),
            pl.BlockSpec((64, 48, HALF), lambda j: (0, 1, 0)),
            pl.BlockSpec((16, 48, HALF), lambda j: (j, 2, 0)),
        ],
        out_specs=tuple(full(s.shape) for s in ffn_out[:3])
        + (column,) * 4
        + tuple(full(s.shape) for s in ffn_out[7:]),
        scratch_shapes=[
            pltpu.VMEM((D, D), BF),
            pltpu.VMEM((2, 4, D, HALF), BF),
            pltpu.VMEM((TOK, D), BF),
            pltpu.VMEM((2, D, TOK), BF),
            pltpu.VMEM((TOK, D), BF),
            pltpu.VMEM((TOK, D), F32),
            pltpu.VMEM((TOK, D), F32),
            pltpu.VMEM((FF // 2, D), F32),
        ],
        compiler_params=params(),
        cost_estimate=cost(4),
        name="feed_forward",
    )(
        scal,
        chips,
        x_chip,
        po,
        po_other,
        cotangent[0],
        cot_other,
        wanted,
        g2,
        *((ffn_w,) * 3),
    )

    dh2_other = permute(dh2, CORE_PAIRS)
    dh2_other, kg, sg, ku, su, kd, sd = lax.optimization_barrier((dh2_other, kg, sg, ku, su, kd, sd))
    at_tile = lambda i: jnp.maximum(i - 1, 0)
    short = pl.BlockSpec((TOK, 128), lambda i: (0, at_tile(i)))
    long = pl.BlockSpec((LEN, 128), lambda i: (0, at_tile(i)))
    dres, dq, dk, dv, grads = pl.pallas_call(
        attn_backward_kernel,
        out_shape=(
            shape((2, 128, D), F32),
            shape((TOK, HALF), BF),
            shape((LEN, HALF), BF),
            shape((LEN, HALF), BF),
            shape((8, HALF, HALF), BF),
        ),
        grid=(4,),
        in_specs=[
            scalars(),
            full((TOK, D)),
            full((TOK, D)),
            full((TOK, D)),
            full((8, D)),
            full((128, D)),
            full((128, D)),
            pl.BlockSpec((8, 96, HALF), lambda i: (0, 3, 0)),
            pl.BlockSpec((8, 96, HALF), lambda i: (0, 4, 0)),
            full((8, D)),
            pl.BlockSpec((2, LEN, TOK), lambda i: (at_tile(i), 0, 0)),
            pl.BlockSpec((TOK, HALF), lambda i: (0, 2)),
            pl.BlockSpec((TOK, HALF), lambda i: (0, 2)),
            short,
            long,
            long,
            *([pl.BlockSpec(memory_space=pl.ANY)] * 3),
        ],
        out_specs=(
            full((2, 128, D)),
            short,
            long,
            long,
            pl.BlockSpec((8, HALF, 128), lambda i: (0, 0, at_tile(i))),
        ),
        scratch_shapes=[
            pltpu.VMEM((3, TOK, 128), BF),
            pltpu.VMEM((8, TOK), F32),
            pltpu.VMEM((3, 8, 96, 128), BF),
            pltpu.VMEM((D, D), BF),
            pltpu.VMEM((D, LEN), BF),
            pltpu.VMEM((LEN, 128), F32),
            pltpu.VMEM((LEN, 128), F32),
            pltpu.SemaphoreType.DMA((3,)),
        ],
        compiler_params=params(),
        cost_estimate=cost(1),
        name="attention_backward",
    )(
        scal,
        resid,
        dh2,
        dh2_other,
        g2,
        cotangent[0],
        cot_other,
        attn,
        attn,
        wanted,
        probs,
        po,
        po_other,
        q,
        k_all,
        v_all,
        h_t,
        cosine,
        sine,
    )
    parts = [(kg, sg), (ku, su), (kd.reshape(4, HALF, HALF), sd.reshape(4, HALF, HALF))]
    got = first_terms(parts)
    exchanged = exchange(grads, 3)
    grads, dq, dk, dv, got = lax.optimization_barrier((grads, dq, dk, dv, got))
    grads = exchanged
    dh1 = pl.pallas_call(
        dh1_kernel,
        out_shape=shape((LEN, D), BF),
        grid=(4,),
        in_specs=[
            scalars(),
            full((TOK, HALF)),
            pl.BlockSpec((TOK, HALF), lambda b: (b, 0)),
            pl.BlockSpec((TOK, HALF), lambda b: (b, 0)),
            pl.BlockSpec((8, 288, HALF), lambda b: (0, 0, 0)),
            full((8, D)),
        ],
        out_specs=pl.BlockSpec((TOK, D), lambda b: (b, 0)),
        scratch_shapes=[pltpu.VMEM((D, D), BF), pltpu.VMEM((TOK, D), F32)],
        compiler_params=params(),
        cost_estimate=cost(1),
        name="attention_input_gradient",
    )(scal, dq, dk, dv, attn, wanted)
    terms, dh1 = reduce_rows(parts, got, dh1)
    dh1 = lax.psum_scatter(dh1, ("z", "core"), scatter_dimension=0, tiled=True)
    blocks = call(padded_kernel, shape((8, 15, 16, HALF), BF), (*terms, grads), smem=0, name="padded_rows", mib=54)
    blocks = exchange(blocks, 1)

    grads, theirs = call(
        sum_kernel, (shape((15, 16, HALF), F32), shape((15, 8, HALF), F32)), (scal, blocks), name="sum_blocks", mib=16
    )
    theirs = permute(theirs, CORE_PAIRS)
    shapes = tuple(shape(m.shape, F32) for m in masters)
    outs = call(
        update_kernel,
        shapes * 3 + tuple(shape(m.shape, BF) for m in masters) + (shape((128, D), BF), shape((128, D), F32)),
        (scal, grads, theirs, inputs[0], dh1, g1, dres, resid, out_keep, dh2_other, *masters, *moments, *averages),
        name="update",
        mib=56,
    )
    outs, output, input_grad = outs[:32], *outs[32:]
    outs = tuple(v.T if k % 8 == 7 else v for k, v in enumerate(outs))
    return (output[None], input_grad[None], *outs)


def solution(mesh):
    fine = Mesh(mesh.devices.reshape(4, 2, 4, 4), AXES)
    tokens = P(("y", "x"), ("z", "core"), None)
    rows = P(("z", "core", "y", "x"), None)
    return jax.shard_map(
        shards,
        mesh=fine,
        in_specs=(tokens, P(("y", "x"), ("z", "core")), tokens) + (rows,) * 24,
        out_specs=(tokens, tokens) + (rows,) * 32,
        check_vma=False,
    )
```

```python
import functools
import math

import jax
import jax.numpy as jnp
import numpy as np
from jax import lax
from jax.experimental import pallas as pl
from jax.experimental.pallas import tpu as pltpu
from jax.sharding import Mesh
from jax.sharding import PartitionSpec as P


BF = jnp.bfloat16
F32 = jnp.float32
HD = 64
D = 768
FF = 3072
HALF = 384
TOK = 256
LEN = 1024
HEADS = 6
EPS = 1e-05
MOMENTUM = 0.9
AVERAGE = 0.5
RATES = (0.01, 0.01, 0.01, 4.0, 0.02, 0.02, 0.015, 0.1)
MASKED = -1e30
AXES = ("z", "core", "y", "x")


def params(mib=60):
    return pltpu.CompilerParams(vmem_limit_bytes=mib * 1024 * 1024)


def cost(micros):
    return pl.CostEstimate(flops=1 + int(micros * 1e3), bytes_accessed=1, transcendentals=0)


def device_pairs(move):
    pairs = []
    for z in range(4):
        for c in range(2):
            for y in range(4):
                for x in range(4):
                    to = move(z, c, y, x)
                    pairs.append((((z * 2 + c) * 4 + y) * 4 + x, ((to[0] * 2 + to[1]) * 4 + to[2]) * 4 + to[3]))
    return pairs


CORE_PAIRS = device_pairs(lambda z, c, y, x: (z, 1 - c, y, x))


AXIS = {"z": 0, "y": 2, "x": 3}
FLIPS = (0, 1, 3, 2)
ORDERS = (("x", "y", "z"), ("y", "z", "x"), ("z", "x", "y"))


def flip_pairs(axis, flip):
    def move(z, c, y, x):
        at = [z, c, y, x]
        at[AXIS[axis]] = (((at[AXIS[axis]] + c) % 4 ^ flip) - c) % 4
        return tuple(at)

    return device_pairs(move)


def permute(value, pairs):
    return lax.ppermute(value, AXES, pairs)


def cube_groups(flip):
    groups = {}
    for z in range(4):
        for c in range(2):
            for y in range(4):
                for x in range(4):
                    u = [(v + c) % 4 for v in (z, y, x)]
                    key = (c,) + tuple(min(v, v ^ flip) for v in u)
                    place = sum((v & 1 if flip == 1 else v >> 1) << (2 - k) for k, v in enumerate(u))
                    groups.setdefault(key, [None] * 8)[place] = ((z * 2 + c) * 4 + y) * 4 + x
    return list(groups.values())


def exchange(blocks, flip):
    return lax.all_to_all(blocks, AXES, 0, 0, tiled=True, axis_index_groups=cube_groups(flip))


def chip_of_place(me, core):
    place = np.arange(64)
    rows = []
    for order in ORDERS + (None,):
        at = {}
        for k, axis in enumerate("zyx"):
            low = jnp.asarray((place >> (2 - k)) & 1)
            high = jnp.asarray((place >> (5 - (order.index(axis) if order else k))) & 1)
            if order:
                high = high ^ (((me[axis] + core) % 4) >> 1)
            at[axis] = (high * 2 + low - core) % 4
        rows.append(at["z"] * 16 + at["y"] * 4 + at["x"])
    return jnp.stack(rows).astype(jnp.int32)


def placed_features(chips):
    chips = jnp.concatenate([chips, jnp.arange(64, dtype=jnp.int32)[None, :]], axis=0)
    row = jnp.arange(12, dtype=jnp.int32)[None, None, :]
    chip = chips[:, :, None]
    wanted = (((chip // 16) * 2 + row // 6) * 16 + chip % 16) * 6 + row % 6
    return jnp.pad(wanted.reshape(5, D), ((0, 3), (0, 0)))


def placed_matrix(wanted):
    return (lax.broadcasted_iota(jnp.int32, (D, D), 0) == wanted).astype(BF)


def dot(left, right):
    return jnp.dot(left, right, preferred_element_type=F32)


def dot_nt(left, right):
    return lax.dot_general(left, right, (((1,), (1,)), ((), ())), preferred_element_type=F32)


def dot_tn(left, right):
    return lax.dot_general(left, right, (((0,), (0,)), ((), ())), preferred_element_type=F32)


def swap_halves(tile):
    lane = lax.broadcasted_iota(jnp.int32, tile.shape, 1)
    return jnp.where(lane % HD < HD // 2, pltpu.roll(tile, 96, 1), pltpu.roll(tile, 32, 1))


def lanes_of(tile, odd):
    lane = lax.broadcasted_iota(jnp.int32, tile.shape, 1)
    return jnp.where((lane >= HD) == bool(odd), tile, jnp.zeros_like(tile))


def join_lanes(even, odd):
    lane = lax.broadcasted_iota(jnp.int32, even.shape, 1)
    return jnp.where(lane < HD, even, odd)


def put_halves(core, w, keep, send, at):
    for part in range(w.shape[1] // D):
        halves = [w[:, part * D + h * HALF : part * D + (h + 1) * HALF] for h in range(2)]
        keep[at + part, 0:6, :] = jnp.where(core == 0, halves[0], halves[1])
        send[at + part, 0:6, :] = jnp.where(core == 0, halves[1], halves[0])
        keep[at + part, 6:8, :] = jnp.zeros((2, HALF), F32)
        send[at + part, 6:8, :] = jnp.zeros((2, HALF), F32)


def pack_ffn_kernel(scal, wg, wu, keep, send):
    put_halves(scal[1], wg, keep, send, 0)
    put_halves(scal[1], wu, keep, send, 4)


def pack_attn_kernel(scal, wq, wk, wv, wo, gains, keep, send, lines):
    core = scal[1]
    for k, w in enumerate((wq, wk, wv)):
        put_halves(core, w, keep, send, k)
    for h in range(2):
        for out in (keep, send):
            out[3 + h, 0:6, :] = wo[:, h * HALF : (h + 1) * HALF]
            out[3 + h, 6:8, :] = jnp.zeros((2, HALF), F32)
    lines[...] = jnp.zeros_like(lines)
    lines[0:2, 0:6] = gains[...]
    moved = jnp.where(core == 0, lines[...], pltpu.roll(lines[...], 8, 1))
    keep[0, 6:8, 0:128] = moved[0:2, :]
    send[0, 6:8, 0:128] = moved[0:2, :]


def both_cores(core, keep, other):
    low = jnp.where(core == 0, keep, other)
    high = jnp.where(core == 0, other, keep)
    return jnp.concatenate([low, high], axis=0).astype(BF)


def merge_ffn_kernel(scal, keep, other, wd, ffn):
    to = lax.broadcasted_iota(jnp.int32, (48, 64), 0)
    at = lax.broadcasted_iota(jnp.int32, (48, 64), 1)
    row = to % 12
    pick = (at == (to // 12) * 16 + (row // 6) * 8 + row % 6).astype(BF)
    for w in range(2):
        blocks = [both_cores(scal[1], keep[4 * w + k], other[4 * w + k]) for k in range(4)]
        ffn[48 * w : 48 * w + 48, :] = dot(pick, jnp.concatenate(blocks, axis=0)).astype(BF)
    for j in range(3):
        rows = wd[8 * j : 8 * j + 8, :]
        ffn[96 + 16 * j : 112 + 16 * j, :] = jnp.concatenate([rows[:, :HALF], rows[:, HALF:]], axis=0).astype(BF)


def merge_attn_kernel(scal, keep, other, attn):
    for k in range(5):
        value = both_cores(scal[1], keep[k], other[k])
        for copy in range(8):
            attn[copy, k] = value


def dense_rows():
    to = lax.broadcasted_iota(jnp.int32, (96, 128), 0)
    at = lax.broadcasted_iota(jnp.int32, (96, 128), 1)
    row = to % 12
    return (at == (to // 12) * 16 + (row // 6) * 8 + row % 6).astype(BF)


def dense_kernel(blocks, attn):
    pick = dense_rows()
    to = lax.broadcasted_iota(jnp.int32, (32, 128), 0)
    at = lax.broadcasted_iota(jnp.int32, (32, 128), 1)
    gains = ((at // 16 == to % 8) & (at % 8 == 6 + to // 8) & (to < 16)).astype(BF)
    rows = [blocks[:, k].reshape(128, HALF) for k in range(5)]
    found = [dot(pick, value).astype(BF) for value in rows] + [dot(gains, rows[0]).astype(BF)]
    for copy in range(8):
        for k, value in enumerate(found):
            attn[copy, 96 * k : 96 * k + value.shape[0], :] = value


def weight_at(attn, k):
    return attn[:, 96 * k : 96 * k + 96, :].reshape(D, HALF)


def attn_forward_kernel(
    scal,
    seq,
    seq_other,
    cosine,
    sine,
    start,
    wanted,
    attn,
    q,
    k_all,
    v_all,
    h_all,
    h_t,
    x_chip,
    probs,
    po,
    g1_out,
    g2_out,
    x_all,
    bias,
    pa,
):
    z, core = scal[0], scal[1]
    own = pl.ds(pl.multiple_of(z * TOK, TOK), TOK)
    pa[...] = placed_matrix(wanted[3:4, :])
    held = attn[:, 480:496, 0:128].astype(F32).reshape(8, 2, 8, 128)
    block = lax.broadcasted_iota(jnp.int32, (64, D), 0)
    place = lax.broadcasted_iota(jnp.int32, (64, D), 1)
    lane = lax.broadcasted_iota(jnp.int32, (128, D), 0)
    row = lax.broadcasted_iota(jnp.int32, (128, D), 1) % 12
    fold = (lane == (row // 6) * 8 + row % 6).astype(BF)
    for k, out in ((0, g1_out), (1, g2_out)):
        wide = dot(held[:, k].reshape(64, 128).astype(BF), fold)
        line = jnp.sum(jnp.where(place // 12 == block, wide, 0.0), axis=0, keepdims=True)
        out[...] = dot_nt(jnp.broadcast_to(line, (8, D)).astype(BF), pa[...])
    g1 = g1_out[0:1, :]
    wq, wk, wv = (weight_at(attn, k) for k in range(3))

    def turn(raw, at, t):
        u = raw[:, 128 * t : 128 * t + 128]
        return (u * cosine[at, :] + swap_halves(u) * sine[at, :]).astype(BF)

    for c, blocks in ((core, seq), (1 - core, seq_other)):
        for k, flip in enumerate(FLIPS):
            at = (((z + c) % 4 ^ flip) + 4 - c) % 4 * TOK + c * 128
            x_all[pl.ds(pl.multiple_of(at, 128), 128), :] = blocks[k, 0:128, :]
    x_chip[...] = x_all[own, :]
    for b in range(4):
        at = slice(b * TOK, (b + 1) * TOK)
        x16 = x_all[at, :]
        x = x16.astype(F32)
        scale = lax.rsqrt(jnp.mean(x * x, axis=1, keepdims=True) + EPS)
        h1 = dot((x * scale * g1).astype(BF), pa[...]).astype(BF)
        h_all[at, :] = h1
        raw = dot(h1, wk)
        for t in range(3):
            k_all[at, 128 * t : 128 * t + 128] = turn(raw, at, t)
        v_all[at, :] = dot(h1, wv).astype(BF)

    raw = dot(h_all[own, :], wq)
    for t in range(3):
        q[:, 128 * t : 128 * t + 128] = turn(raw, own, t) * BF(0.125)

    key = lax.broadcasted_iota(jnp.int32, (LEN, TOK), 0).astype(F32)
    query = (lax.broadcasted_iota(jnp.int32, (LEN, TOK), 1) + z * TOK).astype(F32)
    bias[...] = jnp.where((key >= start[0:1, own]) & (key <= query), 0.0, MASKED)
    sub = lax.broadcasted_iota(jnp.int32, (128, TOK), 0)
    for t in range(3):
        cols = slice(128 * t, 128 * t + 128)
        q_tile, k_tile = q[:, cols], k_all[:, cols]
        v_t = v_all[:, cols].T
        mixed = []
        for odd in range(2):
            s = dot_nt(k_tile, lanes_of(q_tile, odd)) + bias[...]
            top = jnp.max(s, axis=0, keepdims=True)
            expo = jnp.exp(s - top)
            total = jnp.sum(expo, axis=0, keepdims=True)
            pb = (expo * (1.0 / total)).astype(BF)
            probs[2 * t + odd] = pb
            mixed.append(dot(v_t, pb))
        po[:, D + 128 * t : D + 128 * t + 128] = jnp.where(sub < HD, mixed[0], mixed[1]).T.astype(BF)
    h_t[...] = h_all[...].T
    half = pl.ds(pl.multiple_of(core * HALF, HALF), HALF)
    placed = dot(po[:, D:], pa[half, :]).astype(BF)
    po[:, :HALF] = dot(placed, weight_at(attn, 3)).astype(BF)
    po[:, HALF:D] = dot(placed, weight_at(attn, 4)).astype(BF)


def ffn_kernel(
    scal,
    chips,
    x,
    part_a,
    part_b,
    cot,
    cot_other,
    wanted,
    g2,
    wg,
    wu,
    wd,
    out_keep,
    dh2_out,
    resid,
    keep_g,
    send_g,
    keep_u,
    send_u,
    keep_d,
    send_d,
    pn,
    dense,
    h2p,
    h2p_t,
    dy,
    acc_out,
    acc_dh2,
    grad_d,
):
    core = scal[1]
    j = pl.program_id(0)

    @pl.when(j == 0)
    def _():
        r = x[...].astype(F32) + (part_a[...].astype(F32) + part_b[...].astype(F32))
        resid[...] = r
        scale = lax.rsqrt(jnp.mean(r * r, axis=1, keepdims=True) + EPS)
        h2 = (r * scale * g2[0:1, :]).astype(BF)
        pn[...] = placed_matrix(wanted[4:5, :])
        to = lax.broadcasted_iota(jnp.int32, (HALF, HALF), 0)
        at = (to % 96 // 12) * 48 + 12 * (to // 96) + to % 12
        pick = (lax.broadcasted_iota(jnp.int32, (HALF, HALF), 1) == at).astype(BF)
        for k, w in ((0, wg), (1, wu)):
            for q in range(8):
                rows = dot(pick, w[8 * q : 8 * q + 8].reshape(HALF, HALF)).astype(BF)
                dense[k, :, 96 * q : 96 * q + 96, :] = rows.reshape(4, 96, HALF)
        h2p[...] = dot(h2, pn[...]).astype(BF)
        for k in range(2):
            h2p_t[k] = dot(h2, placed_matrix(wanted[k : k + 1, :])).astype(BF).T
        dy[pl.ds(pl.multiple_of(core * 128, 128), 128), :] = cot[...]
        dy[pl.ds(pl.multiple_of((1 - core) * 128, 128), 128), :] = cot_other[...]
        acc_out[...] = jnp.zeros_like(acc_out)
        acc_dh2[...] = jnp.zeros_like(acc_dh2)

    w_gate, w_up = dense[0, j], dense[1, j]
    gate, up = dot(h2p[...], w_gate), dot(h2p[...], w_up)
    blocks = wd[...].reshape(16, 3, 16, HALF).astype(F32)
    w_down = jnp.concatenate(
        [blocks[:, :, 0:8, :].reshape(HALF, HALF), blocks[:, :, 8:16, :].reshape(HALF, HALF)], axis=1
    ).astype(BF)
    sig = jax.nn.sigmoid(gate)
    hidden = (gate * sig * up).astype(BF)
    acc_out[...] += dot(hidden, w_down)
    dhid = dot_nt(dy[...], w_down)
    dgate = (dhid * up * sig * (1.0 + gate * (1.0 - sig))).astype(BF)
    dup = (dhid * gate * sig).astype(BF)
    acc_dh2[...] += dot_nt(dgate, w_gate) + dot_nt(dup, w_up)

    for part, value, keep, send in ((0, dgate, keep_g, send_g), (1, dup, keep_u, send_u)):
        grad = dot(h2p_t[part], value).astype(BF).reshape(8, 96, HALF)
        keep[...] = grad[:4]
        send[...] = grad[4:]
    grad_d[pl.ds(pl.multiple_of(j * HALF, HALF), HALF), :] = dot_tn(hidden, dy[...])

    @pl.when(j == 3)
    def _():
        mine = pl.multiple_of(core * 128, 128)
        other = pl.multiple_of((1 - core) * 128, 128)
        out_keep[...] = acc_out[pl.ds(mine, 128), :]
        dh2_out[:TOK, :] = dot_nt(acc_dh2[...].astype(BF), pn[...]).astype(BF)
        dh2_out[TOK:, :] = acc_out[pl.ds(other, 128), :].astype(BF)

        def write(w, carry):
            for at, out in ((w, keep_d), (w + 32, send_d)):
                base = chips[2, at] * 24
                for k in range(3):
                    rows = grad_d[pl.ds(pl.multiple_of(base + 8 * k, 8), 8), :]
                    out[w, k] = jnp.concatenate([rows[:, :HALF], rows[:, HALF:]], axis=0).astype(BF)
            return carry

        lax.fori_loop(0, 32, write, 0, unroll=2)


def attn_backward_kernel(
    scal,
    resid,
    dh2_a,
    dh2_b,
    g2,
    cot,
    cot_other,
    wo_a,
    wo_b,
    wanted,
    probs,
    o_mine,
    o_other,
    q,
    k_all,
    v_all,
    h_t_in,
    cosine_in,
    sine_in,
    dres_out,
    dq_out,
    dk_out,
    dv_out,
    grads,
    do,
    inner,
    grad_o,
    pa,
    h_t,
    cosine,
    sine,
    sems,
):
    core = scal[1]
    own = pl.ds(pl.multiple_of(scal[0] * TOK, TOK), TOK)
    step = pl.program_id(0)
    copies = [
        pltpu.make_async_copy(source, target, sems.at[k])
        for k, (source, target) in enumerate(((h_t_in, h_t), (cosine_in, cosine), (sine_in, sine)))
    ]

    @pl.when(step == 0)
    def _():
        for copy in copies:
            copy.start()
        pa[...] = placed_matrix(wanted[3:4, :])
        r = resid[...]
        dh2 = dh2_a[...].astype(F32) + dh2_b[...].astype(F32)
        scale = lax.rsqrt(jnp.mean(r * r, axis=1, keepdims=True) + EPS)
        weighted = dh2 * g2[0:1, :]
        mean = jnp.mean(weighted * r, axis=1, keepdims=True)
        mine, theirs = cot[...].astype(F32), cot_other[...].astype(F32)
        dy = jnp.concatenate([jnp.where(core == 0, mine, theirs), jnp.where(core == 0, theirs, mine)], axis=0)
        dres = dy + (scale * weighted - r * (scale * scale * scale) * mean)
        dresb = dres.astype(BF)
        placed = dot_nt(dresb[:, :HALF], wo_a[...].reshape(D, HALF)) + dot_nt(dresb[:, HALF:], wo_b[...].reshape(D, HALF))
        half = pl.ds(pl.multiple_of(core * HALF, HALF), HALF)
        found = dot_nt(placed.astype(BF), pa[half, :]).astype(BF)
        head_of = (
            lax.broadcasted_iota(jnp.int32, (8, HALF), 1) // HD == lax.broadcasted_iota(jnp.int32, (8, HALF), 0)
        ).astype(F32)
        o_a, o_b = o_mine[...], o_other[...]
        inner[...] = lax.dot_general(
            head_of,
            found.astype(F32) * o_a.astype(F32),
            (((1,), (1,)), ((), ())),
            precision=lax.Precision.HIGHEST,
            preferred_element_type=F32,
        )
        o_full = jnp.concatenate([jnp.where(core == 0, o_a, o_b), jnp.where(core == 0, o_b, o_a)], axis=1)
        d_mine = jnp.where(core == 0, dresb[:, :HALF], dresb[:, HALF:])
        found_o = dot_tn(dot(o_full, pa[...]).astype(BF), d_mine).astype(BF)
        for t in range(3):
            do[t] = found[:, 128 * t : 128 * t + 128]
            grad_o[t] = found_o[:, 128 * t : 128 * t + 128].reshape(8, 96, 128)
        dres_out[0] = dres[0:128, :]
        dres_out[1] = dres[128:256, :]

    @pl.when(step == 1)
    def _():
        for copy in copies:
            copy.wait()

    @pl.when(step > 0)
    def _():
        t = step - 1
        sub = lax.broadcasted_iota(jnp.int32, (128, TOK), 0)
        q_tile, do_tile, v_tile = q[...], do[t], v_all[...]
        k_t = k_all[...].T
        dqs, dks, dvs = [], [], []
        for odd in range(2):
            pb = probs[odd]
            dp = dot_nt(v_tile, lanes_of(do_tile, odd))
            ds = (pb.astype(F32) * (dp - inner[pl.ds(2 * t + odd, 1), :])).astype(BF)
            dks.append(dot(ds, q_tile))
            dvs.append(dot(pb, do_tile))
            dqs.append(dot(k_t, ds))
        u = jnp.where(sub < HD, dqs[0], dqs[1]).T * 0.125
        dq = (u * cosine[own, :] - swap_halves(u) * sine[own, :]).astype(BF)
        u = join_lanes(dks[0], dks[1])
        dk = (u * cosine[...] - swap_halves(u) * sine[...]).astype(BF)
        dv = join_lanes(dvs[0], dvs[1]).astype(BF)
        dq_out[...] = dq
        dk_out[...] = dk
        dv_out[...] = dv
        both = dot(h_t[...], jnp.concatenate([dk, dv], axis=1)).astype(BF)
        grads[:, 0:96, :] = dot(h_t[:, own], dq).astype(BF).reshape(8, 96, 128)
        grads[:, 96:192, :] = both[:, :128].reshape(8, 96, 128)
        grads[:, 192:288, :] = both[:, 128:].reshape(8, 96, 128)
        grads[:, 288:384, :] = grad_o[t]


def dh1_kernel(scal, dq, dk, dv, attn, wanted, out, pa, total):
    @pl.when(pl.program_id(0) == 0)
    def _():
        pa[...] = placed_matrix(wanted[3:4, :])

    total[...] = dot_nt(dk[...], weight_at(attn, 1)) + dot_nt(dv[...], weight_at(attn, 2))

    @pl.when(scal[0] == pl.program_id(0))
    def _():
        total[...] += dot_nt(dq[...], weight_at(attn, 0))

    out[...] = dot_nt(total[...].astype(BF), pa[...]).astype(BF)


def terms_kernel(*refs):
    for k in range(3):
        total = (refs[2 * k][...].astype(F32) + refs[2 * k + 1][...].astype(F32)).astype(BF)
        half = total.shape[0] // 2
        refs[6 + 2 * k][...] = total[:half]
        refs[7 + 2 * k][...] = total[half:]


def blocks_kernel(x0, y0, x1, y1, x2, y2, attn, out):
    to = lax.broadcasted_iota(jnp.int32, (HALF, HALF), 0)
    at = (to % 48 // 12) * 96 + to // 48 * 12 + to % 12
    pick = (lax.broadcasted_iota(jnp.int32, (HALF, HALF), 1) == at).astype(BF)

    def write(k, rows):
        out[:, 48 * k : 48 * k + 48, :] = dot(pick, rows).astype(BF).reshape(8, 48, HALF)

    for k, x, y in ((0, x0, y0), (1, x1, y1)):
        write(k, (x[0].astype(F32) + y[0].astype(F32)).astype(BF))
    out[:, 144:192, :] = (x2[0].astype(F32) + y2[0].astype(F32)).astype(BF).reshape(8, 48, HALF)
    total = attn[0].astype(F32)
    for b in range(1, 8):
        total += attn[b].astype(F32)
    write(2, total.astype(BF))


def sum_kernel(scal, blocks, mine, other, down):
    core = scal[1]
    total = blocks[0].astype(F32)
    for b in range(1, 8):
        total += blocks[b].astype(F32)
    for k in range(12):
        low, high = total[12 * k : 12 * k + 6, :], total[12 * k + 6 : 12 * k + 12, :]
        mine[k, 0:6, :] = jnp.where(core == 0, low, high)
        other[k, 0:6, :] = jnp.where(core == 0, high, low)
        for out in (mine, other):
            out[k, 6:8, :] = jnp.zeros((2, HALF), F32)
    down[...] = total[144:192, :].reshape(3, 16, HALF)


def update_kernel(scal, mine, theirs, down, x_ref, dh1_ref, g1, dres, resid, out_a, out_b, *refs):
    core = scal[1]
    output, input_grad = refs[56:58]
    x = x_ref[...].astype(F32)
    dh1 = dh1_ref[...].astype(F32)
    scale = lax.rsqrt(jnp.mean(x * x, axis=1, keepdims=True) + EPS)
    weighted = dh1 * g1[0:1, :]
    inner = jnp.mean(weighted * x, axis=1, keepdims=True)
    input_grad[...] = dres[core] + (scale * weighted - x * (scale * scale * scale) * inner)
    tokens = pl.ds(pl.multiple_of(core * 128, 128), 128)
    output[...] = (resid[tokens, :] + (out_a[...] + out_b[TOK:, :].astype(F32))).astype(BF)
    masters, moments, averages = refs[0:8], refs[8:16], refs[16:24]
    news, moms, means, copies = refs[24:32], refs[32:40], refs[40:48], refs[48:56]
    base = 1.0 / math.sqrt(16384)

    def step(k, at, grad):
        rate = RATES[k] * base
        moment = MOMENTUM * moments[k][at] + grad
        new = masters[k][at] - rate * (grad + MOMENTUM * moment)
        news[k][at] = new
        moms[k][at] = moment
        means[k][at] = AVERAGE * averages[k][at] + (1.0 - AVERAGE) * new
        copies[k][at] = new.astype(BF)

    def halves(a, b):
        return (jnp.where(core == 0, a, b), jnp.where(core == 0, b, a))

    gain_sums = [jnp.zeros((6, 128), F32), jnp.zeros((6, 128), F32)]

    def weigh(which, k, at, grad):
        product = masters[k][at].astype(BF).astype(F32) * grad
        for c in range(0, product.shape[1], 128):
            gain_sums[which] += product[:, c : c + 128]

    def chunk(k):
        a, b = mine[k][0:6, :], theirs[k][0:6, :]
        return (jnp.where(core == 0, a, b), jnp.where(core == 0, b, a))

    for k, weight, offset, gain in (
        (8, 0, 0, 0),
        (9, 1, 0, 0),
        (10, 2, 0, 0),
        (11, 3, 0, None),
        (0, 4, 0, 1),
        (1, 4, D, 1),
        (2, 4, 2 * D, 1),
        (3, 4, 3 * D, 1),
        (4, 5, 0, 1),
        (5, 5, D, 1),
        (6, 5, 2 * D, 1),
        (7, 5, 3 * D, 1),
    ):
        for h, grad in enumerate(chunk(k)):
            at = (slice(0, 6), slice(offset + h * HALF, offset + (h + 1) * HALF))
            step(weight, at, grad)
            if gain is not None:
                weigh(gain, weight, at, grad)
    for j in range(3):
        for h in range(2):
            grad = down[j, 8 * h : 8 * h + 8, :]
            step(6, (slice(8 * j, 8 * j + 8), slice(h * HALF, (h + 1) * HALF)), grad)
    row = lax.broadcasted_iota(jnp.int32, (6, 128), 0)
    lane = lax.broadcasted_iota(jnp.int32, (6, 128), 1)
    for k in range(2):
        column = jnp.sum(gain_sums[k], axis=1, keepdims=True)
        line = jnp.sum(jnp.where(lane == row, column, 0.0), axis=0, keepdims=True)[:, 0:6]
        at = (slice(k, k + 1), slice(0, 6))
        step(7, at, line / masters[7][at].astype(BF).astype(F32))


def whole():
    return pl.BlockSpec(memory_space=pltpu.VMEM)


def scalars():
    return pl.BlockSpec(memory_space=pltpu.SMEM)


def call(kernel, out_shape, operands, scratch=(), smem=1, name=None, micros=1.0, mib=60):
    specs = [scalars() if k < smem else whole() for k in range(len(operands))]
    return pl.pallas_call(
        kernel,
        out_shape=out_shape,
        in_specs=specs,
        out_specs=jax.tree.map(lambda _: whole(), out_shape),
        scratch_shapes=list(scratch),
        compiler_params=params(mib),
        cost_estimate=cost(micros),
        name=name,
    )(*operands)


def shape(dims, kind):
    return jax.ShapeDtypeStruct(dims, kind)


def add(a, b):
    return (a.astype(F32) + b.astype(F32)).astype(BF)


def fetch(block, axis):
    return permute(block, flip_pairs(axis, 3))


def first_terms(parts):
    return [fetch(send, order[0]) for order, (_, send) in reversed(list(zip(ORDERS, parts)))][::-1]


def next_terms(keeps, got):
    count, rows = keeps[0].shape[0], 192
    pair = [pl.BlockSpec((count // 2, rows, HALF), lambda j: (0, j, 0))] * 6
    out = pl.pallas_call(
        terms_kernel,
        out_shape=(shape((count // 2, HALF, HALF), BF),) * 6,
        grid=(HALF // rows,),
        in_specs=[pl.BlockSpec((count, rows, HALF), lambda j: (0, j, 0))] * 6,
        out_specs=tuple(pair),
        compiler_params=params(54),
        cost_estimate=cost(1),
        name="next_terms",
    )(*(v for pair in zip(keeps, got) for v in pair))
    return out[::2], out[1::2]


def reduce_rows(parts, got, after):
    keeps, sents = next_terms([keep for keep, _ in parts], got)
    got = [fetch(sent, order[1]) for sent, order in zip(sents, ORDERS)]
    got, after = lax.optimization_barrier((got, after))
    keeps, sents = next_terms(keeps, got)
    got = [fetch(sent, order[2]) for sent, order in zip(sents, ORDERS)]
    return [term for pair in zip(keeps, got) for term in pair], after


def flipped(block, flip):
    return permute(block, flip_pairs("z", flip))


def shards(inputs, doc_ids, cotangent, *state):
    state = tuple(v.T if k % 8 == 7 else v for k, v in enumerate(state))
    masters, moments, averages = state[0:8], state[8:16], state[16:24]
    z, core = lax.axis_index("z"), lax.axis_index("core")
    y, x_at = lax.axis_index("y"), lax.axis_index("x")
    scal = jnp.stack([z, core]).astype(jnp.int32)
    chips = chip_of_place({"z": z, "y": y, "x": x_at}, core)

    halves = shape((8, 8, HALF), F32)
    wq, wk, wv, wo, wg, wu, wd, gains = masters
    keep, send = call(pack_ffn_kernel, (halves, halves), (scal, wg, wu), name="pack_feed_forward")
    ffn_w = call(
        merge_ffn_kernel,
        shape((144, HALF), BF),
        (scal, keep, permute(send, CORE_PAIRS), wd),
        name="merge_feed_forward",
        mib=56,
    )
    ffn_w, wq, wk, wv, wo, gains, inputs, doc_ids, cotangent = lax.optimization_barrier(
        (ffn_w, wq, wk, wv, wo, gains, inputs, doc_ids, cotangent)
    )
    ffn_w = lax.all_gather(ffn_w, ("z", "y", "x"), axis=0, tiled=False)
    halves = shape((5, 8, HALF), F32)
    keep, send = call(
        pack_attn_kernel,
        (halves, halves),
        (scal, wq, wk, wv, wo, gains),
        scratch=(pltpu.VMEM((8, 128), F32),),
        name="pack_attention",
    )
    theirs, cot_other = permute(send, CORE_PAIRS), permute(cotangent[0], CORE_PAIRS)
    theirs, cot_other = lax.optimization_barrier((theirs, cot_other))
    attn = call(merge_attn_kernel, shape((8, 5, 16, HALF), BF), (scal, keep, theirs), name="merge_attention", mib=56)

    ids_row = jnp.zeros((16, D), BF).at[0, :128].set(doc_ids[0].astype(BF))
    block = jnp.concatenate([inputs[0], ids_row], axis=0)
    attn, block = lax.optimization_barrier((attn, block))
    attn = exchange(attn, 1)
    seq = [block, flipped(block, 1), flipped(block, 3)]
    wanted = placed_features(chips)
    attn, wanted, chips = lax.optimization_barrier((attn, wanted, chips))
    attn = call(dense_kernel, shape((8, 512, HALF), BF), (attn,), smem=0, name="dense_rows", mib=16)
    attn = exchange(attn, 3)
    seq.append(flipped(seq[1], 3))
    seq = jnp.stack(seq)
    seq_other = permute(seq, CORE_PAIRS)
    ids = jnp.concatenate([seq[:, 128, :128], seq_other[:, 128, :128]], axis=0).astype(F32)
    spots = [(((z + c) % 4 ^ flip) + 4 - c) % 4 * 2 + c for c in (core, 1 - core) for flip in FLIPS]
    here = jnp.stack(spots)[None, :] == jnp.arange(8)[:, None]
    ids = jnp.sum(jnp.where(here[:, :, None], ids[None], 0.0), axis=1).reshape(LEN)
    starts = jnp.sum((ids[None, :] < ids[:, None]).astype(jnp.int32), axis=1)
    freq = 10000.0 ** (-jnp.arange(0, HD, 2, dtype=F32) / HD)
    spot = (jnp.arange(LEN, dtype=jnp.int32) - starts).astype(F32)
    theta = spot[:, None] * jnp.tile(freq, 4)[None, :]
    sign = jnp.tile(jnp.repeat(jnp.array([-1.0, 1.0], F32), HD // 2), 2)
    cosine, sine = jnp.cos(theta), jnp.sin(theta) * sign[None, :]
    start_row = jnp.broadcast_to(starts.astype(F32)[None, :], (8, LEN))

    q, k_all, v_all, h_all, h_t, x_chip, probs, po, g1, g2 = call(
        attn_forward_kernel,
        (
            shape((TOK, HALF), BF),
            shape((LEN, HALF), BF),
            shape((LEN, HALF), BF),
            shape((LEN, D), BF),
            shape((D, LEN), BF),
            shape((TOK, D), BF),
            shape((HEADS, LEN, TOK), BF),
            shape((TOK, D + HALF), BF),
            shape((8, D), F32),
            shape((8, D), F32),
        ),
        (scal, seq, seq_other, cosine, sine, start_row, wanted, attn),
        scratch=(pltpu.VMEM((LEN, D), BF), pltpu.VMEM((LEN, TOK), F32), pltpu.VMEM((D, D), BF)),
        name="attention_forward",
        mib=54,
        micros=1.3e7,
    )
    po_other = permute(po, CORE_PAIRS)

    def full(dims):
        return pl.BlockSpec(dims, lambda i, n=len(dims): (0,) * n)

    ffn_out = (
        shape((128, D), F32),
        shape((TOK + 128, D), BF),
        shape((TOK, D), F32),
    ) + tuple(shape((4, HALF, HALF), BF) for _ in range(4)) + tuple(shape((32, 3, 16, HALF), BF) for _ in range(2))
    column = pl.BlockSpec((4, 96, HALF), lambda j: (0, j, 0))
    out_keep, dh2, resid, kg, sg, ku, su, kd, sd = pl.pallas_call(
        ffn_kernel,
        out_shape=ffn_out,
        grid=(4,),
        in_specs=[
            scalars(),
            scalars(),
            full((TOK, D)),
            full((TOK, D)),
            full((TOK, D)),
            full((128, D)),
            full((128, D)),
            full((8, D)),
            full((8, D)),
            pl.BlockSpec((64, 48, HALF), lambda j: (0, 0, 0)),
            pl.BlockSpec((64, 48, HALF), lambda j: (0, 1, 0)),
            pl.BlockSpec((16, 48, HALF), lambda j: (j, 2, 0)),
        ],
        out_specs=tuple(full(s.shape) for s in ffn_out[:3])
        + (column,) * 4
        + tuple(full(s.shape) for s in ffn_out[7:]),
        scratch_shapes=[
            pltpu.VMEM((D, D), BF),
            pltpu.VMEM((2, 4, D, HALF), BF),
            pltpu.VMEM((TOK, D), BF),
            pltpu.VMEM((2, D, TOK), BF),
            pltpu.VMEM((TOK, D), BF),
            pltpu.VMEM((TOK, D), F32),
            pltpu.VMEM((TOK, D), F32),
            pltpu.VMEM((FF // 2, D), F32),
        ],
        compiler_params=params(),
        cost_estimate=cost(4),
        name="feed_forward",
    )(
        scal,
        chips,
        x_chip,
        po,
        po_other,
        cotangent[0],
        cot_other,
        wanted,
        g2,
        *((ffn_w,) * 3),
    )

    dh2_other = permute(dh2, CORE_PAIRS)
    dh2_other, kg, sg, ku, su, kd, sd = lax.optimization_barrier((dh2_other, kg, sg, ku, su, kd, sd))
    at_tile = lambda i: jnp.maximum(i - 1, 0)
    short = pl.BlockSpec((TOK, 128), lambda i: (0, at_tile(i)))
    long = pl.BlockSpec((LEN, 128), lambda i: (0, at_tile(i)))
    dres, dq, dk, dv, grads = pl.pallas_call(
        attn_backward_kernel,
        out_shape=(
            shape((2, 128, D), F32),
            shape((TOK, HALF), BF),
            shape((LEN, HALF), BF),
            shape((LEN, HALF), BF),
            shape((8, HALF, HALF), BF),
        ),
        grid=(4,),
        in_specs=[
            scalars(),
            full((TOK, D)),
            full((TOK, D)),
            full((TOK, D)),
            full((8, D)),
            full((128, D)),
            full((128, D)),
            pl.BlockSpec((8, 96, HALF), lambda i: (0, 3, 0)),
            pl.BlockSpec((8, 96, HALF), lambda i: (0, 4, 0)),
            full((8, D)),
            pl.BlockSpec((2, LEN, TOK), lambda i: (at_tile(i), 0, 0)),
            pl.BlockSpec((TOK, HALF), lambda i: (0, 2)),
            pl.BlockSpec((TOK, HALF), lambda i: (0, 2)),
            short,
            long,
            long,
            *([pl.BlockSpec(memory_space=pl.ANY)] * 3),
        ],
        out_specs=(
            full((2, 128, D)),
            short,
            long,
            long,
            pl.BlockSpec((8, HALF, 128), lambda i: (0, 0, at_tile(i))),
        ),
        scratch_shapes=[
            pltpu.VMEM((3, TOK, 128), BF),
            pltpu.VMEM((8, TOK), F32),
            pltpu.VMEM((3, 8, 96, 128), BF),
            pltpu.VMEM((D, D), BF),
            pltpu.VMEM((D, LEN), BF),
            pltpu.VMEM((LEN, 128), F32),
            pltpu.VMEM((LEN, 128), F32),
            pltpu.SemaphoreType.DMA((3,)),
        ],
        compiler_params=params(),
        cost_estimate=cost(1),
        name="attention_backward",
    )(
        scal,
        resid,
        dh2,
        dh2_other,
        g2,
        cotangent[0],
        cot_other,
        attn,
        attn,
        wanted,
        probs,
        po,
        po_other,
        q,
        k_all,
        v_all,
        h_t,
        cosine,
        sine,
    )
    parts = [(kg, sg), (ku, su), (kd.reshape(4, HALF, HALF), sd.reshape(4, HALF, HALF))]
    got = first_terms(parts)
    exchanged = exchange(grads, 3)
    grads, dq, dk, dv, got = lax.optimization_barrier((grads, dq, dk, dv, got))
    grads = exchanged
    dh1 = pl.pallas_call(
        dh1_kernel,
        out_shape=shape((LEN, D), BF),
        grid=(4,),
        in_specs=[
            scalars(),
            full((TOK, HALF)),
            pl.BlockSpec((TOK, HALF), lambda b: (b, 0)),
            pl.BlockSpec((TOK, HALF), lambda b: (b, 0)),
            pl.BlockSpec((8, 288, HALF), lambda b: (0, 0, 0)),
            full((8, D)),
        ],
        out_specs=pl.BlockSpec((TOK, D), lambda b: (b, 0)),
        scratch_shapes=[pltpu.VMEM((D, D), BF), pltpu.VMEM((TOK, D), F32)],
        compiler_params=params(),
        cost_estimate=cost(1),
        name="attention_input_gradient",
    )(scal, dq, dk, dv, attn, wanted)
    terms, dh1 = reduce_rows(parts, got, dh1)
    dh1 = lax.psum_scatter(dh1, ("z", "core"), scatter_dimension=0, tiled=True)
    blocks = call(blocks_kernel, shape((8, 192, HALF), BF), (*terms, grads), smem=0, name="own_rows", mib=54)
    blocks = exchange(blocks, 1)

    rows = shape((12, 8, HALF), F32)
    grads, theirs, down = call(
        sum_kernel, (rows, rows, shape((3, 16, HALF), F32)), (scal, blocks), name="sum_blocks", mib=16
    )
    theirs = permute(theirs, CORE_PAIRS)
    shapes = tuple(shape(m.shape, F32) for m in masters)
    outs = call(
        update_kernel,
        shapes * 3 + tuple(shape(m.shape, BF) for m in masters) + (shape((128, D), BF), shape((128, D), F32)),
        (scal, grads, theirs, down, inputs[0], dh1, g1, dres, resid, out_keep, dh2_other, *masters, *moments, *averages),
        name="update",
        mib=56,
    )
    outs, output, input_grad = outs[:32], *outs[32:]
    outs = tuple(v.T if k % 8 == 7 else v for k, v in enumerate(outs))
    return (output[None], input_grad[None], *outs)


def solution(mesh):
    fine = Mesh(mesh.devices.reshape(4, 2, 4, 4), AXES)
    tokens = P(("y", "x"), ("z", "core"), None)
    rows = P(("z", "core", "y", "x"), None)
    return jax.shard_map(
        shards,
        mesh=fine,
        in_specs=(tokens, P(("y", "x"), ("z", "core")), tokens) + (rows,) * 24,
        out_specs=(tokens, tokens) + (rows,) * 32,
        check_vma=False,
    )
```
